32 devices in a mesh: wide: 16 (over z, y, core), narrow: 2 (over x).
Axes of the slice: x: 2, y: 2, z: 4, core: 2. Of those that a mesh axis runs over, the one named last changes fastest.
Arguments:
- pixels: bfloat16 [2, 32, 272, 261], P(None, ('wide', 'narrow')), may hold values from -4 to 4
- labels: int32 [2, 32], P(None, ('wide', 'narrow')), may hold values from 0 to 999
- partner: int32 [2, 32], P(None, ('wide', 'narrow')), may hold values from 0 to 31
- pair_on: int32 [2, 32], P(None, ('wide', 'narrow')), may hold values 0 or 1
- step_count: int32 [1], replicated, may hold values from 1 to 20
- matrices: float32 [1024, 10240], P(('wide', 'narrow')), may hold values from -0.75 to 0.75, as said below
- kv_weight: float32 [2048, 261], P(('wide', 'narrow')), may hold values from -0.375 to 0.375
- norm_gains: float32 [1024, 10], P(('wide', 'narrow')), may hold values from -1.2 to 1.4, as said below
- head_weight: float32 [1024, 1000], P(('wide', 'narrow')), may hold values from -0.1875 to 0.1875
- latent_init: float32 [1024, 512], P(('wide', 'narrow')), may hold values from -5 to 5
- matrices_first: float32 [1024, 10240], P(('wide', 'narrow')), may hold values from -3.8146973e-05 to 3.8146973e-05
- kv_first: float32 [2048, 261], P(('wide', 'narrow')), may hold values from -3.8146973e-05 to 3.8146973e-05
- gains_first: float32 [1024, 10], P(('wide', 'narrow')), may hold values from -3.8146973e-05 to 3.8146973e-05
- head_first: float32 [1024, 1000], P(('wide', 'narrow')), may hold values from -3.8146973e-05 to 3.8146973e-05
- latent_first: float32 [1024, 512], P(('wide', 'narrow')), may hold values from -8.34465e-07 to 8.34465e-07
- matrices_second: float32 [1024, 10240], P(('wide', 'narrow')), may hold values from 7.949873e-12 to 3.1799494e-11
- kv_second: float32 [2048, 261], P(('wide', 'narrow')), may hold values from 7.949873e-12 to 3.1799494e-11
- gains_second: float32 [1024, 10], P(('wide', 'narrow')), may hold values from 7.949873e-12 to 3.1799494e-11
- head_second: float32 [1024, 1000], P(('wide', 'narrow')), may hold values from 7.949873e-12 to 3.1799494e-11
- latent_second: float32 [1024, 512], P(('wide', 'narrow')), may hold values from 1.5899748e-15 to 6.359899e-15
Outputs:
- total_loss: float32 [], replicated
- grad_norm: float32 [], replicated
- counts: int32 [2], replicated
- new_matrices_first: float32 [1024, 10240], P(('wide', 'narrow'))
- new_matrices_second: float32 [1024, 10240], P(('wide', 'narrow'))
- new_matrices: float32 [1024, 10240], P(('wide', 'narrow'))
- new_kv_first: float32 [2048, 261], P(('wide', 'narrow'))
- new_kv_second: float32 [2048, 261], P(('wide', 'narrow'))
- new_kv_weight: float32 [2048, 261], P(('wide', 'narrow'))
- new_gains_first: float32 [1024, 10], P(('wide', 'narrow'))
- new_gains_second: float32 [1024, 10], P(('wide', 'narrow'))
- clipped_gains: float32 [1024, 10], P(('wide', 'narrow'))
- new_head_first: float32 [1024, 1000], P(('wide', 'narrow'))
- new_head_second: float32 [1024, 1000], P(('wide', 'narrow'))
- new_head_weight: float32 [1024, 1000], P(('wide', 'narrow'))
- new_latent_first: float32 [1024, 512], P(('wide', 'narrow'))
- new_latent_second: float32 [1024, 512], P(('wide', 'narrow'))
- clipped_latent: float32 [1024, 512], P(('wide', 'narrow'))
The draws below stay inside these ranges and needn't reach their ends.
Inputs may be any that keep to these rules, and one draw needn't show every extreme that they name: `matrices`: the cross and latent output blocks (1 and 7) are four times larger than the others. `norm_gains`: even columns are gains, odd columns biases.
All inputs are finite; a program needn't handle non-finite values. No bound on the sum of `pair_on` on one device may be relied on, other than what follows from the above.
Results may differ from the reference program's by a relative error of at most 0.012.
The reference program's roundings to bfloat16 on the way count: a program that leaves them out, or rounds other values in their place, can miss the bound.
Values may be sent and summed in bfloat16 or wider, within the bound.
No kernel may reach another device: no remote copies, remote signals or barrier semaphores. Data moves between devices by JAX's collectives and lax.ppermute only.
A program may use at most 320 MiB of HBM per device.

```python
import math
from functools import partial
import jax
import jax.numpy as jnp
from jax import lax

D = 1024
HEADS = 8
HEAD = 128
C = 261
K = 1000
L = 512
P_SIZE = 272
REPEATS = 1
MICRO = 2
EXAMPLES = 32
NPARAM = 12578816


def draw_matrices(key, part):
    normal_draw = jnp.clip(jax.random.normal(key, (D, 10 * D), jnp.float32), -6.0, 6.0)
    column = jnp.arange(10 * D) // D
    factor = jnp.where((column == 1) | (column == 7), 4.0, 1.0)
    return normal_draw * factor[None, :] * D ** (-0.5)


def draw_norm_gains(key, part):
    first_key, second_key = jax.random.split(key)
    scaling = jax.random.uniform(first_key, (D, 10), jnp.float32, 0.6, 1.4)
    shifted = jnp.clip(0.3 * jax.random.normal(second_key, (D, 10), jnp.float32), -1.2, 1.2)
    parity = (jnp.arange(10) % 2)[None, :]
    return jnp.where(parity == 1, shifted, scaling)


def touch_ends(entries, own_key, low, largest):
    longest = entries.shape.index(max(entries.shape))
    spots = []
    for shift in (0, 1):
        where = [jax.random.randint(jax.random.fold_in(own_key, axis), (), 0, length) for axis, length in enumerate(entries.shape)]
        where[longest] = (where[longest] + shift) % entries.shape[longest]
        spots.append(tuple(where))
    return entries.at[spots[0]].set(low).at[spots[1]].set(largest)


def shard_levels(stream_key, shape, pieces, least, top_value):
    level, own = 1.0, jax.random.fold_in(stream_key, 6)
    for dim, parts in pieces:
        steps = jnp.exp(jax.random.uniform(jax.random.fold_in(own, dim), (parts,), jnp.float32, least / len(pieces), top_value / len(pieces)))
        level = level * jnp.repeat(steps, shape[dim] // parts).reshape([-1 if axis == dim else 1 for axis in range(len(shape))])
    return level


def scatter_about(own_key, extent, scale, limit, shards=(), kind=jnp.bfloat16):
    array = jax.random.normal(own_key, extent, jnp.float32) * scale
    if len(shards) > 0:
        array = shard_levels(own_key, extent, shards, -0.22, 0.18) * array
    return jnp.clip(array, min=-limit, max=limit).astype(kind)


def setup_inputs(seed: int = 0) -> dict:
    splits = jax.random.split(jax.random.key(seed), 21)
    return {
        "pixels": scatter_about(splits[0], (MICRO, EXAMPLES, P_SIZE, C), 1.0, 4.0, ((1, 32),)),
        "labels": touch_ends(jax.random.randint(splits[1], (MICRO, EXAMPLES), 0, K), jax.random.fold_in(splits[1], 1), 0, K - 1).astype(jnp.int32),
        "partner": touch_ends(jax.random.randint(splits[2], (MICRO, EXAMPLES), 0, EXAMPLES), jax.random.fold_in(splits[2], 1), 0, EXAMPLES - 1).astype(jnp.int32),
        "pair_on": touch_ends((jax.random.randint(splits[3], (MICRO, EXAMPLES), 0, 2) < 1).astype(jnp.int32), jax.random.fold_in(splits[3], 1), 0, 1),
        "step_count": jax.random.randint(splits[4], (1,), 1, 21).astype(jnp.int32),
        "matrices": draw_matrices(jax.random.fold_in(splits[20], 71), 0),
        "kv_weight": scatter_about(splits[6], (2 * D, C), C ** -0.5, 0.375, ((0, 32),), jnp.float32),
        "norm_gains": draw_norm_gains(jax.random.fold_in(splits[20], 71), 0),
        "head_weight": scatter_about(splits[8], (D, K), D ** -0.5, 0.1875, ((0, 32),), jnp.float32),
        "latent_init": scatter_about(splits[9], (D, L), 1.0, 5.0, ((0, 32),), jnp.float32),
        "matrices_first": scatter_about(splits[10], (D, 10 * D), (0.01 / NPARAM ** 0.5), 3.814697265625e-05, ((0, 32),), jnp.float32),
        "kv_first": scatter_about(splits[11], (2 * D, C), (0.01 / NPARAM ** 0.5), 3.814697265625e-05, ((0, 32),), jnp.float32),
        "gains_first": scatter_about(splits[12], (D, 10), (0.01 / NPARAM ** 0.5), 3.814697265625e-05, ((0, 32),), jnp.float32),
        "head_first": scatter_about(splits[13], (D, K), (0.01 / NPARAM ** 0.5), 3.814697265625e-05, ((0, 32),), jnp.float32),
        "latent_first": scatter_about(splits[14], (D, L), (0.0002 / NPARAM ** 0.5), 8.344650268554688e-07, ((0, 32),), jnp.float32),
        "matrices_second": jnp.clip(jnp.exp(math.log(3.179949359388701e-11) - 1.3862944 * jax.random.uniform(splits[15], (D, 10 * D), jnp.float32) ** shard_levels(splits[15], (D, 10 * D), ((0, 32),), -0.2, 0.2)), 7.949873398471752e-12, 3.179949359388701e-11),
        "kv_second": jnp.clip(jnp.exp(math.log(3.179949359388701e-11) - 1.3862944 * jax.random.uniform(splits[16], (2 * D, C), jnp.float32) ** shard_levels(splits[16], (2 * D, C), ((0, 32),), -0.2, 0.2)), 7.949873398471752e-12, 3.179949359388701e-11),
        "gains_second": jnp.clip(jnp.exp(math.log(3.179949359388701e-11) - 1.3862944 * jax.random.uniform(splits[17], (D, 10), jnp.float32) ** shard_levels(splits[17], (D, 10), ((0, 32),), -0.2, 0.2)), 7.949873398471752e-12, 3.179949359388701e-11),
        "head_second": jnp.clip(jnp.exp(math.log(3.179949359388701e-11) - 1.3862944 * jax.random.uniform(splits[18], (D, K), jnp.float32) ** shard_levels(splits[18], (D, K), ((0, 32),), -0.2, 0.2)), 7.949873398471752e-12, 3.179949359388701e-11),
        "latent_second": jnp.clip(jnp.exp(math.log(6.359899027097394e-15) - 1.3862944 * jax.random.uniform(splits[19], (D, L), jnp.float32) ** shard_levels(splits[19], (D, L), ((0, 32),), -0.2, 0.2)), 1.5899747567743486e-15, 6.359899027097394e-15),
    }


EPSILON = 1e-05
RATE = 0.03
DECAY = 0.1
TINY = 1e-08
THRESH = 0.01
HIGH = lax.Precision.HIGHEST

@jax.custom_vjp
def low(v):
    return lax.optimization_barrier(v.astype(jnp.bfloat16)).astype(jnp.float32)

@jax.custom_vjp
def low_back(v):
    return v

def low_keep(v):
    return (low(v), None)

def low_pass(kept, grad):
    return (grad,)

def back_keep(v):
    return (v, None)

def back_low(kept, grad):
    return (low(grad),)
low.defvjp(low_keep, low_pass)
low_back.defvjp(back_keep, back_low)

def product(first_op, second_op):
    return low_back(jnp.dot(first_op, second_op, precision=HIGH))

def layer_norm(inputs, gain_vec, bias_vec):
    center = inputs - lax.optimization_barrier(jnp.mean(inputs, axis=-1, keepdims=True))
    spread = lax.optimization_barrier(jnp.mean(center * center, axis=-1, keepdims=True))
    return center * lax.rsqrt(spread + EPSILON) * gain_vec + bias_vec

def gelu_tanh(values):
    return jax.nn.gelu(values, approximate=True)

def columns(blocks, first, count):
    return blocks[:, first * D:(first + count) * D]

def feed(blocks, scales, latent, column, block):
    hidden = low(layer_norm(latent, scales[:, column], scales[:, column + 1]))
    active = low(gelu_tanh(product(hidden, columns(blocks, block, 1))))
    return latent + product(active, columns(blocks, block + 1, 1))

def cross_block(blocks, scales, key_value, latent):
    hidden = low(layer_norm(latent, scales[:, 0], scales[:, 1]))
    queries = low(product(hidden, columns(blocks, 0, 1)))
    scores = product(queries, key_value[:, :D].T) * D ** (-0.5)
    attend = low(jax.nn.softmax(scores, axis=-1))
    blended = low(product(attend, key_value[:, D:]))
    latent = latent + product(blended, columns(blocks, 1, 1))
    return feed(blocks, scales, latent, 2, 2)

def latent_block(blocks, scales, latent):
    hidden = low(layer_norm(latent, scales[:, 4], scales[:, 5]))
    packed = low(product(hidden, columns(blocks, 4, 3))).reshape(L, 3, HEADS, HEAD)
    scores = low_back(jnp.einsum('lhe,mhe->hlm', packed[:, 0], packed[:, 1], precision=HIGH)) * HEAD ** (-0.5)
    attend = low(jax.nn.softmax(scores, axis=-1))
    blended = low(low_back(jnp.einsum('hlm,mhe->lhe', attend, packed[:, 2], precision=HIGH)).reshape(L, D))
    latent = latent + product(blended, columns(blocks, 7, 1))
    return feed(blocks, scales, latent, 6, 8)

def crop_forward(weights, picture):
    blocks, kv_low, scales, head_low, initial = weights
    key_value = low(product(picture.astype(jnp.float32), kv_low.T))
    latent = initial.T
    for repeat in range(REPEATS):
        latent = cross_block(blocks, scales, key_value, latent)
        latent = latent_block(blocks, scales, latent)
    return low(lax.optimization_barrier(jnp.mean(layer_norm(latent, scales[:, 8], scales[:, 9]), axis=0)))

def step_loss(weights, pixels, labels, partner, pair_on):
    result = jnp.zeros((), jnp.float32)
    for position in range(MICRO):
        pooled = lax.map(jax.checkpoint(partial(crop_forward, weights)), pixels[position])
        logits = product(pooled, weights[3])
        label_hot = (labels[position][:, None] == jnp.arange(K)[None, :]).astype(jnp.float32)
        cross_entropy = jax.nn.logsumexp(logits, axis=-1) - lax.optimization_barrier(jnp.sum(logits * label_hot, axis=-1))
        distance = pooled - pooled[partner[position]]
        divisor = jnp.maximum(jnp.sum(pair_on[position]), 1).astype(jnp.float32) * D ** 0.5
        agreement = jnp.sum(pair_on[position].astype(jnp.float32) * lax.optimization_barrier(jnp.sum(distance * distance, axis=-1))) / divisor
        result = result + (jnp.mean(cross_entropy) + agreement) / MICRO
    return result

def reference(pixels, labels, partner, pair_on, step_count, matrices, kv_weight, norm_gains, head_weight, latent_init, matrices_first, kv_first, gains_first, head_first, latent_first, matrices_second, kv_second, gains_second, head_second, latent_second):
    masters = (matrices, kv_weight, norm_gains, head_weight, latent_init)
    firsts = (matrices_first, kv_first, gains_first, head_first, latent_first)
    seconds = (matrices_second, kv_second, gains_second, head_second, latent_second)

    def objective(params):
        return step_loss(tuple((low(member) for member in params)), pixels, labels, partner, pair_on)
    total_loss, pullback = jax.vjp(objective, masters)
    gradients = pullback(jnp.ones_like(total_loss))[0]
    square = jnp.zeros((), jnp.float32)
    for member in gradients:
        square = square + jnp.sum(member * member)
    grad_norm = jnp.sqrt(square)
    factor = jnp.minimum(1.0, THRESH / grad_norm)
    correction = 1.0 - jnp.power(0.5, step_count[0].astype(jnp.float32))
    results = []
    for index, (grad_item, master, moment_one, moment_two) in enumerate(zip(gradients, masters, firsts, seconds)):
        clipped = grad_item * factor
        moment_one = 0.5 * moment_one + 0.5 * clipped
        moment_two = 0.5 * moment_two + 0.5 * clipped * clipped
        if index == 2 or index == 4:
            results = results + [moment_one, moment_two, clipped]
        else:
            master = master - RATE * (moment_one / correction / (jnp.sqrt(moment_two / correction) + TINY) + DECAY * master)
            results = results + [moment_one, moment_two, master]
    counts = lax.optimization_barrier(jnp.sum(pair_on, axis=1)).astype(jnp.int32)
    return (total_loss, grad_norm, counts, results[0], results[1], results[2], results[3], results[4], results[5], results[6], results[7], results[8], results[9], results[10], results[11], results[12], results[13], results[14])
```

```python
import jax
import jax.numpy as jnp
from jax import lax
from jax.sharding import PartitionSpec as P

HEADS = 8
AXES = ("wide", "narrow")


EPSILON = 1e-05
RATE = 0.03
DECAY = 0.1
TINY = 1e-08
THRESH = 0.01


def lowered(values):
    return values.astype(jnp.bfloat16)


def matmul(first_op, second_op):
    return jnp.dot(first_op, second_op, preferred_element_type=jnp.float32)


def left_dot(first_op, second_op):
    return lax.dot_general(
        first_op, second_op, (((0,), (0,)), ((), ())), preferred_element_type=jnp.float32
    )


def right_dot(first_op, second_op):
    return lax.dot_general(
        first_op, second_op, (((1,), (1,)), ((), ())), preferred_element_type=jnp.float32
    )


def layer_norm(inputs, gain_vec, bias_vec):
    center = inputs - jnp.mean(inputs, axis=-1, keepdims=True)
    spread = jnp.mean(center * center, axis=-1, keepdims=True)
    return center * lax.rsqrt(spread + EPSILON) * gain_vec + bias_vec


def gelu_tanh(values):
    return jax.nn.gelu(values, approximate=True)


def norm_back(inputs, gain_vec, bias_vec, upstream):
    pullback = jax.vjp(layer_norm, inputs, gain_vec, bias_vec)[1]
    return pullback(upstream)


def softmax_back(attend, upstream):
    return attend * (upstream - jnp.sum(upstream * attend, axis=-1, keepdims=True))


def digits():
    n_wide = lax.axis_size("wide")
    n_narrow = lax.axis_size("narrow")
    rest = n_wide // 2
    top = min(4, rest)
    return (
        ("z", n_narrow * n_wide // top, top),
        ("y", 2 * n_narrow, rest // top),
        ("c", n_narrow, 2),
        ("x", 1, n_narrow),
    )


def device_index():
    return lax.axis_index("wide") * lax.axis_size("narrow") + lax.axis_index("narrow")


def exchange(values, offset):
    total = lax.axis_size(AXES)
    return lax.ppermute(values, AXES, [(i, i ^ offset) for i in range(total)])


def in_place(pieces, mine, axis):
    stacked = jnp.stack(pieces, axis=axis)
    bit = 1
    while bit < len(pieces):
        swapped = jnp.stack(
            [lax.index_in_dim(stacked, k ^ bit, axis, keepdims=False) for k in range(len(pieces))],
            axis=axis,
        )
        stacked = jnp.where((mine & bit) != 0, swapped, stacked)
        bit = bit * 2
    return stacked


def gather_rows(shard, order):
    me = device_index()
    table = digits()
    present = []
    current = shard
    for name in order:
        place = [entry[0] for entry in table].index(name)
        _, stride, size = table[place]
        if size == 1:
            continue
        mine = (me // stride) % size
        pieces = [current] + [exchange(current, k * stride) for k in range(1, size)]
        axis = sum(1 for other in present if other < place)
        present.append(place)
        current = in_place(pieces, mine, axis)
    return current.reshape((-1,) + shard.shape[1:])


def scatter_rows(full, order):
    me = device_index()
    table = digits()
    total = lax.axis_size(AXES)
    rows = full.shape[0] // total
    current = full.reshape(tuple(entry[2] for entry in table) + (rows,) + full.shape[1:])
    left = [entry[0] for entry in table]
    for name in order:
        place = [entry[0] for entry in table].index(name)
        _, stride, size = table[place]
        axis = left.index(name)
        left.remove(name)
        mine = (me // stride) % size
        kept = lax.dynamic_index_in_dim(current, mine, axis, keepdims=False).astype(jnp.float32)
        for k in range(1, size):
            sent = lax.dynamic_index_in_dim(current, mine ^ k, axis, keepdims=False)
            kept = kept + exchange(sent, k * stride).astype(jnp.float32)
        current = kept if not left else lowered(kept)
    return current


def gather_small(values):
    total = lax.axis_size(AXES)
    me = device_index()
    current = values[None]
    done = 1
    while done < total:
        step = min(8, total // done)
        current = jnp.concatenate(
            [current] + [exchange(current, k * done) for k in range(1, step)], axis=0
        )
        done = done * step
    return jnp.take(current, jnp.arange(total) ^ me, axis=0)


def feed_inner(first, second, gain_vec, bias_vec, latent):
    hidden = lowered(layer_norm(latent, gain_vec, bias_vec))
    before = matmul(hidden, first)
    active = lowered(gelu_tanh(before))
    return (latent + matmul(active, second), (hidden, before, active))


def feed_back(first, second, gain_vec, bias_vec, latent, stored, upstream):
    hidden, before, active = stored
    grad_low = lowered(upstream)
    grad_second = lowered(left_dot(active, grad_low))
    grad_active = right_dot(grad_low, second)
    pullback = jax.vjp(gelu_tanh, before)[1]
    grad_before = lowered(pullback(grad_active)[0])
    grad_first = lowered(left_dot(hidden, grad_before))
    grad_input, grad_gain, grad_bias = norm_back(
        latent, gain_vec, bias_vec, right_dot(grad_before, first)
    )
    return (upstream + grad_input, grad_first, grad_second, grad_gain, grad_bias)


def on_device(
    pixels,
    labels,
    partner,
    pair_on,
    step_count,
    matrices,
    kv_weight,
    norm_gains,
    head_weight,
    latent_init,
    matrices_first,
    kv_first,
    gains_first,
    head_first,
    latent_first,
    matrices_second,
    kv_second,
    gains_second,
    head_second,
    latent_second,
):
    axis_count = lax.axis_size(AXES)
    me = device_index()
    micro_count, _, spots, _ = pixels.shape
    examples = axis_count
    tokens = latent_init.shape[1]
    width = matrices.shape[1] // 10
    own_rows = matrices.shape[0]
    part = width // HEADS
    first_order = ("z", "y", "x", "c")
    second_order = ("z", "x", "y", "c")

    small = jnp.pad(
        jnp.concatenate([lowered(latent_init), lowered(norm_gains)], axis=1),
        ((0, 0), (0, 128 - norm_gains.shape[1])),
    )
    small = gather_rows(small, first_order)
    kv_low = gather_rows(lowered(kv_weight), second_order)
    weights = {}
    for turn, (block, count) in enumerate(
        ((0, 1), (1, 1), (2, 1), (3, 1), (4, 3), (7, 1), (8, 1), (9, 1))
    ):
        weights[block] = gather_rows(
            lowered(matrices[:, block * width : (block + count) * width]),
            first_order if turn % 2 == 0 else second_order,
        )
    head_low = gather_rows(lowered(head_weight), first_order)
    marks = gather_small(jnp.concatenate([labels, partner, pair_on], axis=0)[:, 0])
    labels_all = marks[:, 0:micro_count]
    partner_all = marks[:, micro_count : 2 * micro_count]
    pair_all = marks[:, 2 * micro_count : 3 * micro_count]
    counts = jnp.sum(pair_all, axis=0)

    initial = small[:, :tokens].astype(jnp.float32).T
    scales = small[:, tokens : tokens + 10].astype(jnp.float32).T

    flat = (micro_count * tokens, width)
    split = (micro_count, tokens, width)
    pictures = pixels[:, 0]
    key_value = lowered(
        matmul(pictures.reshape(micro_count * spots, -1), kv_low.T)
    ).reshape(micro_count, spots, 2 * width)
    keys, values = key_value[:, :, :width], key_value[:, :, width:]
    hidden_zero = lowered(layer_norm(initial, scales[0], scales[1]))
    queries = lowered(matmul(hidden_zero, weights[0]))
    scores = jnp.einsum(
        "ld,mpd->mlp", queries, keys, preferred_element_type=jnp.float32
    ) * width ** (-0.5)
    attend = jax.nn.softmax(scores, axis=-1)
    attend_low = lowered(attend)
    blended = lowered(
        jnp.einsum("mlp,mpd->mld", attend_low, values, preferred_element_type=jnp.float32)
    ).reshape(flat)
    latent_one = (initial[None] + matmul(blended, weights[1]).reshape(split)).reshape(flat)
    latent_two, stored_cross = feed_inner(weights[2], weights[3], scales[2], scales[3], latent_one)
    hidden_two = lowered(layer_norm(latent_two, scales[4], scales[5]))
    packed = lowered(matmul(hidden_two, weights[4])).reshape(micro_count, tokens, 3, HEADS, part)
    scores_self = jnp.einsum(
        "blhe,bmhe->bhlm", packed[:, :, 0], packed[:, :, 1], preferred_element_type=jnp.float32
    ) * part ** (-0.5)
    attend_self = jax.nn.softmax(scores_self, axis=-1)
    attend_self_low = lowered(attend_self)
    blended_self = lowered(
        jnp.einsum(
            "bhlm,bmhe->blhe", attend_self_low, packed[:, :, 2], preferred_element_type=jnp.float32
        )
    ).reshape(flat)
    latent_three = latent_two + matmul(blended_self, weights[7])
    result, stored_self = feed_inner(weights[8], weights[9], scales[6], scales[7], latent_three)
    normed = layer_norm(result, scales[8], scales[9])
    pooled_own = lowered(jnp.mean(normed.reshape(split), axis=1))

    pooled_all = gather_small(pooled_own)
    logits = matmul(pooled_all.reshape(-1, width), head_low).reshape(axis_count, micro_count, -1)
    label_hot = (labels_all[:, :, None] == jnp.arange(logits.shape[-1])).astype(jnp.float32)
    cross_entropy = jax.nn.logsumexp(logits, axis=-1) - jnp.sum(logits * label_hot, axis=-1)
    micro_index = jnp.arange(micro_count)[None]
    pooled_wide = pooled_all.astype(jnp.float32)
    distance = pooled_wide - pooled_wide[partner_all, micro_index]
    active = pair_all.astype(jnp.float32)
    divisor = jnp.maximum(counts, 1).astype(jnp.float32) * width**0.5
    agreement = active * jnp.sum(distance * distance, axis=-1) / divisor
    total_loss = jnp.sum(cross_entropy / examples + agreement) / micro_count
    grad_logits = lowered((jax.nn.softmax(logits, axis=-1) - label_hot) / (examples * micro_count))
    pull_term = (2.0 / micro_count * (active / divisor))[:, :, None] * distance
    aimed = (partner_all == me).astype(jnp.float32)
    grad_logits_own = lax.dynamic_index_in_dim(grad_logits, me, 0, keepdims=False)
    pull_own = lax.dynamic_index_in_dim(pull_term, me, 0, keepdims=False)
    grad_pooled = (
        right_dot(grad_logits_own, head_low) + pull_own - jnp.sum(aimed[:, :, None] * pull_term, axis=0)
    )
    pooled_rows = lax.dynamic_slice_in_dim(
        pooled_all.reshape(-1, width), me * own_rows, own_rows, axis=1
    )
    grad_head = left_dot(pooled_rows, grad_logits.reshape(pooled_rows.shape[0], -1))

    orders = (("c", "x", "y", "z"), ("c", "y", "x", "z"))
    owned = {}
    gain_grads = {}
    spread_grad = jnp.broadcast_to((grad_pooled / tokens)[:, None], split).reshape(flat)
    upstream, gain_grads[8], gain_grads[9] = norm_back(result, scales[8], scales[9], spread_grad)
    upstream, first, second, gain_grads[6], gain_grads[7] = feed_back(
        weights[8], weights[9], scales[6], scales[7], latent_three, stored_self, upstream
    )
    owned[9] = scatter_rows(second, orders[0])
    owned[8] = scatter_rows(first, orders[1])
    grad_low = lowered(upstream)
    owned[7] = scatter_rows(lowered(left_dot(blended_self, grad_low)), orders[0])
    grad_blended = lowered(right_dot(grad_low, weights[7])).reshape(micro_count, tokens, HEADS, part)
    grad_attend = jnp.einsum(
        "blhe,bmhe->bhlm", grad_blended, packed[:, :, 2], preferred_element_type=jnp.float32
    )
    grad_values = jnp.einsum(
        "bhlm,blhe->bmhe", attend_self_low, grad_blended, preferred_element_type=jnp.float32
    )
    grad_scores = lowered(softmax_back(attend_self, grad_attend) * part ** (-0.5))
    grad_queries = jnp.einsum(
        "bhlm,bmhe->blhe", grad_scores, packed[:, :, 1], preferred_element_type=jnp.float32
    )
    grad_keys = jnp.einsum(
        "bhlm,blhe->bmhe", grad_scores, packed[:, :, 0], preferred_element_type=jnp.float32
    )
    grad_packed = lowered(
        jnp.stack([grad_queries, grad_keys, grad_values], axis=2).reshape(flat[0], 3 * width)
    )
    owned[4] = scatter_rows(lowered(left_dot(hidden_two, grad_packed)), orders[1])
    grad_input, gain_grads[4], gain_grads[5] = norm_back(
        latent_two, scales[4], scales[5], right_dot(grad_packed, weights[4])
    )
    upstream = upstream + grad_input
    upstream, first, second, gain_grads[2], gain_grads[3] = feed_back(
        weights[2], weights[3], scales[2], scales[3], latent_one, stored_cross, upstream
    )
    owned[3] = scatter_rows(second, orders[0])
    owned[2] = scatter_rows(first, orders[1])
    grad_low = lowered(upstream)
    owned[1] = scatter_rows(lowered(left_dot(blended, grad_low)), orders[0])
    grad_blended = lowered(right_dot(grad_low, weights[1])).reshape(split)
    grad_attend = jnp.einsum("mld,mpd->mlp", grad_blended, values, preferred_element_type=jnp.float32)
    grad_values = jnp.einsum(
        "mlp,mld->mpd", attend_low, grad_blended, preferred_element_type=jnp.float32
    )
    grad_scores = lowered(softmax_back(attend, grad_attend) * width ** (-0.5))
    grad_queries = lowered(
        jnp.einsum("mlp,mpd->mld", grad_scores, keys, preferred_element_type=jnp.float32)
    )
    grad_keys = jnp.einsum("mlp,ld->mpd", grad_scores, queries, preferred_element_type=jnp.float32)
    grad_pairs = lowered(jnp.concatenate([grad_keys, grad_values], axis=2))
    grad_kv = left_dot(
        grad_pairs.reshape(micro_count * spots, 2 * width),
        pictures.reshape(micro_count * spots, -1),
    )
    owned_kv = scatter_rows(lowered(grad_kv), orders[1])
    grad_first = jnp.einsum(
        "ld,mle->de", hidden_zero, grad_queries, preferred_element_type=jnp.float32
    )
    owned[0] = scatter_rows(lowered(grad_first), orders[0])
    grad_hidden = right_dot(grad_queries.reshape(flat), weights[0]).reshape(split)
    grad_input, gain_grads[0], gain_grads[1] = norm_back(
        initial, scales[0], scales[1], jnp.sum(grad_hidden, axis=0)
    )
    grad_initial = jnp.sum(upstream.reshape(split), axis=0) + grad_input
    gains = jnp.stack([gain_grads[column] for column in range(10)], axis=0)
    gains = jnp.pad(gains, ((0, 118), (0, 0)))
    owned_small = scatter_rows(
        lowered(jnp.concatenate([grad_initial, gains], axis=0)).T, orders[1]
    )
    grad_matrices = jnp.concatenate([owned[block] for block in (0, 1, 2, 3, 4, 7, 8, 9)], axis=1)
    shares = (
        grad_matrices,
        owned_kv,
        owned_small[:, tokens : tokens + 10],
        grad_head,
        owned_small[:, :tokens],
    )
    square = jnp.zeros((), jnp.float32)
    for member in shares:
        square = square + jnp.sum(member * member)
    square = jnp.sum(gather_small(jnp.broadcast_to(square, (128,))), axis=0)[0]
    grad_norm = jnp.sqrt(square)
    factor = jnp.minimum(1.0, THRESH / grad_norm)
    correction = 1.0 - jnp.power(0.5, step_count[0].astype(jnp.float32))
    masters = (matrices, kv_weight, norm_gains, head_weight, latent_init)
    firsts = (matrices_first, kv_first, gains_first, head_first, latent_first)
    seconds = (matrices_second, kv_second, gains_second, head_second, latent_second)
    results = []
    for index, (grad_item, master, moment_one, moment_two) in enumerate(
        zip(shares, masters, firsts, seconds)
    ):
        clipped = grad_item * factor
        moment_one = 0.5 * moment_one + 0.5 * clipped
        moment_two = 0.5 * moment_two + 0.5 * clipped * clipped
        if index == 2 or index == 4:
            results = results + [moment_one, moment_two, clipped]
        else:
            master = master - RATE * (
                moment_one / correction / (jnp.sqrt(moment_two / correction) + TINY)
                + DECAY * master
            )
            results = results + [moment_one, moment_two, master]
    return (
        total_loss,
        grad_norm,
        counts,
        results[0],
        results[1],
        results[2],
        results[3],
        results[4],
        results[5],
        results[6],
        results[7],
        results[8],
        results[9],
        results[10],
        results[11],
        results[12],
        results[13],
        results[14],
    )


def solution(mesh):
    in_specs = (
        P(None, ("wide", "narrow"), None, None),
        P(None, ("wide", "narrow")),
        P(None, ("wide", "narrow")),
        P(None, ("wide", "narrow")),
        P(),
        P(("wide", "narrow"), None),
        P(("wide", "narrow"), None),
        P(("wide", "narrow"), None),
        P(("wide", "narrow"), None),
        P(("wide", "narrow"), None),
        P(("wide", "narrow"), None),
        P(("wide", "narrow"), None),
        P(("wide", "narrow"), None),
        P(("wide", "narrow"), None),
        P(("wide", "narrow"), None),
        P(("wide", "narrow"), None),
        P(("wide", "narrow"), None),
        P(("wide", "narrow"), None),
        P(("wide", "narrow"), None),
        P(("wide", "narrow"), None),
    )
    out_specs = (
        P(),
        P(),
        P(),
        P(("wide", "narrow"), None),
        P(("wide", "narrow"), None),
        P(("wide", "narrow"), None),
        P(("wide", "narrow"), None),
        P(("wide", "narrow"), None),
        P(("wide", "narrow"), None),
        P(("wide", "narrow"), None),
        P(("wide", "narrow"), None),
        P(("wide", "narrow"), None),
        P(("wide", "narrow"), None),
        P(("wide", "narrow"), None),
        P(("wide", "narrow"), None),
        P(("wide", "narrow"), None),
        P(("wide", "narrow"), None),
        P(("wide", "narrow"), None),
    )
    return jax.shard_map(
        on_device, mesh=mesh, in_specs=in_specs, out_specs=out_specs, check_vma=False
    )
```

```python
import functools

import jax
import jax.numpy as jnp
from jax import lax
from jax.experimental import pallas as pl
from jax.experimental.pallas import tpu as pltpu
from jax.sharding import PartitionSpec as P

HEADS = 8
AXES = ("wide", "narrow")

EPSILON = 1e-05
RATE = 0.03
DECAY = 0.1
TINY = 1e-08
THRESH = 0.01
BEND = 0.044715
MARKS = 128
SLOPE = 0.7978845608028654
VMEM = pltpu.VMEM
MIB = 1 << 20


def lowered(values):
    return values.astype(jnp.bfloat16)


def dot_nn(first_op, second_op):
    return jnp.dot(first_op, second_op, preferred_element_type=jnp.float32)


def dot_tn(first_op, second_op):
    return lax.dot_general(
        first_op, second_op, (((0,), (0,)), ((), ())), preferred_element_type=jnp.float32
    )


def dot_nt(first_op, second_op):
    return lax.dot_general(
        first_op, second_op, (((1,), (1,)), ((), ())), preferred_element_type=jnp.float32
    )


def standard(inputs):
    center = inputs - jnp.mean(inputs, axis=-1, keepdims=True)
    scale = lax.rsqrt(jnp.mean(center * center, axis=-1, keepdims=True) + EPSILON)
    return center * scale, scale


def layer_norm(inputs, scales, column):
    return standard(inputs)[0] * scales[column : column + 1, :] + scales[column + 1 : column + 2, :]


def norm_back(inputs, scales, column, upstream):
    unit, scale = standard(inputs)
    gain = jnp.sum(upstream * unit, axis=0, keepdims=True)
    bias = jnp.sum(upstream, axis=0, keepdims=True)
    inner = upstream * scales[column : column + 1, :]
    back = scale * (
        inner
        - jnp.mean(inner, axis=-1, keepdims=True)
        - unit * jnp.mean(inner * unit, axis=-1, keepdims=True)
    )
    return back, gain, bias


def gelu_both(values):
    square = values * values
    bent = jnp.tanh(SLOPE * values * (1.0 + BEND * square))
    half = 0.5 * (1.0 + bent)
    steep = half + 0.5 * values * (1.0 - bent * bent) * SLOPE * (1.0 + 3.0 * BEND * square)
    return values * half, steep


def softmax(scores):
    raised = jnp.exp(scores - jnp.max(scores, axis=-1, keepdims=True))
    return raised * (1.0 / jnp.sum(raised, axis=-1, keepdims=True))


def softmax_back(attend, upstream):
    return attend * (upstream - jnp.sum(upstream * attend, axis=-1, keepdims=True))


class Half:
    def __init__(self, arrays, offsets, rows):
        self.arrays = arrays
        self.offsets = offsets
        self.rows = rows

    def start(self, refs, me, target, sem, column, stride=None, shift=0):
        width = target.shape[1]
        if self.offsets is None:
            pltpu.make_async_copy(refs[0].at[0, :, column : column + width], target, sem).start()
            return
        stride = self.rows if stride is None else stride
        for ref, offsets in zip(refs, self.offsets):
            for group, offset in enumerate(offsets):
                spot = pl.multiple_of((me ^ offset) * stride + shift, self.rows)
                pltpu.make_async_copy(
                    ref.at[group, :, column : column + width],
                    target.at[pl.ds(spot, self.rows), :],
                    sem,
                ).start()


def arrived(target, sem):
    pltpu.make_async_copy(target, target, sem).wait()


def cost(micros):
    return pl.CostEstimate(flops=int(micros * 1.1e9), bytes_accessed=1 << 20, transcendentals=0)


def params(mib, dims=1):
    return pltpu.CompilerParams(
        vmem_limit_bytes=mib * MIB, dimension_semantics=("arbitrary",) * dims
    )


def launch(kernel, after, operands, in_specs, **rest):
    extra = len(after)

    def inner(*refs):
        kernel(*refs[: len(operands)], *refs[len(operands) + extra :])

    return pl.pallas_call(inner, in_specs=list(in_specs) + [ANY] * extra, **rest)(*operands, *after)


ANY = pl.BlockSpec(memory_space=pl.ANY)
SMEM = pl.BlockSpec(memory_space=pltpu.SMEM)


def whole(shape):
    return pl.BlockSpec(shape, lambda *ids: (0,) * len(shape))


def by_crop(shape, rank=1):
    return pl.BlockSpec(shape, lambda m, *ids: (m,) + (0,) * (len(shape) - 1))


def shaped(shape, dtype):
    return jax.ShapeDtypeStruct(shape, dtype)


def run_cross_forward(me, pictures, small, kv, first, second, width, tokens, after=()):
    micro, spots, channels = pictures.shape
    parts = (small, kv, first, second)
    counts = [len(part[0].arrays) for part in parts]
    small_columns = tokens + 128

    def kernel(me_ref, pic_ref, *refs):
        groups = []
        at = 0
        for count in counts:
            groups.append(refs[at : at + count])
            at += count
        latent_ref, blended_ref, attend_ref, pair_ref, initial_ref, hidden_ref, query_ref, scale_ref = refs[at : at + 8]
        small_s, kv_s, first_s, second_s, sems = refs[at + 8 :]
        me_now = me_ref[0]
        step = pl.program_id(0)

        @pl.when(step == 0)
        def _():
            small[0].start(groups[0], me_now, small_s, sems.at[0], small[1])
            if kv[0].offsets is None:
                kv[0].start(groups[1], me_now, kv_s, sems.at[1], 0)
            else:
                rows = kv[0].rows
                kv[0].start(groups[1], me_now, kv_s, sems.at[1], kv[1], 2 * rows, 0)
                kv[0].start(groups[1], me_now, kv_s, sems.at[1], kv[1] + channels, 2 * rows, rows)
            first[0].start(groups[2], me_now, first_s, sems.at[2], first[1])
            second[0].start(groups[3], me_now, second_s, sems.at[3], second[1])
            arrived(small_s, sems.at[0])
            turned = small_s[...].astype(jnp.float32).T
            initial_ref[...] = turned[:tokens]
            scale_ref[...] = turned[tokens : tokens + 16]
            hidden_ref[...] = lowered(layer_norm(initial_ref[...], scale_ref, 0))
            arrived(first_s, sems.at[2])
            query_ref[...] = lowered(dot_nn(hidden_ref[...], first_s[...]))
            arrived(kv_s, sems.at[1])
            arrived(second_s, sems.at[3])

        pair_ref[0] = lowered(dot_nt(pic_ref[0], kv_s[...]))
        scores = dot_nt(query_ref[...], pair_ref[0, :, :width]) * width ** (-0.5)
        attend = softmax(scores)
        attend_ref[0] = attend
        blended_ref[...] = lowered(dot_nn(lowered(attend), pair_ref[0, :, width:]))
        latent_ref[...] = initial_ref[...] + dot_nn(blended_ref[...], second_s[...])

    total = micro * tokens
    return launch(
        kernel,
        after,
        [me, pictures, *[array for part in parts for array in part[0].arrays]],
        grid=(micro,),
        in_specs=[SMEM, by_crop((1, spots, channels))] + [ANY] * sum(counts),
        out_specs=[
            by_crop((tokens, width)),
            by_crop((tokens, width)),
            by_crop((1, tokens, spots)),
            by_crop((1, spots, 2 * width)),
            whole((tokens, width)),
            whole((tokens, width)),
            whole((tokens, width)),
            whole((16, width)),
        ],
        out_shape=[
            shaped((total, width), jnp.float32),
            shaped((total, width), jnp.bfloat16),
            shaped((micro, tokens, spots), jnp.float32),
            shaped((micro, spots, 2 * width), jnp.bfloat16),
            shaped((tokens, width), jnp.float32),
            shaped((tokens, width), jnp.bfloat16),
            shaped((tokens, width), jnp.bfloat16),
            shaped((16, width), jnp.float32),
        ],
        scratch_shapes=[
            VMEM((width, small_columns), jnp.bfloat16),
            VMEM((2 * width, channels), jnp.bfloat16),
            VMEM((width, width), jnp.bfloat16),
            VMEM((width, width), jnp.bfloat16),
            pltpu.SemaphoreType.DMA((4,)),
        ],
        compiler_params=params(48),
        cost_estimate=cost(18),
        name="cross_forward",
    )


def run_feed_forward(me, scales, latent, first, second, column, micro, pool, after=()):
    total, width = latent.shape
    tokens = total // micro
    parts = (first, second)
    counts = [len(part[0].arrays) for part in parts]

    def kernel(me_ref, scale_ref, latent_ref, *refs):
        first_refs, refs = refs[: counts[0]], refs[counts[0] :]
        second_refs, refs = refs[: counts[1]], refs[counts[1] :]
        out_ref, hidden_ref, active_ref, steep_ref = refs[:4]
        first_s, second_s, sems = refs[-3:]
        step = pl.program_id(0)

        @pl.when(step == 0)
        def _():
            first[0].start(first_refs, me_ref[0], first_s, sems.at[0], first[1])
            second[0].start(second_refs, me_ref[0], second_s, sems.at[1], second[1])

        hidden_ref[...] = lowered(layer_norm(latent_ref[...], scale_ref, column))

        @pl.when(step == 0)
        def _():
            arrived(first_s, sems.at[0])

        pieces = 4
        span = width // pieces
        for piece in range(pieces):
            cut = slice(piece * span, (piece + 1) * span)
            active, steep = gelu_both(dot_nn(hidden_ref[...], first_s[:, cut]))
            active_ref[:, cut] = lowered(active)
            steep_ref[:, cut] = lowered(steep)

        @pl.when(step == 0)
        def _():
            arrived(second_s, sems.at[1])

        out_ref[...] = latent_ref[...] + dot_nn(active_ref[...], second_s[...])
        if pool:
            normed = layer_norm(out_ref[...], scale_ref, 8)
            refs[4][0] = lowered(jnp.mean(normed, axis=0, keepdims=True))

    out_shape = [shaped((total, width), jnp.float32)] + [shaped((total, width), jnp.bfloat16)] * 3
    out_specs = [by_crop((tokens, width))] * 4
    if pool:
        out_shape.append(shaped((micro, 1, width), jnp.bfloat16))
        out_specs.append(by_crop((1, 1, width)))
    return launch(
        kernel,
        after,
        [me, scales, latent, *[array for part in parts for array in part[0].arrays]],
        grid=(micro,),
        in_specs=[SMEM, whole((16, width)), by_crop((tokens, width))] + [ANY] * sum(counts),
        out_specs=out_specs,
        out_shape=out_shape,
        scratch_shapes=[
            VMEM((width, width), jnp.bfloat16),
            VMEM((width, width), jnp.bfloat16),
            pltpu.SemaphoreType.DMA((2,)),
        ],
        compiler_params=params(48),
        cost_estimate=cost(16),
        name="feed_forward",
    )


def run_self_forward(me, scales, latent, query, key, value, out, micro, after=()):
    total, width = latent.shape
    tokens = total // micro
    part = width // HEADS
    pair = 2 * part
    turns = HEADS // 2
    parts = (query, key, value, out)
    counts = [len(entry[0].arrays) for entry in parts]

    def kernel(me_ref, scale_ref, latent_ref, *refs):
        groups = []
        at = 0
        for count in counts:
            groups.append(refs[at : at + count])
            at += count
        out_ref, hidden_ref, packed_ref, attend_ref, blended_ref = refs[at : at + 5]
        packed_s, out_s, sems = refs[at + 5 :]
        step, turn = pl.program_id(0), pl.program_id(1)

        @pl.when((step == 0) & (turn == 0))
        def _():
            for number in range(3):
                parts[number][0].start(
                    groups[number], me_ref[0], packed_s.at[number], sems.at[number], parts[number][1]
                )
            out[0].start(groups[3], me_ref[0], out_s, sems.at[3], out[1])

        @pl.when(turn == 0)
        def _():
            hidden_ref[...] = lowered(layer_norm(latent_ref[...], scale_ref, 4))
            for number in range(3):

                @pl.when(step == 0)
                def _():
                    arrived(packed_s.at[number], sems.at[number])

                packed_ref[:, number * width : (number + 1) * width] = lowered(
                    dot_nn(hidden_ref[...], packed_s[number])
                )

        base = pl.multiple_of(turn * pair, pair)
        queries = packed_ref[:, pl.ds(base, pair)]
        keys = packed_ref[:, pl.ds(pl.multiple_of(width + base, pair), pair)]
        values = packed_ref[:, pl.ds(pl.multiple_of(2 * width + base, pair), pair)]
        joined = []
        for head in range(2):
            cut = slice(head * part, (head + 1) * part)
            attend = softmax(dot_nt(queries[:, cut], keys[:, cut]) * part ** (-0.5))
            attend_ref[0, head] = attend
            joined.append(lowered(dot_nn(lowered(attend), values[:, cut])))
        blended_ref[:, pl.ds(base, pair)] = jnp.concatenate(joined, axis=1)

        @pl.when((step == 0) & (turn == turns - 1))
        def _():
            arrived(out_s, sems.at[3])

        @pl.when(turn == turns - 1)
        def _():
            out_ref[...] = latent_ref[...] + dot_nn(blended_ref[...], out_s[...])

    return launch(
        kernel,
        after,
        [me, scales, latent, *[array for entry in parts for array in entry[0].arrays]],
        grid=(micro, turns),
        in_specs=[SMEM, whole((16, width)), by_crop((tokens, width))] + [ANY] * sum(counts),
        out_specs=[
            by_crop((tokens, width)),
            by_crop((tokens, width)),
            by_crop((tokens, 3 * width)),
            pl.BlockSpec((1, 2, tokens, tokens), lambda m, h: (m, h, 0, 0)),
            by_crop((tokens, width)),
        ],
        out_shape=[
            shaped((total, width), jnp.float32),
            shaped((total, width), jnp.bfloat16),
            shaped((total, 3 * width), jnp.bfloat16),
            shaped((micro, HEADS, tokens, tokens), jnp.float32),
            shaped((total, width), jnp.bfloat16),
        ],
        scratch_shapes=[
            VMEM((3, width, width), jnp.bfloat16),
            VMEM((width, width), jnp.bfloat16),
            pltpu.SemaphoreType.DMA((4,)),
        ],
        compiler_params=params(52, 2),
        cost_estimate=cost(30),
        name="self_forward",
    )


def run_losses(me, pooled, head, classes, examples, micro, after=()):
    count, width = pooled.shape[0], pooled.shape[1] - MARKS
    parts = (head[0], head[1])
    counts = [len(entry[0].arrays) for entry in parts]
    span = width // 2

    def kernel(me_ref, pooled_ref, *refs):
        groups = (refs[: counts[0]], refs[counts[0] : counts[0] + counts[1]])
        loss_ref, logits_ref, grad_ref, left_s, right_s, sems = refs[counts[0] + counts[1] :]
        me_now = me_ref[0]
        halves = (left_s, right_s)
        for number in range(2):
            parts[number][0].start(
                groups[number], me_now, halves[number], sems.at[number], parts[number][1]
            )
        rows = lax.broadcasted_iota(jnp.int32, (count, 1), 0)
        turn = rows % micro
        marks = pooled_ref[:, width:].astype(jnp.float32)
        labels = (marks[:, 0:1] * 256.0 + marks[:, 1:2]).astype(jnp.int32)
        partner = (marks[:, 2:3] * 256.0 + marks[:, 3:4]).astype(jnp.int32)
        active = marks[:, 4:5]
        pooled_low = pooled_ref[:, :width]
        pooled_wide = pooled_low.astype(jnp.float32)
        columns = lax.broadcasted_iota(jnp.int32, (count, count), 1)
        aimed = lowered((columns == partner * micro + turn).astype(jnp.float32))
        distance = pooled_wide - dot_nn(aimed, pooled_low)
        divisor = jnp.zeros((count, 1), jnp.float32)
        for number in range(micro):
            here = (turn == number).astype(jnp.float32)
            counted = jnp.sum(here * active, axis=0, keepdims=True)
            loss_ref[1 + number : 2 + number] = jnp.broadcast_to(counted, (1, 128))
            counted = jnp.maximum(counted, 1.0)
            divisor = divisor + here * (counted * width**0.5)
        agreement = active * jnp.sum(distance * distance, axis=-1, keepdims=True) / divisor
        pull = (2.0 / micro) * (active / divisor) * distance
        for number in range(2):
            arrived(halves[number], sems.at[number])
        logits = jnp.concatenate([dot_nn(pooled_low, half[...]) for half in halves], axis=1)
        column = lax.broadcasted_iota(jnp.int32, (count, 2 * span), 1)
        logits = jnp.where(column < classes, logits, -1e30)
        top = jnp.max(logits, axis=-1, keepdims=True)
        raised = jnp.exp(logits - top)
        mass = jnp.sum(raised, axis=-1, keepdims=True)
        hot = (column == labels).astype(jnp.float32)
        entropy = top + jnp.log(mass) - jnp.sum(logits * hot, axis=-1, keepdims=True)
        loss = jnp.sum(entropy / examples + agreement, axis=0, keepdims=True) / micro
        loss_ref[0:1] = jnp.broadcast_to(loss, (1, 128))
        grad_logits = lowered((raised / mass - hot) / (examples * micro))
        logits_ref[...] = grad_logits
        grad = pull + sum(
            dot_nt(grad_logits[:, number * span : (number + 1) * span], halves[number][...])
            for number in range(2)
        )
        for number in range(micro):
            own = (rows == me_now * micro + number).astype(jnp.float32)
            aiming = ((partner == me_now) & (turn == number)).astype(jnp.float32)
            grad_ref[number] = jnp.sum(own * grad - aiming * pull, axis=0, keepdims=True)

    vmem = pl.BlockSpec(memory_space=pltpu.VMEM)
    return launch(
        kernel,
        after,
        [me, pooled, *[array for entry in parts for array in entry[0].arrays]],
        in_specs=[SMEM, vmem] + [ANY] * sum(counts),
        out_specs=[vmem] * 3,
        out_shape=[
            shaped((8, 128), jnp.float32),
            shaped((count, width), jnp.bfloat16),
            shaped((micro, 1, width), jnp.float32),
        ],
        scratch_shapes=[
            VMEM((width, span), jnp.bfloat16),
            VMEM((width, span), jnp.bfloat16),
            pltpu.SemaphoreType.DMA((2,)),
        ],
        compiler_params=pltpu.CompilerParams(vmem_limit_bytes=24 * MIB),
        cost_estimate=cost(5),
        name="losses",
    )


class Sender:
    def __init__(self, total, core_rows):
        self.total = total
        self.core_rows = core_rows
        self.groups = total // (2 * core_rows)

    def shapes(self, columns):
        return [shaped((self.groups, self.core_rows, columns), jnp.bfloat16)] * 2

    def start(self, source, core, keep, send, column, sem):
        width = source.shape[1]
        rows = self.core_rows
        for group in range(self.groups):
            for target, side in ((send, 1 - core), (keep, core)):
                spot = pl.multiple_of((2 * group + side) * rows, rows)
                pltpu.make_async_copy(
                    source.at[pl.ds(spot, rows), :],
                    target.at[group, :, column : column + width],
                    sem,
                ).start()


def run_feed_backward(
    me, scales, latent, upstream, steep, first, second, column, micro, pool, after=()
):
    total, width = latent.shape
    tokens = total // micro
    parts = (first, second)
    counts = [len(entry[0].arrays) for entry in parts]
    span = width // 2

    def kernel(me_ref, scale_ref, latent_ref, up_ref, *refs):
        if pool:
            pooled_ref, refs = refs[0], refs[1:]
        steep_ref, refs = refs[0], refs[1:]
        first_refs, refs = refs[: counts[0]], refs[counts[0] :]
        second_refs, refs = refs[: counts[1]], refs[counts[1] :]
        out_ref, gain_ref, low_ref, before_ref, after_ref, first_s, second_s, sems = refs
        step = pl.program_id(0)

        @pl.when(step == 0)
        def _():
            second[0].start(second_refs, me_ref[0], second_s, sems.at[1], second[1])
            first[0].start(first_refs, me_ref[0], first_s, sems.at[0], first[1])
            gain_ref[...] = jnp.zeros(gain_ref.shape, jnp.float32)

        if pool:
            spread = jnp.broadcast_to(pooled_ref[0] / tokens, (tokens, width))
            upstream, gain, bias = norm_back(up_ref[...], scale_ref, 8, spread)
            gain_ref[2:3] += gain
            gain_ref[3:4] += bias
            out_ref[...] = upstream
        else:
            out_ref[...] = up_ref[...]
        low_ref[...] = lowered(out_ref[...])

        @pl.when(step == 0)
        def _():
            arrived(second_s, sems.at[1])

        for number in range(2):
            cut = slice(number * span, (number + 1) * span)
            grad = dot_nt(low_ref[...], second_s[cut, :])
            before_ref[:, cut] = lowered(grad * steep_ref[:, cut].astype(jnp.float32))

        @pl.when(step == 0)
        def _():
            arrived(first_s, sems.at[0])

        back, gain, bias = norm_back(
            latent_ref[...], scale_ref, column, dot_nt(before_ref[...], first_s[...])
        )
        gain_ref[0:1] += gain
        gain_ref[1:2] += bias
        out_ref[...] += back
        after_ref[...] = lowered(out_ref[...])

    in_specs = [SMEM, whole((16, width)), by_crop((tokens, width)), by_crop((tokens, width))]
    operands = [me, scales, latent]
    if pool:
        in_specs.append(by_crop((1, 1, width)))
        operands += list(upstream)
    else:
        operands.append(upstream)
    in_specs += [by_crop((tokens, width))] + [ANY] * sum(counts)
    operands += [steep] + [array for entry in parts for array in entry[0].arrays]
    return launch(
        kernel,
        after,
        operands,
        in_specs,
        grid=(micro,),
        out_specs=[by_crop((tokens, width)), whole((8, width))] + [by_crop((tokens, width))] * 3,
        out_shape=[shaped((total, width), jnp.float32), shaped((8, width), jnp.float32)]
        + [shaped((total, width), jnp.bfloat16)] * 3,
        scratch_shapes=[
            VMEM((width, width), jnp.bfloat16),
            VMEM((width, width), jnp.bfloat16),
            pltpu.SemaphoreType.DMA((2,)),
        ],
        compiler_params=params(48),
        cost_estimate=cost(16),
        name="feed_backward",
    )


def run_self_backward(crop, me, scales, latent, upstream, stored, query, key, value, out, micro, onward, after=()):
    total, width = latent.shape
    tokens = total // micro
    part = width // HEADS
    pair = 2 * part
    turns = HEADS // 2
    packed, attend = stored
    parts = (query, key, value, out)
    counts = [len(entry[0].arrays) for entry in parts]

    def kernel(me_ref, scale_ref, latent_ref, up_ref, packed_ref, attend_ref, *refs):
        groups = []
        at = 0
        for count in counts:
            groups.append(refs[at : at + count])
            at += count
        if onward is not None:
            at += 1
        grad_ref, out_ref, gain_ref, packed_s, out_s, blend_s, sems = refs[at:]
        turn = pl.program_id(0)

        @pl.when(turn == 0)
        def _():
            out[0].start(groups[3], me_ref[0], out_s, sems.at[3], out[1])
            for number in range(3):
                parts[number][0].start(
                    groups[number], me_ref[0], packed_s.at[number], sems.at[number], parts[number][1]
                )
            arrived(out_s, sems.at[3])
            blend_s[...] = lowered(dot_nt(lowered(up_ref[...]), out_s[...]))

        base = pl.multiple_of(turn * pair, pair)
        queries = packed_ref[:, pl.ds(base, pair)]
        keys = packed_ref[:, pl.ds(pl.multiple_of(width + base, pair), pair)]
        values = packed_ref[:, pl.ds(pl.multiple_of(2 * width + base, pair), pair)]
        blends = blend_s[:, pl.ds(base, pair)]
        grads = ([], [], [])
        for head in range(2):
            cut = slice(head * part, (head + 1) * part)
            attend = attend_ref[0, head]
            grad_attend = dot_nt(blends[:, cut], values[:, cut])
            scores = lowered(softmax_back(attend, grad_attend) * part ** (-0.5))
            grads[2].append(lowered(dot_tn(lowered(attend), blends[:, cut])))
            grads[0].append(lowered(dot_nn(scores, keys[:, cut])))
            grads[1].append(lowered(dot_tn(scores, queries[:, cut])))
        for number in range(3):
            spot = pl.ds(pl.multiple_of(number * width + base, pair), pair)
            grad_ref[:, spot] = jnp.concatenate(grads[number], axis=1)

        @pl.when(turn == turns - 1)
        def _():
            for number in range(3):
                arrived(packed_s.at[number], sems.at[number])
            grad_hidden = sum(
                dot_nt(grad_ref[:, number * width : (number + 1) * width], packed_s[number])
                for number in range(3)
            )
            back, gain, bias = norm_back(latent_ref[...], scale_ref, 4, grad_hidden)
            gain_ref[0:1] = gain
            gain_ref[1:2] = bias
            out_ref[...] = up_ref[...] + back

    def crop_rows(columns):
        return pl.BlockSpec((tokens, columns), lambda h: (crop, 0))

    operands = [me, scales, latent, upstream, packed, attend]
    operands += [array for entry in parts for array in entry[0].arrays]
    aliases = {}
    if onward is not None:
        aliases = {len(operands): 1}
        operands.append(onward)
    return launch(
        kernel,
        after,
        operands,
        grid=(turns,),
        in_specs=[
            SMEM,
            whole((16, width)),
            crop_rows(width),
            crop_rows(width),
            crop_rows(3 * width),
            pl.BlockSpec((1, 2, tokens, tokens), lambda h: (crop, h, 0, 0)),
        ]
        + [ANY] * (sum(counts) + len(aliases)),
        input_output_aliases=aliases,
        out_specs=[whole((tokens, 3 * width)), crop_rows(width), whole((8, width))],
        out_shape=[
            shaped((tokens, 3 * width), jnp.bfloat16),
            shaped((total, width), jnp.float32),
            shaped((8, width), jnp.float32),
        ],
        scratch_shapes=[
            VMEM((3, width, width), jnp.bfloat16),
            VMEM((width, width), jnp.bfloat16),
            VMEM((tokens, width), jnp.bfloat16),
            pltpu.SemaphoreType.DMA((4,)),
        ],
        compiler_params=params(56),
        cost_estimate=cost(20),
        name="self_backward",
    )


def run_weights(me, products, sender, columns, after=()):
    flat = []
    for lefts, rights, _ in products:
        for array, _, _ in lefts + rights:
            if not any(array is known for known in flat):
                flat.append(array)
    where = {id(array): number for number, array in enumerate(flat)}
    count = len(columns)
    depth = products[0][0][0][0].shape[1]
    width = max(last for _, _, places in products for _, last, _, _ in places)

    def kernel(me_ref, *refs):
        sources, refs = refs[: len(flat)], refs[len(flat) :]
        targets, (mat_s, sem) = refs[: 2 * count], refs[2 * count :]
        core = (me_ref[0] // me_ref[1]) % 2
        for number, (lefts, rights, places) in enumerate(products):
            for column, last, buffer, spot in places:
                mat_s[number, :, column:last] = lowered(
                    sum(
                        dot_tn(
                            sources[where[id(left)]][begin : begin + size, :],
                            sources[where[id(right)]][:, at + column : at + last],
                        )
                        for (left, begin, size), (right, at, _) in zip(lefts, rights)
                    )
                )
                sender.start(
                    mat_s.at[number, :, column:last],
                    core,
                    targets[2 * buffer],
                    targets[2 * buffer + 1],
                    spot,
                    sem,
                )
        for number, (lefts, rights, places) in enumerate(products):
            for column, last, buffer, spot in places:
                arrived(mat_s.at[number, :, column:last], sem)

    vmem = pl.BlockSpec(memory_space=pltpu.VMEM)
    return launch(
        kernel,
        after,
        [me] + flat,
        [SMEM] + [vmem] * len(flat),
        out_specs=[ANY] * (2 * count),
        out_shape=[shape for number in columns for shape in sender.shapes(number)],
        scratch_shapes=[
            VMEM((len(products), depth, width), jnp.bfloat16),
            pltpu.SemaphoreType.DMA,
        ],
        compiler_params=pltpu.CompilerParams(vmem_limit_bytes=40 * MIB),
        cost_estimate=cost(3 * len(products)),
        name="weights",
    )


def run_cross_backward(
    me, scales, initial, upstream, stored, gains, first, second, micro, sender, after=()
):
    total, width = upstream.shape
    tokens = total // micro
    queries, attend, pairs = stored
    spots = pairs.shape[1]
    parts = (first, second)
    counts = [len(entry[0].arrays) for entry in parts]
    small_columns = tokens + 128

    def kernel(me_ref, scale_ref, initial_ref, up_ref, query_ref, attend_ref, pair_ref, gains_ref, *refs):
        first_refs, refs = refs[: counts[0]], refs[counts[0] :]
        second_refs, refs = refs[: counts[1]], refs[counts[1] :]
        query_out, pair_out, keep, send, first_s, second_s, up_s, back_s, small_s, sems = refs
        step = pl.program_id(0)
        core = (me_ref[0] // me_ref[1]) % 2

        @pl.when(step == 0)
        def _():
            second[0].start(second_refs, me_ref[0], second_s, sems.at[1], second[1])
            first[0].start(first_refs, me_ref[0], first_s, sems.at[0], first[1])
            up_s[...] = jnp.zeros(up_s.shape, jnp.float32)
            back_s[...] = jnp.zeros(back_s.shape, jnp.float32)
            arrived(second_s, sems.at[1])

        keys, values = pair_ref[0, :, :width], pair_ref[0, :, width:]
        attend = attend_ref[0]
        blend = lowered(dot_nt(lowered(up_ref[...]), second_s[...]))
        scores = lowered(softmax_back(attend, dot_nt(blend, values)) * width ** (-0.5))
        query_out[...] = lowered(dot_nn(scores, keys))
        pair_out[:, :width] = lowered(dot_tn(scores, query_ref[...]))
        pair_out[:, width:] = lowered(dot_tn(lowered(attend), blend))
        up_s[...] += up_ref[...]

        @pl.when(step == 0)
        def _():
            arrived(first_s, sems.at[0])

        back_s[...] += dot_nt(query_out[...], first_s[...])

        @pl.when(step == micro - 1)
        def _():
            back, gain, bias = norm_back(initial_ref[...], scale_ref, 0, back_s[...])
            gains_all = jnp.concatenate(
                [gain, bias, gains_ref[2:, :], jnp.zeros((128 - gains_ref.shape[0], width), jnp.float32)], axis=0
            )
            small_s[:, :tokens] = lowered((up_s[...] + back).T)
            small_s[:, tokens:] = lowered(gains_all.T)
            sender.start(small_s, core, keep, send, 0, sems.at[2])
            arrived(small_s, sems.at[2])

    return launch(
        kernel,
        after,
        [me, scales, initial, upstream, queries, attend, pairs, gains]
        + [array for entry in parts for array in entry[0].arrays],
        [
            SMEM,
            whole((16, width)),
            whole((tokens, width)),
            by_crop((tokens, width)),
            whole((tokens, width)),
            by_crop((1, tokens, spots)),
            by_crop((1, spots, 2 * width)),
            whole((16, width)),
        ]
        + [ANY] * sum(counts),
        grid=(micro,),
        out_specs=[by_crop((tokens, width)), by_crop((spots, 2 * width)), ANY, ANY],
        out_shape=[
            shaped((total, width), jnp.bfloat16),
            shaped((micro * spots, 2 * width), jnp.bfloat16),
        ]
        + sender.shapes(small_columns),
        scratch_shapes=[
            VMEM((width, width), jnp.bfloat16),
            VMEM((width, width), jnp.bfloat16),
            VMEM((tokens, width), jnp.float32),
            VMEM((tokens, width), jnp.float32),
            VMEM((width, small_columns), jnp.bfloat16),
            pltpu.SemaphoreType.DMA((3,)),
        ],
        compiler_params=params(48),
        cost_estimate=cost(16),
        name="cross_backward",
    )


def run_last_weights(me, hidden, grad_queries, grad_pairs, pictures, sender, kv_sender, after=()):
    tokens, width = hidden.shape
    micro = grad_queries.shape[0] // tokens
    channels = pictures.shape[1]

    def kernel(me_ref, hidden_ref, query_ref, pair_ref, pic_ref, keep, send, keep_kv, send_kv, mat_s, kv_s, sems):
        core = (me_ref[0] // me_ref[1]) % 2
        span = width // 2
        for number in range(2):
            cut = slice(number * span, (number + 1) * span)
            mat_s[:, cut] = lowered(
                sum(
                    dot_tn(hidden_ref[...], query_ref[crop * tokens : (crop + 1) * tokens, cut])
                    for crop in range(micro)
                )
            )
        sender.start(mat_s, core, keep, send, 0, sems.at[0])
        kv_s[...] = lowered(dot_tn(pair_ref[...], pic_ref[...]))
        kv_sender.start(kv_s, core, keep_kv, send_kv, 0, sems.at[1])
        arrived(mat_s, sems.at[0])
        arrived(kv_s, sems.at[1])

    vmem = pl.BlockSpec(memory_space=pltpu.VMEM)
    return launch(
        kernel,
        after,
        [me, hidden, grad_queries, grad_pairs, pictures],
        [SMEM] + [vmem] * 4,
        out_specs=[ANY] * 4,
        out_shape=sender.shapes(width) + kv_sender.shapes(channels),
        scratch_shapes=[
            VMEM((width, width), jnp.bfloat16),
            VMEM((2 * width, channels), jnp.bfloat16),
            pltpu.SemaphoreType.DMA((2,)),
        ],
        compiler_params=pltpu.CompilerParams(vmem_limit_bytes=32 * MIB),
        cost_estimate=cost(6),
        name="last_weights",
    )


def run_shards(matrices, kv_weight, norm_gains, head_weight, latent_init, columns):
    rows = matrices.shape[0]
    tokens, gains = latent_init.shape[1], norm_gains.shape[1]
    channels = kv_weight.shape[1]
    wide_channels = -(-channels // 128) * 128
    classes = head_weight.shape[1]
    width = matrices.shape[1] // 10
    small = tokens + 128

    def kernel(mat_ref, kv_ref, gain_ref, head_ref, latent_ref, first_ref, *refs):
        first_ref[...] = jnp.zeros(first_ref.shape, jnp.bfloat16)
        first_ref[:, :tokens] = lowered(latent_ref[...])
        first_ref[:, tokens : tokens + gains] = lowered(gain_ref[...])
        for side in range(2):
            at = small + side * wide_channels
            first_ref[:, at : at + channels] = lowered(kv_ref[side * rows : (side + 1) * rows, :])
        for (begin, end), ref in zip(columns, refs):
            ref[...] = lowered(mat_ref[:, begin * width : end * width])
        refs[-1][...] = jnp.zeros(refs[-1].shape, jnp.bfloat16)
        refs[-1][:, :classes] = lowered(head_ref[...])

    widths = [small + 2 * wide_channels] + [(end - begin) * width for begin, end in columns] + [width]
    vmem = pl.BlockSpec(memory_space=pltpu.VMEM)
    return pl.pallas_call(
        kernel,
        in_specs=[vmem] * 5,
        out_specs=[vmem] * len(widths),
        out_shape=[shaped((rows, number), jnp.bfloat16) for number in widths],
        compiler_params=pltpu.CompilerParams(vmem_limit_bytes=24 * MIB),
        cost_estimate=cost(3),
        name="shards",
    )(matrices, kv_weight, norm_gains, head_weight, latent_init)


def run_join(targets, passing, after):
    moves = [move for _, parts in targets for move in parts]
    count, kept = len(moves), len(passing)

    def kernel(*refs):
        sources = refs[:count]
        outs = refs[count + kept : count + kept + len(targets)]
        sems = refs[-1]
        copies = []
        at = 0
        for target, (_, parts) in zip(outs, targets):
            for _, cut, first in parts:
                source = sources[at] if cut is None else sources[at].at[:, cut]
                size = 1 if len(source.shape) == 2 else source.shape[0]
                spot = target.at[first] if len(source.shape) == 2 else target.at[first : first + size]
                copies.append(pltpu.make_async_copy(source, spot, sems.at[at]))
                at += 1
        for copy in copies:
            copy.start()
        for copy in copies:
            copy.wait()

    outs = launch(
        kernel,
        after,
        [move[0] for move in moves] + list(passing),
        [ANY] * (count + kept),
        out_specs=[ANY] * (len(targets) + kept),
        out_shape=[shaped(shape, jnp.bfloat16) for shape, _ in targets]
        + [shaped(array.shape, array.dtype) for array in passing],
        scratch_shapes=[pltpu.SemaphoreType.DMA((count,))],
        input_output_aliases={count + number: len(targets) + number for number in range(kept)},
        compiler_params=pltpu.CompilerParams(vmem_limit_bytes=1 * MIB),
        cost_estimate=cost(3),
        name="join",
    )
    return outs[: len(targets)], outs[len(targets) :]


def run_fold(me, parts, after):
    depth = 4
    operands = [me]
    in_specs = [SMEM]
    out_specs = []
    out_shape = []
    for terms, axis in parts:
        groups, rows, columns = terms[0].shape
        each = groups // depth
        for term in terms:
            operands.append(term)
            in_specs.append(pl.BlockSpec((each, rows, columns), lambda z: (z, 0, 0)))
        if axis == "x":
            block = (each, rows // 2, columns)
        else:
            block = (1, rows, columns)
        for _ in range(2):
            out_specs.append(pl.BlockSpec(block, lambda z: (z, 0, 0)))
            out_shape.append(shaped((block[0] * depth,) + block[1:], jnp.bfloat16))

    def kernel(me_ref, *refs):
        at = 0
        out = sum(len(terms) for terms, _ in parts)
        mine = {"x": me_ref[0] % 2, "y": (me_ref[0] // 4) % 2}
        for terms, axis in parts:
            sources = refs[at : at + len(terms)]
            at += len(terms)
            for side in range(2):
                spot = mine[axis] if side == 0 else 1 - mine[axis]
                if axis == "x":
                    rows = sources[0].shape[1] // 2
                    cut = (slice(None), pl.ds(pl.multiple_of(spot * rows, rows), rows), slice(None))
                else:
                    cut = (pl.ds(spot, 1), slice(None), slice(None))
                refs[out][...] = lowered(sum(source[cut].astype(jnp.float32) for source in sources))
                out += 1

    outs = launch(
        kernel,
        after,
        operands,
        in_specs,
        grid=(depth,),
        out_specs=out_specs,
        out_shape=out_shape,
        compiler_params=params(32),
        cost_estimate=cost(4),
        name="fold",
    )
    return [(outs[2 * number], outs[2 * number + 1]) for number in range(len(parts))]


def run_fold_z(me, parts, after):
    depth = 4

    def kernel(me_ref, *refs):
        mine = me_ref[0] // 8
        at = 0
        out = sum(len(terms) for terms in parts)
        for terms in parts:
            sources = refs[at : at + len(terms)]
            at += len(terms)
            for k in range(depth):
                spot = mine ^ k
                refs[out][...] = lowered(
                    sum(source[pl.ds(spot, 1)].astype(jnp.float32) for source in sources)
                )[0]
                out += 1

    vmem = pl.BlockSpec(memory_space=pltpu.VMEM)
    operands = [me] + [term for terms in parts for term in terms]
    shapes = [
        shaped(terms[0].shape[1:], jnp.bfloat16) for terms in parts for _ in range(depth)
    ]
    outs = launch(
        kernel,
        after,
        operands,
        [SMEM] + [vmem] * (len(operands) - 1),
        out_specs=[vmem] * len(shapes),
        out_shape=shapes,
        compiler_params=pltpu.CompilerParams(vmem_limit_bytes=24 * MIB),
        cost_estimate=cost(3),
        name="fold_z",
    )
    return [outs[depth * number : depth * (number + 1)] for number in range(len(parts))]


def digits():
    n_wide = lax.axis_size("wide")
    n_narrow = lax.axis_size("narrow")
    rest = n_wide // 2
    top = min(4, rest)
    return (
        ("z", n_narrow * n_wide // top, top),
        ("y", 2 * n_narrow, rest // top),
        ("c", n_narrow, 2),
        ("x", 1, n_narrow),
    )


def device_index():
    return lax.axis_index("wide") * lax.axis_size("narrow") + lax.axis_index("narrow")


def exchange(values, offset):
    total = lax.axis_size(AXES)
    return lax.ppermute(values, AXES, [(i, i ^ offset) for i in range(total)])


class Gather:
    def __init__(self, shard, left, plain):
        self.shard = shard
        self.widths = (left, shard.shape[1] - left)
        self.rows = shard.shape[0]
        self.table = {name: (stride, size) for name, stride, size in digits()}
        self.names = (("y", "x"), ("x", "y"))
        self.plain = plain

    def send_z(self):
        stride, size = self.table["z"]
        self.got = [exchange(self.shard, k * stride) for k in range(1, size)]
        return self.got

    def join(self, targets, passing, after):
        if self.plain:
            flats = []
            for _, parts in targets:
                flats.append(
                    jnp.concatenate(
                        [
                            array if array.ndim == 3 else array[None, :, cut]
                            for array, cut, _ in parts
                        ]
                    )
                )
            return flats, passing
        return run_join(targets, passing, after)

    def join_z(self, passing=(), after=()):
        stride, size = self.table["z"]
        pieces = [self.shard] + self.got
        targets = []
        at = 0
        for width in self.widths:
            parts = [(piece, slice(at, at + width), k) for k, piece in enumerate(pieces)]
            targets.append(((size, self.rows, width), parts))
            at += width
        self.flats, passing = self.join(targets, passing, after)
        self.offsets = [[k * stride for k in range(size)]] * 2
        return passing

    def send(self, turn):
        self.got = []
        for half in range(2):
            stride, size = self.table[self.names[half][turn]]
            self.got.append([exchange(self.flats[half], k * stride) for k in range(1, size)])
        return self.got[0] + self.got[1]

    def pieces(self, turn):
        halves = []
        for half in range(2):
            stride, size = self.table[self.names[half][turn]]
            arrays = [self.flats[half]] + self.got[half]
            halves.append(
                (arrays, [[offset ^ (k * stride) for offset in self.offsets[half]] for k in range(size)])
            )
        return halves

    def join_first(self, passing=(), after=()):
        targets = []
        offsets = []
        for arrays, groups in self.pieces(0):
            count = arrays[0].shape[0]
            parts = [(array, None, k * count) for k, array in enumerate(arrays)]
            targets.append(((count * len(arrays),) + arrays[0].shape[1:], parts))
            offsets.append([offset for group in groups for offset in group])
        self.flats, passing = self.join(targets, passing, after)
        self.offsets = offsets
        return passing

    def send_across(self):
        stride = self.table["c"][0]
        self.state = []
        fresh = []
        for arrays, offsets in self.pieces(1):
            sent = [exchange(array, stride) for array in arrays]
            fresh += sent
            self.state.append(
                (
                    arrays + sent,
                    offsets + [[offset ^ stride for offset in group] for group in offsets],
                )
            )
        return fresh

    def done(self):
        halves = []
        me = device_index()
        total = lax.axis_size(AXES)
        for arrays, offsets in self.state:
            if not self.plain:
                halves.append(Half(arrays, offsets, self.rows))
            else:
                flat = jnp.concatenate(arrays)
                spots = jnp.argsort(jnp.array([o for group in offsets for o in group]) ^ me)
                flat = jnp.take(flat, spots, axis=0).reshape(1, total * self.rows, -1)
                halves.append(Half([flat], None, total * self.rows))
        return halves


class Scatter:
    def __init__(self, me, parts, turns, plain):
        self.me = me
        self.parts = parts
        self.turns = turns
        self.plain = plain
        self.table = {name: (stride, size) for name, stride, size in digits()}

    def send_across(self):
        stride = self.table["c"][0]
        sizes = tuple(self.table[name][1] for name in ("z", "y", "x"))
        fresh = [exchange(send, stride) for _, send in self.parts]
        self.state = []
        for (keep, _), received in zip(self.parts, fresh):
            terms = [keep, received]
            if self.plain:
                rows = keep.shape[0] * keep.shape[1] // (sizes[0] * sizes[1] * sizes[2])
                terms = [term.reshape(sizes + (rows, keep.shape[2])) for term in terms]
            self.state.append((["z", "y", "x"], terms))
        return fresh

    def send(self, turn, after=()):
        fresh = []
        if not self.plain:
            names = [ways[turn] for ways in self.turns]
            if turn < 2:
                pairs = run_fold(
                    self.me, [(terms, name) for (_, terms), name in zip(self.state, names)], after
                )
            else:
                pairs = run_fold_z(self.me, [terms for _, terms in self.state], after)
            self.state = []
            for (kept, *sends), name in zip(pairs, names):
                stride = self.table[name][0]
                sent = [exchange(send, (k + 1) * stride) for k, send in enumerate(sends)]
                fresh += sent
                self.state.append((None, [kept] + sent))
            return fresh
        me = device_index()
        for number, (left, terms) in enumerate(self.state):
            name = self.turns[number][turn]
            stride, size = self.table[name]
            mine = (me // stride) % size
            axis = left.index(name)

            def part(index):
                return lowered(
                    sum(
                        lax.dynamic_index_in_dim(term, index, axis, keepdims=False).astype(jnp.float32)
                        for term in terms
                    )
                )

            sent = [exchange(part(mine ^ k), k * stride) for k in range(1, size)]
            fresh += sent
            self.state[number] = ([entry for entry in left if entry != name], [part(mine)] + sent)
        return fresh

    def done(self):
        return [sum(term.astype(jnp.float32) for term in terms) for _, terms in self.state]


def share(values):
    total = lax.axis_size(AXES)
    spread = jnp.broadcast_to(values[None], (total,) + values.shape)
    return lax.all_to_all(spread, AXES, 0, 0, tiled=True)


def on_device(
    pixels,
    labels,
    partner,
    pair_on,
    step_count,
    matrices,
    kv_weight,
    norm_gains,
    head_weight,
    latent_init,
    matrices_first,
    kv_first,
    gains_first,
    head_first,
    latent_first,
    matrices_second,
    kv_second,
    gains_second,
    head_second,
    latent_second,
):
    axis_count = lax.axis_size(AXES)
    n_narrow = lax.axis_size("narrow")
    index = device_index()
    me = jnp.stack([index, jnp.int32(n_narrow)]).astype(jnp.int32)
    micro = pixels.shape[0]
    tokens = latent_init.shape[1]
    width = matrices.shape[1] // 10
    rows = matrices.shape[0]
    channels = pixels.shape[3]
    wide_channels = -(-channels // 128) * 128
    classes = head_weight.shape[1]

    half = width // 2
    small_columns = tokens + 128
    plain = rows % 16 != 0 or tuple(size for _, _, size in digits()) != (4, 2, 2, 2)
    pictures = jnp.pad(pixels[:, 0], ((0, 0), (0, 0), (0, wide_channels - channels)))
    blocks = ((0, 2), (2, 4), (4, 8), (8, 10))
    shards = run_shards(matrices, kv_weight, norm_gains, head_weight, latent_init, blocks)
    lefts = [small_columns] + [(end - begin) * half for begin, end in blocks] + [half]
    chunks = [Gather(shard, left, plain) for shard, left in zip(shards, lefts)]

    a, b, c, d, e, f = chunks
    a.send_z()
    b.send_z()
    (c.shard,) = a.join_z([c.shard])
    a.send(0)
    c.send_z()
    (d.shard,) = b.join_z([d.shard], after=a.flats)
    b.send(0)
    a.join_first(after=b.flats)
    a.send(1)
    d.send_z()
    (e.shard,) = c.join_z([e.shard], after=a.flats)
    c.send(0)
    b.join_first(after=c.flats)
    b.send(1)
    a.send_across()
    e.send_z()
    (f.shard,) = d.join_z([f.shard], after=b.flats)
    d.send(0)
    c.join_first(after=d.flats)
    c.send(1)
    b.send_across()
    weights = {}
    small_half, kv_half = a.done()
    weights[0], weights[1] = [(entry, 0) for entry in b.done()]
    kv_column = 0
    if kv_half.offsets is None:
        array = kv_half.arrays[0].reshape(axis_count, rows, 2, wide_channels)
        array = array.transpose(0, 2, 1, 3).reshape(1, 2 * width, wide_channels)
        kv_half = Half([array], None, 2 * width)
    latent_one, blended, attend, pairs, initial, hidden_zero, queries, scales = run_cross_forward(
        me, pictures, (small_half, 0), (kv_half, 0), weights[0], weights[1], width, tokens,
        after=c.flats,
    )
    f.send_z()
    e.join_z(after=[latent_one])
    e.send(0)
    d.join_first(after=e.flats)
    d.send(1)
    c.send_across()
    weights[2], weights[3] = [(entry, 0) for entry in c.done()]
    latent_two, hidden_one, active_one, steep_one = run_feed_forward(
        me, scales, latent_one, weights[2], weights[3], 2, micro, False,
        after=d.flats,
    )
    f.join_z(after=[latent_two])
    f.send(0)
    e.join_first(after=f.flats)
    e.send(1)
    d.send_across()
    left, right = d.done()
    for number in range(2):
        weights[4 + number] = (left, number * width)
        weights[6 + number] = (right, number * width)
    latent_three, hidden_two, packed, attend_self, blended_self = run_self_forward(
        me, scales, latent_two, weights[4], weights[5], weights[6], weights[7], micro,
        after=e.flats,
    )
    f.join_first(after=[latent_three])
    f.send(1)
    e.send_across()
    weights[8], weights[9] = [(entry, 0) for entry in e.done()]
    result, hidden_three, active_three, steep_three, pooled = run_feed_forward(
        me, scales, latent_three, weights[8], weights[9], 6, micro, True,
        after=f.flats,
    )
    f.send_across()
    marks = jnp.stack(
        [labels[:, 0] // 256, labels[:, 0] % 256, partner[:, 0] // 256, partner[:, 0] % 256, pair_on[:, 0]],
        axis=1,
    )
    marks = jnp.pad(lowered(marks), ((0, 0), (0, MARKS - marks.shape[1])))
    pooled_all = share(jnp.concatenate([pooled.reshape(micro, width), marks], axis=1))
    pooled_all = pooled_all.reshape(axis_count * micro, width + MARKS)
    loss_tile, grad_logits, grad_pooled = run_losses(
        me, pooled_all, [(entry, 0) for entry in f.done()], classes, axis_count, micro
    )
    total_loss = loss_tile[0, 0]
    counts = loss_tile[1 : 1 + micro, 0].astype(jnp.int32)
    pooled_rows = lax.dynamic_slice_in_dim(pooled_all, index * rows, rows, axis=1)
    grad_head = dot_tn(pooled_rows, grad_logits)[:, :classes]

    sender = Sender(width, n_narrow * rows)
    kv_sender = Sender(2 * width, 2 * n_narrow * rows)
    turns = (("x", "y", "z"), ("y", "x", "z"))
    wide_half = width + half
    columns = (wide_half, wide_half)
    total_tokens = micro * tokens

    def triple(pairs_of):
        places = (
            [(0, half, 0, 0), (half, width, 0, half)],
            [(0, half, 1, 0), (half, width, 1, half)],
            [(0, half, 0, width), (half, width, 1, width)],
        )
        return [(lefts, rights, place) for (lefts, rights), place in zip(pairs_of, places)]

    def single(left, right):
        return [(left, 0, total_tokens)], [(right, 0, 0)]

    upstream, gain_high, low, before, behind = run_feed_backward(
        me, scales, latent_three, (result, grad_pooled), steep_three, weights[8], weights[9], 6, micro, True
    )
    parts = run_weights(
        me,
        triple((single(active_three, low), single(hidden_three, before), single(blended_self, behind))),
        sender,
        columns,
    )
    one = Scatter(me, [parts[0:2], parts[2:4]], turns, plain)
    one_c = one.send_across()
    grads = []
    gain_mid = 0.0
    onward = None
    for crop in range(micro):
        waits = ()
        if crop == 1:
            one_x = one.send(0, after=[onward])
            waits = [one.state[0][1][0]]
        grad_packed, onward, gain = run_self_backward(
            crop, me, scales, latent_two, upstream, (packed, attend_self),
            weights[4], weights[5], weights[6], weights[7], micro, onward, after=waits,
        )
        grads.append(grad_packed)
        gain_mid = gain_mid + gain
    upstream = onward
    one_y = one.send(1, after=[onward])
    parts = run_weights(
        me,
        triple(
            [
                (
                    [(hidden_two, crop * tokens, tokens) for crop in range(micro)],
                    [(grads[crop], number * width, 0) for crop in range(micro)],
                )
                for number in range(3)
            ]
        ),
        sender,
        columns,
        after=[one.state[0][1][0]],
    )
    two = Scatter(me, [parts[0:2], parts[2:4]], turns, plain)
    two_c = two.send_across()
    one_z = one.send(2, after=[parts[0]])
    upstream, gain_low, low, before, behind = run_feed_backward(
        me, scales, latent_one, upstream, steep_one, weights[2], weights[3], 2, micro, False,
        after=[one.state[0][1][0]],
    )
    two_x = two.send(0, after=[low])
    parts = run_weights(
        me,
        triple((single(active_one, low), single(hidden_one, before), single(blended, behind))),
        sender,
        columns,
        after=[two.state[0][1][0]],
    )
    three = Scatter(me, [parts[0:2], parts[2:4]], turns, plain)
    three_c = three.send_across()
    two_y = two.send(1, after=[parts[0]])
    gains = jnp.concatenate(
        [
            jnp.zeros((2, width), jnp.float32),
            gain_low[:2],
            gain_mid[:2],
            gain_high[:4],
            jnp.zeros((6, width), jnp.float32),
        ]
    )
    grad_queries, grad_pairs, *small_parts = run_cross_backward(
        me, scales, initial, upstream, (queries, attend, pairs), gains,
        weights[0], weights[1], micro, sender, after=[two.state[0][1][0]],
    )
    three_x = three.send(0, after=[grad_queries])
    two_z = two.send(2, after=[three.state[0][1][0]])
    parts = run_last_weights(
        me, hidden_zero, grad_queries, grad_pairs, pictures.reshape(-1, wide_channels), sender, kv_sender,
        after=[two.state[0][1][0]],
    )
    four = Scatter(
        me, [parts[0:2], small_parts, parts[2:4]], (turns[0], turns[1], turns[1]), plain
    )
    four.send_across()
    three.send(1, after=[parts[0]])
    four.send(0, after=[three.state[0][1][0]])
    three.send(2, after=[four.state[0][1][0]])
    four.send(1, after=[three.state[0][1][0]])
    four.send(2)
    nine, eight = one.done()
    four_, five = two.done()
    three_, two_ = three.done()
    zero, rest, grad_kv = four.done()
    grad_matrices = jnp.concatenate(
        [
            zero,
            three_[:, width:],
            two_[:, width:],
            two_[:, :width],
            three_[:, :width],
            four_[:, :width],
            five[:, :width],
            four_[:, width:],
            five[:, width:],
            nine[:, width:],
            eight[:, width:],
            eight[:, :width],
            nine[:, :width],
        ],
        axis=1,
    )
    shares = (
        grad_matrices,
        grad_kv[:, :channels],
        rest[:, tokens : tokens + 10],
        grad_head,
        rest[:, :tokens],
    )
    square = jnp.zeros((), jnp.float32)
    for member in shares:
        square = square + jnp.sum(member * member)
    square = jnp.sum(share(jnp.broadcast_to(square, (128,))), axis=0)[0]
    grad_norm = jnp.sqrt(square)
    factor = jnp.minimum(1.0, THRESH / grad_norm)
    correction = 1.0 - jnp.power(0.5, step_count[0].astype(jnp.float32))
    masters = (matrices, kv_weight, norm_gains, head_weight, latent_init)
    firsts = (matrices_first, kv_first, gains_first, head_first, latent_first)
    seconds = (matrices_second, kv_second, gains_second, head_second, latent_second)
    results = []
    for index, (grad_item, master, moment_one, moment_two) in enumerate(
        zip(shares, masters, firsts, seconds)
    ):
        clipped = grad_item * factor
        moment_one = 0.5 * moment_one + 0.5 * clipped
        moment_two = 0.5 * moment_two + 0.5 * clipped * clipped
        if index == 2 or index == 4:
            results = results + [moment_one, moment_two, clipped]
        else:
            master = master - RATE * (
                moment_one / correction / (jnp.sqrt(moment_two / correction) + TINY)
                + DECAY * master
            )
            results = results + [moment_one, moment_two, master]
    return (
        total_loss,
        grad_norm,
        counts,
        results[0],
        results[1],
        results[2],
        results[3],
        results[4],
        results[5],
        results[6],
        results[7],
        results[8],
        results[9],
        results[10],
        results[11],
        results[12],
        results[13],
        results[14],
    )


def solution(mesh):
    in_specs = (
        P(None, ("wide", "narrow"), None, None),
        P(None, ("wide", "narrow")),
        P(None, ("wide", "narrow")),
        P(None, ("wide", "narrow")),
        P(),
        P(("wide", "narrow"), None),
        P(("wide", "narrow"), None),
        P(("wide", "narrow"), None),
        P(("wide", "narrow"), None),
        P(("wide", "narrow"), None),
        P(("wide", "narrow"), None),
        P(("wide", "narrow"), None),
        P(("wide", "narrow"), None),
        P(("wide", "narrow"), None),
        P(("wide", "narrow"), None),
        P(("wide", "narrow"), None),
        P(("wide", "narrow"), None),
        P(("wide", "narrow"), None),
        P(("wide", "narrow"), None),
        P(("wide", "narrow"), None),
    )
    out_specs = (
        P(),
        P(),
        P(),
        P(("wide", "narrow"), None),
        P(("wide", "narrow"), None),
        P(("wide", "narrow"), None),
        P(("wide", "narrow"), None),
        P(("wide", "narrow"), None),
        P(("wide", "narrow"), None),
        P(("wide", "narrow"), None),
        P(("wide", "narrow"), None),
        P(("wide", "narrow"), None),
        P(("wide", "narrow"), None),
        P(("wide", "narrow"), None),
        P(("wide", "narrow"), None),
        P(("wide", "narrow"), None),
        P(("wide", "narrow"), None),
        P(("wide", "narrow"), None),
    )
    return jax.shard_map(
        on_device, mesh=mesh, in_specs=in_specs, out_specs=out_specs, check_vma=False
    )
```

```python
import functools

import jax
import jax.numpy as jnp
from jax import lax
from jax.experimental import pallas as pl
from jax.experimental.pallas import tpu as pltpu
from jax.sharding import PartitionSpec as P

HEADS = 8
AXES = ("wide", "narrow")

EPSILON = 1e-05
RATE = 0.03
DECAY = 0.1
TINY = 1e-08
THRESH = 0.01
BEND = 0.044715
MARKS = 128
SLOPE = 0.7978845608028654
VMEM = pltpu.VMEM
MIB = 1 << 20
BIG = 48
PACE = 0.5


def lowered(values):
    return values.astype(jnp.bfloat16)


def dot_nn(first_op, second_op):
    return jnp.dot(first_op, second_op, preferred_element_type=jnp.float32)


def dot_tn(first_op, second_op):
    return lax.dot_general(
        first_op, second_op, (((0,), (0,)), ((), ())), preferred_element_type=jnp.float32
    )


def dot_nt(first_op, second_op):
    return lax.dot_general(
        first_op, second_op, (((1,), (1,)), ((), ())), preferred_element_type=jnp.float32
    )


def standard(inputs):
    center = inputs - jnp.mean(inputs, axis=-1, keepdims=True)
    scale = lax.rsqrt(jnp.mean(center * center, axis=-1, keepdims=True) + EPSILON)
    return center * scale, scale


def layer_norm(inputs, scales, column):
    return standard(inputs)[0] * scales[column : column + 1, :] + scales[column + 1 : column + 2, :]


def norm_back(inputs, scales, column, upstream):
    unit, scale = standard(inputs)
    gain = jnp.sum(upstream * unit, axis=0, keepdims=True)
    bias = jnp.sum(upstream, axis=0, keepdims=True)
    inner = upstream * scales[column : column + 1, :]
    back = scale * (
        inner
        - jnp.mean(inner, axis=-1, keepdims=True)
        - unit * jnp.mean(inner * unit, axis=-1, keepdims=True)
    )
    return back, gain, bias


def gelu_both(values):
    square = values * values
    bent = jnp.tanh(SLOPE * values * (1.0 + BEND * square))
    half = 0.5 * (1.0 + bent)
    steep = half + 0.5 * values * (1.0 - bent * bent) * SLOPE * (1.0 + 3.0 * BEND * square)
    return values * half, steep


def softmax(scores):
    raised = jnp.exp(scores - jnp.max(scores, axis=-1, keepdims=True))
    return raised * (1.0 / jnp.sum(raised, axis=-1, keepdims=True))


def softmax_back(attend, upstream):
    return attend * (upstream - jnp.sum(upstream * attend, axis=-1, keepdims=True))


class Half:
    def __init__(self, arrays, offsets, rows):
        self.arrays = arrays
        self.offsets = offsets
        self.rows = rows

    def start(self, refs, me, target, sem, column, stride=None, shift=0):
        width = target.shape[1]
        if self.offsets is None:
            pltpu.make_async_copy(refs[0].at[0, :, column : column + width], target, sem).start()
            return
        stride = self.rows if stride is None else stride
        for ref, offsets in zip(refs, self.offsets):
            for group, offset in enumerate(offsets):
                spot = pl.multiple_of((me ^ offset) * stride + shift, self.rows)
                pltpu.make_async_copy(
                    ref.at[group, :, column : column + width],
                    target.at[pl.ds(spot, self.rows), :],
                    sem,
                ).start()


class Joint:
    def __init__(self, pieces):
        self.pieces = pieces
        self.arrays = [array for half, *_ in pieces for array in half.arrays]

    def start(self, refs, me, target, sem, column):
        at = 0
        for half, spot, first, last in self.pieces:
            count = len(half.arrays)
            half.start(refs[at : at + count], me, target.at[:, first:last], sem, spot)
            at += count


def arrived(target, sem):
    pltpu.make_async_copy(target, target, sem).wait()


def cost(micros):
    return pl.CostEstimate(flops=int(micros * PACE * 1.1e9), bytes_accessed=1 << 10, transcendentals=0)


def params(mib, dims=1, big=None):
    return pltpu.CompilerParams(
        vmem_limit_bytes=(big or max(mib, BIG)) * MIB, dimension_semantics=("arbitrary",) * dims
    )


def launch(kernel, after, operands, in_specs, **rest):
    extra = len(after)

    def inner(*refs):
        kernel(*refs[: len(operands)], *refs[len(operands) + extra :])

    return pl.pallas_call(inner, in_specs=list(in_specs) + [ANY] * extra, **rest)(*operands, *after)


ANY = pl.BlockSpec(memory_space=pl.ANY)
SMEM = pl.BlockSpec(memory_space=pltpu.SMEM)


def whole(shape):
    return pl.BlockSpec(shape, lambda *ids: (0,) * len(shape))


def by_crop(shape, rank=1):
    return pl.BlockSpec(shape, lambda m, *ids: (m,) + (0,) * (len(shape) - 1))


def shaped(shape, dtype):
    return jax.ShapeDtypeStruct(shape, dtype)


def run_cross_forward(me, pictures, small, kv, first, second, width, tokens, after=()):
    micro, spots, channels = pictures.shape
    parts = (small, kv, first, second)
    counts = [len(part[0].arrays) for part in parts]
    small_columns = tokens + 128

    def kernel(me_ref, pic_ref, *refs):
        groups = []
        at = 0
        for count in counts:
            groups.append(refs[at : at + count])
            at += count
        latent_ref, blended_ref, attend_ref, pair_ref, initial_ref, hidden_ref, query_ref, scale_ref = refs[at : at + 8]
        small_s, kv_s, first_s, second_s, sems = refs[at + 8 :]
        me_now = me_ref[0]
        step = pl.program_id(0)

        @pl.when(step == 0)
        def _():
            small[0].start(groups[0], me_now, small_s, sems.at[0], small[1])
            if kv[0].offsets is None:
                kv[0].start(groups[1], me_now, kv_s, sems.at[1], 0)
            else:
                rows = kv[0].rows
                kv[0].start(groups[1], me_now, kv_s, sems.at[1], kv[1], 2 * rows, 0)
                kv[0].start(groups[1], me_now, kv_s, sems.at[1], kv[1] + channels, 2 * rows, rows)
            first[0].start(groups[2], me_now, first_s, sems.at[2], first[1])
            second[0].start(groups[3], me_now, second_s, sems.at[3], second[1])
            arrived(small_s, sems.at[0])
            turned = small_s[...].astype(jnp.float32).T
            initial_ref[...] = turned[:tokens]
            scale_ref[...] = turned[tokens : tokens + 16]
            hidden_ref[...] = lowered(layer_norm(initial_ref[...], scale_ref, 0))
            arrived(first_s, sems.at[2])
            query_ref[...] = lowered(dot_nn(hidden_ref[...], first_s[...]))
            arrived(kv_s, sems.at[1])
            arrived(second_s, sems.at[3])

        pair_ref[0] = lowered(dot_nt(pic_ref[0], kv_s[...]))
        scores = dot_nt(query_ref[...], pair_ref[0, :, :width]) * width ** (-0.5)
        attend = softmax(scores)
        attend_ref[0] = attend
        blended_ref[...] = lowered(dot_nn(lowered(attend), pair_ref[0, :, width:]))
        latent_ref[...] = initial_ref[...] + dot_nn(blended_ref[...], second_s[...])

    total = micro * tokens
    return launch(
        kernel,
        after,
        [me, pictures, *[array for part in parts for array in part[0].arrays]],
        grid=(micro,),
        in_specs=[SMEM, by_crop((1, spots, channels))] + [ANY] * sum(counts),
        out_specs=[
            by_crop((tokens, width)),
            by_crop((tokens, width)),
            by_crop((1, tokens, spots)),
            by_crop((1, spots, 2 * width)),
            whole((tokens, width)),
            whole((tokens, width)),
            whole((tokens, width)),
            whole((16, width)),
        ],
        out_shape=[
            shaped((total, width), jnp.float32),
            shaped((total, width), jnp.bfloat16),
            shaped((micro, tokens, spots), jnp.float32),
            shaped((micro, spots, 2 * width), jnp.bfloat16),
            shaped((tokens, width), jnp.float32),
            shaped((tokens, width), jnp.bfloat16),
            shaped((tokens, width), jnp.bfloat16),
            shaped((16, width), jnp.float32),
        ],
        scratch_shapes=[
            VMEM((width, small_columns), jnp.bfloat16),
            VMEM((2 * width, channels), jnp.bfloat16),
            VMEM((width, width), jnp.bfloat16),
            VMEM((width, width), jnp.bfloat16),
            pltpu.SemaphoreType.DMA((4,)),
        ],
        compiler_params=params(48),
        cost_estimate=cost(18),
        name="cross_forward",
    )


def run_feed_forward(me, scales, latent, first, second, column, micro, pool, prior=None, after=()):
    total, width = latent.shape
    tokens = total // micro
    parts = [first, second] + ([prior[1]] if prior else [])
    counts = [len(part[0].arrays) for part in parts]

    def kernel(me_ref, scale_ref, latent_ref, *refs):
        if prior:
            prior_refs, refs = refs[:micro], refs[micro:]
        groups = []
        at = 0
        for count in counts:
            groups.append(refs[at : at + count])
            at += count
        out_ref, hidden_ref, active_ref, steep_ref = refs[at : at + 4]
        more = refs[at + 4 : -1 - len(parts)]
        blocks, sems = refs[-1 - len(parts) : -1], refs[-1]
        first_s, second_s = blocks[:2]
        step = pl.program_id(0)

        @pl.when(step == 0)
        def _():
            for number in range(len(parts) - 1, -1, -1) if prior else range(len(parts)):
                parts[number][0].start(
                    groups[number], me_ref[0], blocks[number], sems.at[number], parts[number][1]
                )

        source_ref = latent_ref
        if prior:
            source_ref = more[-1]

            @pl.when(step == 0)
            def _():
                arrived(blocks[2], sems.at[2])

            for crop in range(micro):

                @pl.when(step == crop)
                def _():
                    source_ref[...] = latent_ref[...] + dot_nn(prior_refs[crop][...], blocks[2][...])

        hidden_ref[...] = lowered(layer_norm(source_ref[...], scale_ref, column))

        @pl.when(step == 0)
        def _():
            arrived(first_s, sems.at[0])

        pieces = 4
        span = width // pieces
        for piece in range(pieces):
            cut = slice(piece * span, (piece + 1) * span)
            active, steep = gelu_both(dot_nn(hidden_ref[...], first_s[:, cut]))
            active_ref[:, cut] = lowered(active)
            steep_ref[:, cut] = lowered(steep)

        @pl.when(step == 0)
        def _():
            arrived(second_s, sems.at[1])

        out_ref[...] = source_ref[...] + dot_nn(active_ref[...], second_s[...])
        if pool:
            normed = layer_norm(out_ref[...], scale_ref, 8)
            more[0][0] = lowered(jnp.mean(normed, axis=0, keepdims=True))

    out_shape = [shaped((total, width), jnp.float32)] + [shaped((total, width), jnp.bfloat16)] * 3
    out_specs = [by_crop((tokens, width))] * 4
    if pool:
        out_shape.append(shaped((micro, 1, width), jnp.bfloat16))
        out_specs.append(by_crop((1, 1, width)))
    in_specs = [SMEM, whole((16, width)), by_crop((tokens, width))]
    operands = [me, scales, latent]
    if prior:
        out_shape.append(shaped((total, width), jnp.float32))
        out_specs.append(by_crop((tokens, width)))
        in_specs += [whole((tokens, width))] * micro
        operands += prior[0]
    return launch(
        kernel,
        after,
        operands + [array for part in parts for array in part[0].arrays],
        in_specs + [ANY] * sum(counts),
        grid=(micro,),
        out_specs=out_specs,
        out_shape=out_shape,
        scratch_shapes=[VMEM((width, width), jnp.bfloat16)] * len(parts)
        + [pltpu.SemaphoreType.DMA((len(parts),))],
        compiler_params=params(48, big=60),
        cost_estimate=cost(18),
        name="feed_forward",
    )


def run_self_forward(crop, me, scales, latent, query, key, value, micro, after=()):
    total, width = latent.shape
    tokens = total // micro
    part = width // HEADS
    pair = 2 * part
    turns = HEADS // 2
    parts = (query, key, value)
    counts = [len(entry[0].arrays) for entry in parts]

    def kernel(me_ref, scale_ref, latent_ref, *refs):
        groups = []
        at = 0
        for count in counts:
            groups.append(refs[at : at + count])
            at += count
        hidden_ref, packed_ref, attend_ref, blended_ref, packed_s, sems = refs[at:]
        turn = pl.program_id(0)

        @pl.when(turn == 0)
        def _():
            for number in range(3):
                parts[number][0].start(
                    groups[number], me_ref[0], packed_s.at[number], sems.at[number], parts[number][1]
                )
            hidden_ref[...] = lowered(layer_norm(latent_ref[...], scale_ref, 4))
            for number in range(3):
                arrived(packed_s.at[number], sems.at[number])
                packed_ref[:, number * width : (number + 1) * width] = lowered(
                    dot_nn(hidden_ref[...], packed_s[number])
                )

        base = pl.multiple_of(turn * pair, pair)
        queries = packed_ref[:, pl.ds(base, pair)]
        keys = packed_ref[:, pl.ds(pl.multiple_of(width + base, pair), pair)]
        values = packed_ref[:, pl.ds(pl.multiple_of(2 * width + base, pair), pair)]
        joined = []
        for head in range(2):
            cut = slice(head * part, (head + 1) * part)
            attend = softmax(dot_nt(queries[:, cut], keys[:, cut]) * part ** (-0.5))
            attend_ref[head] = attend
            joined.append(lowered(dot_nn(lowered(attend), values[:, cut])))
        blended_ref[:, pl.ds(base, pair)] = jnp.concatenate(joined, axis=1)

    return launch(
        kernel,
        after,
        [me, scales, latent, *[array for entry in parts for array in entry[0].arrays]],
        [
            SMEM,
            whole((16, width)),
            pl.BlockSpec((tokens, width), lambda h: (crop, 0)),
        ]
        + [ANY] * sum(counts),
        grid=(turns,),
        out_specs=[
            whole((tokens, width)),
            whole((tokens, 3 * width)),
            pl.BlockSpec((2, tokens, tokens), lambda h: (h, 0, 0)),
            whole((tokens, width)),
        ],
        out_shape=[
            shaped((tokens, width), jnp.bfloat16),
            shaped((tokens, 3 * width), jnp.bfloat16),
            shaped((HEADS, tokens, tokens), jnp.float32),
            shaped((tokens, width), jnp.bfloat16),
        ],
        scratch_shapes=[
            VMEM((3, width, width), jnp.bfloat16),
            pltpu.SemaphoreType.DMA((3,)),
        ],
        compiler_params=params(48),
        cost_estimate=cost(14),
        name="self_forward",
    )


def run_losses(me, pooled, head, classes, examples, micro, after=()):
    count, width = pooled.shape[0], pooled.shape[1] - MARKS
    parts = (head[0], head[1])
    counts = [len(entry[0].arrays) for entry in parts]
    span = width // 2

    def kernel(me_ref, pooled_ref, *refs):
        groups = (refs[: counts[0]], refs[counts[0] : counts[0] + counts[1]])
        loss_ref, logits_ref, grad_ref, left_s, right_s, sems = refs[counts[0] + counts[1] :]
        me_now = me_ref[0]
        halves = (left_s, right_s)
        for number in range(2):
            parts[number][0].start(
                groups[number], me_now, halves[number], sems.at[number], parts[number][1]
            )
        rows = lax.broadcasted_iota(jnp.int32, (count, 1), 0)
        turn = rows % micro
        marks = pooled_ref[:, width:].astype(jnp.float32)
        labels = (marks[:, 0:1] * 256.0 + marks[:, 1:2]).astype(jnp.int32)
        partner = (marks[:, 2:3] * 256.0 + marks[:, 3:4]).astype(jnp.int32)
        active = marks[:, 4:5]
        pooled_low = pooled_ref[:, :width]
        pooled_wide = pooled_low.astype(jnp.float32)
        columns = lax.broadcasted_iota(jnp.int32, (count, count), 1)
        aimed = lowered((columns == partner * micro + turn).astype(jnp.float32))
        distance = pooled_wide - dot_nn(aimed, pooled_low)
        divisor = jnp.zeros((count, 1), jnp.float32)
        for number in range(micro):
            here = (turn == number).astype(jnp.float32)
            counted = jnp.sum(here * active, axis=0, keepdims=True)
            loss_ref[1 + number : 2 + number] = jnp.broadcast_to(counted, (1, 128))
            counted = jnp.maximum(counted, 1.0)
            divisor = divisor + here * (counted * width**0.5)
        agreement = active * jnp.sum(distance * distance, axis=-1, keepdims=True) / divisor
        pull = (2.0 / micro) * (active / divisor) * distance
        for number in range(2):
            arrived(halves[number], sems.at[number])
        logits = jnp.concatenate([dot_nn(pooled_low, half[...]) for half in halves], axis=1)
        column = lax.broadcasted_iota(jnp.int32, (count, 2 * span), 1)
        logits = jnp.where(column < classes, logits, -1e30)
        top = jnp.max(logits, axis=-1, keepdims=True)
        raised = jnp.exp(logits - top)
        mass = jnp.sum(raised, axis=-1, keepdims=True)
        hot = (column == labels).astype(jnp.float32)
        entropy = top + jnp.log(mass) - jnp.sum(logits * hot, axis=-1, keepdims=True)
        loss = jnp.sum(entropy / examples + agreement, axis=0, keepdims=True) / micro
        loss_ref[0:1] = jnp.broadcast_to(loss, (1, 128))
        grad_logits = lowered((raised / mass - hot) / (examples * micro))
        logits_ref[...] = grad_logits
        grad = pull + sum(
            dot_nt(grad_logits[:, number * span : (number + 1) * span], halves[number][...])
            for number in range(2)
        )
        for number in range(micro):
            own = (rows == me_now * micro + number).astype(jnp.float32)
            aiming = ((partner == me_now) & (turn == number)).astype(jnp.float32)
            grad_ref[number] = jnp.sum(own * grad - aiming * pull, axis=0, keepdims=True)

    return launch(
        kernel,
        after,
        [me, pooled, *[array for entry in parts for array in entry[0].arrays]],
        in_specs=[SMEM, whole(pooled.shape)] + [ANY] * sum(counts),
        grid=(1,),
        out_specs=[whole((8, 128)), whole((count, width)), whole((micro, 1, width))],
        out_shape=[
            shaped((8, 128), jnp.float32),
            shaped((count, width), jnp.bfloat16),
            shaped((micro, 1, width), jnp.float32),
        ],
        scratch_shapes=[
            VMEM((width, span), jnp.bfloat16),
            VMEM((width, span), jnp.bfloat16),
            pltpu.SemaphoreType.DMA((2,)),
        ],
        compiler_params=pltpu.CompilerParams(vmem_limit_bytes=24 * MIB),
        cost_estimate=cost(5),
        name="losses",
    )


class Sender:
    def __init__(self, total, core_rows):
        self.total = total
        self.core_rows = core_rows
        self.groups = total // (2 * core_rows)

    def shapes(self, columns):
        return [shaped((self.groups, self.core_rows, columns), jnp.bfloat16)] * 2

    def start(self, source, core, keep, send, column, sem):
        width = source.shape[1]
        rows = self.core_rows
        for group in range(self.groups):
            for target, side in ((send, 1 - core), (keep, core)):
                spot = pl.multiple_of((2 * group + side) * rows, rows)
                pltpu.make_async_copy(
                    source.at[pl.ds(spot, rows), :],
                    target.at[group, :, column : column + width],
                    sem,
                ).start()


    def start_rows(self, source, core, keep, send, column, rows, side, sem):
        width = source.shape[1]
        each = self.core_rows // rows
        for group in range(self.groups):
            for target, half in ((send, 1 - core), (keep, core)):
                for device in range(each):
                    first = ((2 * group + half) * each + device) * 2 * rows + side * rows
                    pltpu.make_async_copy(
                        source.at[pl.ds(pl.multiple_of(first, rows), rows), :],
                        target.at[group, device * rows : (device + 1) * rows, column : column + width],
                        sem,
                    ).start()


def run_feed_backward(
    me, scales, latent, upstream, steep, first, second, column, micro, pool, crop=None, after=()
):
    total, width = latent.shape
    tokens = total // micro
    parts = (first, second)
    counts = [len(entry[0].arrays) for entry in parts]
    span = width // 2

    def kernel(me_ref, scale_ref, latent_ref, up_ref, *refs):
        if pool:
            pooled_ref, refs = refs[0], refs[1:]
        steep_ref, refs = refs[0], refs[1:]
        first_refs, refs = refs[: counts[0]], refs[counts[0] :]
        second_refs, refs = refs[: counts[1]], refs[counts[1] :]
        out_ref, gain_ref, low_ref, before_ref, after_ref, first_s, second_s, sems = refs
        step = pl.program_id(0)

        @pl.when(step == 0)
        def _():
            second[0].start(second_refs, me_ref[0], second_s, sems.at[1], second[1])
            first[0].start(first_refs, me_ref[0], first_s, sems.at[0], first[1])
            gain_ref[...] = jnp.zeros(gain_ref.shape, jnp.float32)

        if pool:
            spread = jnp.broadcast_to(pooled_ref[0] / tokens, (tokens, width))
            upstream, gain, bias = norm_back(up_ref[...], scale_ref, 8, spread)
            gain_ref[2:3] += gain
            gain_ref[3:4] += bias
            out_ref[...] = upstream
        else:
            out_ref[...] = up_ref[...]
        low_ref[...] = lowered(out_ref[...])

        @pl.when(step == 0)
        def _():
            arrived(second_s, sems.at[1])

        for number in range(2):
            cut = slice(number * span, (number + 1) * span)
            grad = dot_nt(low_ref[...], second_s[cut, :])
            before_ref[:, cut] = lowered(grad * steep_ref[:, cut].astype(jnp.float32))

        @pl.when(step == 0)
        def _():
            arrived(first_s, sems.at[0])

        back, gain, bias = norm_back(
            latent_ref[...], scale_ref, column, dot_nt(before_ref[...], first_s[...])
        )
        gain_ref[0:1] += gain
        gain_ref[1:2] += bias
        out_ref[...] += back
        after_ref[...] = lowered(out_ref[...])

    rows_of = by_crop((tokens, width))
    if crop is not None:
        rows_of = pl.BlockSpec((tokens, width), lambda m: (crop, 0))
        total = tokens
    in_specs = [SMEM, whole((16, width)), rows_of, rows_of]
    operands = [me, scales, latent]
    if pool:
        in_specs.append(by_crop((1, 1, width)))
        operands += list(upstream)
    else:
        operands.append(upstream)
    in_specs += [rows_of] + [ANY] * sum(counts)
    operands += [steep] + [array for entry in parts for array in entry[0].arrays]
    return launch(
        kernel,
        after,
        operands,
        in_specs,
        grid=(micro if crop is None else 1,),
        out_specs=[by_crop((tokens, width)), whole((8, width))] + [by_crop((tokens, width))] * 3,
        out_shape=[shaped((total, width), jnp.float32), shaped((8, width), jnp.float32)]
        + [shaped((total, width), jnp.bfloat16)] * 3,
        scratch_shapes=[
            VMEM((width, width), jnp.bfloat16),
            VMEM((width, width), jnp.bfloat16),
            pltpu.SemaphoreType.DMA((2,)),
        ],
        compiler_params=params(48, big=60),
        cost_estimate=cost(16 if crop is None else 9),
        name="feed_backward",
    )


def run_self_backward(crop, me, scales, latent, upstream, stored, query, key, value, out, micro, onward, after=()):
    total, width = latent.shape
    tokens = total // micro
    part = width // HEADS
    pair = 2 * part
    turns = HEADS // 2
    packed, attend = stored
    parts = (query, key, value, out)
    counts = [len(entry[0].arrays) for entry in parts]

    def kernel(me_ref, scale_ref, latent_ref, up_ref, packed_ref, attend_ref, *refs):
        groups = []
        at = 0
        for count in counts:
            groups.append(refs[at : at + count])
            at += count
        if onward is not None:
            at += 1
        grad_ref, out_ref, gain_ref, packed_s, out_s, blend_s, sems = refs[at:]
        turn = pl.program_id(0)

        @pl.when(turn == 0)
        def _():
            out[0].start(groups[3], me_ref[0], out_s, sems.at[3], out[1])
            for number in range(3):
                parts[number][0].start(
                    groups[number], me_ref[0], packed_s.at[number], sems.at[number], parts[number][1]
                )
            arrived(out_s, sems.at[3])
            blend_s[...] = lowered(dot_nt(lowered(up_ref[...]), out_s[...]))

        base = pl.multiple_of(turn * pair, pair)
        queries = packed_ref[:, pl.ds(base, pair)]
        keys = packed_ref[:, pl.ds(pl.multiple_of(width + base, pair), pair)]
        values = packed_ref[:, pl.ds(pl.multiple_of(2 * width + base, pair), pair)]
        blends = blend_s[:, pl.ds(base, pair)]
        grads = ([], [], [])
        for head in range(2):
            cut = slice(head * part, (head + 1) * part)
            attend = attend_ref[head]
            grad_attend = dot_nt(blends[:, cut], values[:, cut])
            scores = lowered(softmax_back(attend, grad_attend) * part ** (-0.5))
            grads[2].append(lowered(dot_tn(lowered(attend), blends[:, cut])))
            grads[0].append(lowered(dot_nn(scores, keys[:, cut])))
            grads[1].append(lowered(dot_tn(scores, queries[:, cut])))
        for number in range(3):
            spot = pl.ds(pl.multiple_of(number * width + base, pair), pair)
            grad_ref[:, spot] = jnp.concatenate(grads[number], axis=1)

        @pl.when(turn == turns - 1)
        def _():
            for number in range(3):
                arrived(packed_s.at[number], sems.at[number])
            grad_hidden = sum(
                dot_nt(grad_ref[:, number * width : (number + 1) * width], packed_s[number])
                for number in range(3)
            )
            back, gain, bias = norm_back(latent_ref[...], scale_ref, 4, grad_hidden)
            gain_ref[0:1] = gain
            gain_ref[1:2] = bias
            out_ref[...] = up_ref[...] + back

    def crop_rows(columns):
        return pl.BlockSpec((tokens, columns), lambda h: (crop, 0))

    operands = [me, scales, latent, upstream, packed, attend]
    operands += [array for entry in parts for array in entry[0].arrays]
    aliases = {}
    if onward is not None:
        aliases = {len(operands): 1}
        operands.append(onward)
    return launch(
        kernel,
        after,
        operands,
        grid=(turns,),
        in_specs=[
            SMEM,
            whole((16, width)),
            crop_rows(width),
            crop_rows(width),
            whole((tokens, 3 * width)),
            pl.BlockSpec((2, tokens, tokens), lambda h: (h, 0, 0)),
        ]
        + [ANY] * (sum(counts) + len(aliases)),
        input_output_aliases=aliases,
        out_specs=[whole((tokens, 3 * width)), crop_rows(width), whole((8, width))],
        out_shape=[
            shaped((tokens, 3 * width), jnp.bfloat16),
            shaped((total, width), jnp.float32),
            shaped((8, width), jnp.float32),
        ],
        scratch_shapes=[
            VMEM((3, width, width), jnp.bfloat16),
            VMEM((width, width), jnp.bfloat16),
            VMEM((tokens, width), jnp.bfloat16),
            pltpu.SemaphoreType.DMA((4,)),
        ],
        compiler_params=params(56),
        cost_estimate=cost(20),
        name="self_backward",
    )


def run_weights(me, products, sender, after=()):
    flat = []
    for lefts, rights in products:
        for array, *_ in lefts + rights:
            if not any(array is known for known in flat):
                flat.append(array)
    where = {id(array): number for number, array in enumerate(flat)}
    width = products[0][0][0][0].shape[1]
    count = len(products)
    span = width // 2

    def kernel(me_ref, *refs):
        sources, (keep, send, mat_s), sems = refs[: len(flat)], refs[len(flat) : len(flat) + 3], refs[-1]
        held = refs[len(flat) + 3 : -1]
        core = (me_ref[0] // me_ref[1]) % 2
        copies = [
            pltpu.make_async_copy(source, target, sems.at[1 + number])
            for number, (source, target) in enumerate(zip(sources, held))
        ]
        for copy in copies:
            copy.start()
        there = set()
        for number, (lefts, rights) in enumerate(products):
            for array, *_ in lefts + rights:
                if where[id(array)] not in there:
                    there.add(where[id(array)])
                    copies[where[id(array)]].wait()
            for side in range(2):
                cut = slice(side * span, (side + 1) * span)
                mat_s[number, :, cut] = lowered(
                    sum(
                        dot_tn(
                            held[where[id(left)]][begin : begin + size, :],
                            held[where[id(right)]][
                                top : top + size, at + side * span : at + (side + 1) * span
                            ],
                        )
                        for (left, begin, size), (right, top, at) in zip(lefts, rights)
                    )
                )
            sender.start(mat_s.at[number], core, keep, send, number * width, sems.at[0])
        arrived(mat_s, sems.at[0])

    return launch(
        kernel,
        after,
        [me] + flat,
        [SMEM] + [ANY] * len(flat),
        out_specs=[ANY] * 2,
        out_shape=sender.shapes(count * width),
        scratch_shapes=[VMEM((count, width, width), jnp.bfloat16)]
        + [VMEM(array.shape, array.dtype) for array in flat]
        + [pltpu.SemaphoreType.DMA((1 + len(flat),))],
        compiler_params=pltpu.CompilerParams(vmem_limit_bytes=BIG * MIB),
        cost_estimate=cost(3 * count),
        name="weights",
    )


def run_cross_backward(
    crop, me, scales, initial, ups, stored, gains, first, second, micro, before, after=()
):
    tokens, width = ups[crop].shape
    queries, attend, pairs = stored
    spots = pairs.shape[1]
    parts = (first, second)
    counts = [len(entry[0].arrays) for entry in parts]
    small_columns = tokens + 128
    last = crop == micro - 1

    def kernel(me_ref, scale_ref, initial_ref, up_ref, query_ref, attend_ref, pair_ref, gains_ref, *refs):
        if before is not None:
            before_ref, refs = refs[0], refs[1:]
        if last:
            others, refs = refs[: micro - 1], refs[micro - 1 :]
        first_refs, refs = refs[: counts[0]], refs[counts[0] :]
        second_refs, refs = refs[: counts[1]], refs[counts[1] :]
        query_out, pair_out, back_ref, first_s, second_s, sems = refs
        second[0].start(second_refs, me_ref[0], second_s, sems.at[1], second[1])
        first[0].start(first_refs, me_ref[0], first_s, sems.at[0], first[1])
        keys, values = pair_ref[0, :, :width], pair_ref[0, :, width:]
        attend = attend_ref[0]
        arrived(second_s, sems.at[1])
        blend = lowered(dot_nt(lowered(up_ref[...]), second_s[...]))
        scores = lowered(softmax_back(attend, dot_nt(blend, values)) * width ** (-0.5))
        query_out[...] = lowered(dot_nn(scores, keys))
        pair_out[:, :width] = lowered(dot_tn(scores, query_ref[...]))
        pair_out[:, width:] = lowered(dot_tn(lowered(attend), blend))
        arrived(first_s, sems.at[0])
        back = dot_nt(query_out[...], first_s[...])
        if before is not None:
            back = before_ref[...] + back
        if not last:
            back_ref[...] = back
            return
        back, gain, bias = norm_back(initial_ref[...], scale_ref, 0, back)
        for other in (up_ref, *others):
            back = back + other[...]
        gains_all = jnp.concatenate(
            [gain, bias, gains_ref[2:, :], jnp.zeros((128 - gains_ref.shape[0], width), jnp.float32)], axis=0
        )
        back_ref[:, :tokens] = lowered(back.T)
        back_ref[:, tokens:] = lowered(gains_all.T)

    back_shape = (
        shaped((width, small_columns), jnp.bfloat16) if last else shaped((tokens, width), jnp.float32)
    )
    extra = [] if before is None else [before]
    if last:
        extra += ups[:crop]
    return launch(
        kernel,
        after,
        [me, scales, initial, ups[crop], queries, attend, pairs, gains]
        + extra
        + [array for entry in parts for array in entry[0].arrays],
        [
            SMEM,
            whole((16, width)),
            whole((tokens, width)),
            whole((tokens, width)),
            whole((tokens, width)),
            pl.BlockSpec((1, tokens, spots), lambda i: (crop, 0, 0)),
            pl.BlockSpec((1, spots, 2 * width), lambda i: (crop, 0, 0)),
            whole((16, width)),
        ]
        + [whole((tokens, width))] * len(extra)
        + [ANY] * sum(counts),
        grid=(1,),
        out_specs=[whole((tokens, width)), whole((spots, 2 * width)), whole(back_shape.shape)],
        out_shape=[
            shaped((tokens, width), jnp.bfloat16),
            shaped((spots, 2 * width), jnp.bfloat16),
            back_shape,
        ],
        scratch_shapes=[
            VMEM((width, width), jnp.bfloat16),
            VMEM((width, width), jnp.bfloat16),
            pltpu.SemaphoreType.DMA((2,)),
        ],
        compiler_params=params(48),
        cost_estimate=cost(9),
        name="cross_backward",
    )


def run_last_weights(me, hidden, grad_queries, grad_pairs, pictures, small, sender, rows, apart, after=()):
    tokens, width = hidden.shape
    micro = len(grad_queries)
    channels = pictures.shape[2]
    small_columns = small.shape[1]
    kv_sender = Sender(2 * width, 2 * sender.core_rows)

    def kernel(me_ref, hidden_ref, *refs):
        query_refs, pair_refs = refs[:micro], refs[micro : 2 * micro]
        pic_ref, small_ref, keep, send = refs[2 * micro : 2 * micro + 4]
        refs = refs[2 * micro + 4 :]
        mat_s, kv_s, sems = refs[-3:]
        core = (me_ref[0] // me_ref[1]) % 2
        sender.start(small_ref, core, keep, send, width, sems.at[2])
        span = width // 2
        for number in range(2):
            cut = slice(number * span, (number + 1) * span)
            mat_s[:, cut] = lowered(
                sum(
                    dot_tn(hidden_ref[...], query_refs[crop][:, cut]) for crop in range(micro)
                )
            )
        sender.start(mat_s, core, keep, send, 0, sems.at[0])
        kv_s[...] = lowered(sum(dot_tn(pair_refs[crop][...], pic_ref[crop]) for crop in range(micro)))
        if apart:
            kv_sender.start(kv_s, core, refs[0], refs[1], 0, sems.at[1])
        else:
            for side in range(2):
                sender.start_rows(
                    kv_s, core, keep, send, width + small_columns + side * channels, rows, side, sems.at[1]
                )
        arrived(mat_s, sems.at[0])
        arrived(kv_s, sems.at[1])
        arrived(small_ref, sems.at[2])

    operands = [me, hidden, *grad_queries, *grad_pairs, pictures, small]
    if apart:
        shapes = sender.shapes(width + small_columns) + kv_sender.shapes(channels)
    else:
        shapes = sender.shapes(width + small_columns + 2 * channels)
    return launch(
        kernel,
        after,
        operands,
        [SMEM] + [whole(array.shape) for array in operands[1:]],
        grid=(1,),
        out_specs=[ANY] * len(shapes),
        out_shape=shapes,
        scratch_shapes=[
            VMEM((width, width), jnp.bfloat16),
            VMEM((2 * width, channels), jnp.bfloat16),
            pltpu.SemaphoreType.DMA((3,)),
        ],
        compiler_params=pltpu.CompilerParams(vmem_limit_bytes=BIG * MIB),
        cost_estimate=cost(6),
        name="last_weights",
    )


def run_shards(matrices, kv_weight, norm_gains, head_weight, latent_init, columns):
    rows = matrices.shape[0]
    tokens, gains = latent_init.shape[1], norm_gains.shape[1]
    channels = kv_weight.shape[1]
    wide_channels = -(-channels // 128) * 128
    classes = head_weight.shape[1]
    width = matrices.shape[1] // 10
    small = tokens + 128

    def kernel(mat_ref, kv_ref, gain_ref, head_ref, latent_ref, first_ref, *refs):
        first_ref[:, tokens:small] = jnp.zeros((rows, small - tokens), jnp.bfloat16)
        first_ref[:, :tokens] = lowered(latent_ref[...])
        first_ref[:, tokens : tokens + gains] = lowered(gain_ref[...])
        first_ref[:, small : small + 2 * width] = lowered(mat_ref[:, : 2 * width])
        first_ref[:, small + 2 * width :] = jnp.zeros((rows, 2 * wide_channels), jnp.bfloat16)
        for side in range(2):
            at = small + 2 * width + side * wide_channels
            first_ref[:, at : at + channels] = lowered(kv_ref[side * rows : (side + 1) * rows, :])
        for (begin, end), ref in zip(columns, refs):
            ref[:, : (end - begin) * width] = lowered(mat_ref[:, begin * width : end * width])
        at = refs[-1].shape[1] - width
        refs[-1][:, at:] = jnp.zeros((rows, width), jnp.bfloat16)
        refs[-1][:, at : at + classes] = lowered(head_ref[...])

    widths = [small + 2 * width + 2 * wide_channels] + [(end - begin) * width for begin, end in columns]
    widths[-1] += width
    return pl.pallas_call(
        kernel,
        grid=(1,),
        in_specs=[
            whole(array.shape)
            for array in (matrices, kv_weight, norm_gains, head_weight, latent_init)
        ],
        out_specs=[whole((rows, number)) for number in widths],
        out_shape=[shaped((rows, number), jnp.bfloat16) for number in widths],
        compiler_params=pltpu.CompilerParams(vmem_limit_bytes=62 * MIB),
        cost_estimate=cost(3),
        name="shards",
    )(matrices, kv_weight, norm_gains, head_weight, latent_init)


def run_join(targets, passing, after):
    moves = [move for _, parts in targets for move in parts]
    sources = []
    for array, _, _ in moves:
        if not any(array is known for known in sources):
            sources.append(array)
    where = {id(array): number for number, array in enumerate(sources)}
    count, kept = len(sources), len(passing)

    def kernel(*refs):
        outs = refs[count + kept : count + kept + len(targets)]
        for target, (_, parts) in zip(outs, targets):
            for array, cut, first in parts:
                source = refs[where[id(array)]]
                if cut is None:
                    target[first : first + source.shape[0]] = source[...]
                else:
                    target[first] = source[:, cut]

    vmem = pl.BlockSpec(memory_space=pltpu.VMEM)
    outs = launch(
        kernel,
        after,
        sources + list(passing),
        [vmem] * count + [ANY] * kept,
        out_specs=[vmem] * len(targets) + [ANY] * kept,
        out_shape=[shaped(shape, jnp.bfloat16) for shape, _ in targets]
        + [shaped(array.shape, array.dtype) for array in passing],
        input_output_aliases={count + number: len(targets) + number for number in range(kept)},
        compiler_params=pltpu.CompilerParams(vmem_limit_bytes=16 * MIB),
        cost_estimate=cost(3),
        name="join",
    )
    return outs[: len(targets)], outs[len(targets) :]


def run_fold(me, parts, after):
    depth = 4
    operands = []
    in_specs = []
    out_specs = []
    out_shape = []
    for terms, first, last, axis in parts:
        groups, rows, _ = terms[0].shape
        each = groups // depth
        for term in terms:
            if not any(term is known for known in operands):
                operands.append(term)
                in_specs.append(
                    pl.BlockSpec((each, rows, term.shape[2]), lambda z: (z, 0, 0))
                )
        block = (each, rows // 2, last - first) if axis == "x" else (1, rows, last - first)
        for _ in range(2):
            out_specs.append(pl.BlockSpec(block, lambda z: (z, 0, 0)))
            out_shape.append(shaped((block[0] * depth,) + block[1:], jnp.bfloat16))
    where = {id(term): number for number, term in enumerate(operands)}

    def kernel(me_ref, *refs):
        out = len(operands)
        mine = {"x": me_ref[0] % 2, "y": (me_ref[0] // 4) % 2}
        for terms, first, last, axis in parts:
            sources = [refs[where[id(term)]] for term in terms]
            for side in range(2):
                spot = mine[axis] if side == 0 else 1 - mine[axis]
                if axis == "x":
                    rows = sources[0].shape[1] // 2
                    cut = (slice(None), pl.ds(pl.multiple_of(spot * rows, rows), rows), slice(first, last))
                else:
                    cut = (pl.ds(spot, 1), slice(None), slice(first, last))
                refs[out][...] = lowered(sum(source[cut].astype(jnp.float32) for source in sources))
                out += 1

    outs = launch(
        kernel,
        after,
        [me] + operands,
        [SMEM] + in_specs,
        grid=(depth,),
        out_specs=out_specs,
        out_shape=out_shape,
        compiler_params=params(32),
        cost_estimate=cost(4),
        name="fold",
    )
    return [(outs[2 * number], outs[2 * number + 1]) for number in range(len(parts))]


def run_fold_z(me, parts, after):
    depth = 4
    columns = [terms[0].shape[2] for terms in parts]

    def kernel(me_ref, *refs):
        mine = me_ref[0] // 8
        outs = refs[-depth:]
        at = 0
        column = 0
        for terms, number in zip(parts, columns):
            sources = refs[at : at + len(terms)]
            at += len(terms)
            for k in range(depth):
                outs[k][:, column : column + number] = lowered(
                    sum(source[pl.ds(mine ^ k, 1)].astype(jnp.float32) for source in sources)
                )[0]
            column += number

    vmem = pl.BlockSpec(memory_space=pltpu.VMEM)
    operands = [me] + [term for terms in parts for term in terms]
    shape = shaped((parts[0][0].shape[1], sum(columns)), jnp.bfloat16)
    return launch(
        kernel,
        after,
        operands,
        [SMEM] + [vmem] * (len(operands) - 1),
        out_specs=[vmem] * depth,
        out_shape=[shape] * depth,
        compiler_params=pltpu.CompilerParams(vmem_limit_bytes=24 * MIB),
        cost_estimate=cost(3),
        name="fold_z",
    )


def run_totals(states, grad_head, channels, tokens, gains):
    rows = grad_head.shape[0]
    flat = [term for terms in states for term in terms]
    widths = [terms[0].shape[1] for terms in states]
    small = tokens + 128
    width = widths[1] // 3
    wide_channels = (widths[0] - width - small) // 2
    blocks = width + sum(widths[1:])

    def kernel(head_ref, *refs):
        mat_ref, kv_ref, gain_ref, latent_ref, square_ref = refs[len(flat) :]
        at = 0
        column = width
        square = jnp.sum(head_ref[...] * head_ref[...], axis=0, keepdims=True)
        square = jnp.sum(square, axis=1, keepdims=True)
        for number, (terms, span) in enumerate(zip(states, widths)):
            total = sum(ref[...].astype(jnp.float32) for ref in refs[at : at + len(terms)])
            at += len(terms)
            part = jnp.sum(total * total, axis=0, keepdims=True)
            square = square + jnp.sum(part, axis=1, keepdims=True)
            if number > 0:
                mat_ref[:, column : column + span] = total
                column += span
                continue
            mat_ref[:, :width] = total[:, :width]
            latent_ref[...] = total[:, width : width + tokens]
            gain_ref[...] = total[:, width + tokens : width + tokens + gains]
            for side in range(2):
                first = width + small + side * wide_channels
                kv_ref[side * rows : (side + 1) * rows, :] = total[:, first : first + channels]
        square_ref[...] = jnp.broadcast_to(square, square_ref.shape)

    shapes = [
            shaped((rows, blocks), jnp.float32),
            shaped((2 * rows, channels), jnp.float32),
            shaped((rows, gains), jnp.float32),
            shaped((rows, tokens), jnp.float32),
            shaped((1, 128), jnp.float32),
    ]
    return pl.pallas_call(
        kernel,
        grid=(1,),
        in_specs=[whole(array.shape) for array in [grad_head] + flat],
        out_specs=[whole(shape.shape) for shape in shapes],
        out_shape=shapes,
        compiler_params=pltpu.CompilerParams(vmem_limit_bytes=32 * MIB),
        cost_estimate=cost(3),
        name="totals",
    )(grad_head, *flat)


def run_update(squares, step_count, shares, masters, firsts, seconds):
    count = len(shares)
    given = [master for master in masters if master is not None]

    def kernel(step_ref, square_ref, *refs):
        share_refs, refs = refs[:count], refs[count:]
        master_refs, refs = list(refs[: len(given)]), refs[len(given) :]
        first_refs, second_refs, outs = refs[:count], refs[count : 2 * count], refs[2 * count :]
        norm = jnp.sqrt(jnp.sum(square_ref[...], axis=0, keepdims=True))
        outs[0][...] = norm
        factor = jnp.minimum(1.0, THRESH / norm[:, 0:1])
        steps = jnp.zeros((1, 1), jnp.float32) + step_ref[0].astype(jnp.float32)
        scale = 1.0 / (1.0 - jnp.exp2(-steps))
        for number in range(count):
            clipped = share_refs[number][...] * factor
            moment_one = 0.5 * first_refs[number][...] + 0.5 * clipped
            moment_two = 0.5 * second_refs[number][...] + 0.5 * clipped * clipped
            outs[1 + 3 * number][...] = moment_one
            outs[2 + 3 * number][...] = moment_two
            if masters[number] is None:
                outs[3 + 3 * number][...] = clipped
                continue
            master = master_refs.pop(0)[...]
            outs[3 + 3 * number][...] = master - RATE * (
                moment_one * scale / (jnp.sqrt(moment_two * scale) + TINY) + DECAY * master
            )

    shapes = [shaped((1, 128), jnp.float32)]
    shapes += [shaped(share.shape, jnp.float32) for share in shares for _ in range(3)]
    operands = [step_count, squares, *shares, *given, *firsts, *seconds]
    return pl.pallas_call(
        kernel,
        grid=(1,),
        in_specs=[SMEM] + [whole(array.shape) for array in operands[1:]],
        out_specs=[whole(shape.shape) for shape in shapes],
        out_shape=shapes,
        compiler_params=pltpu.CompilerParams(vmem_limit_bytes=62 * MIB),
        cost_estimate=cost(5),
        name="update",
    )(*operands)


def digits():
    n_wide = lax.axis_size("wide")
    n_narrow = lax.axis_size("narrow")
    rest = n_wide // 2
    top = min(4, rest)
    return (
        ("z", n_narrow * n_wide // top, top),
        ("y", 2 * n_narrow, rest // top),
        ("c", n_narrow, 2),
        ("x", 1, n_narrow),
    )


def device_index():
    return lax.axis_index("wide") * lax.axis_size("narrow") + lax.axis_index("narrow")


def exchange(values, offset):
    total = lax.axis_size(AXES)
    return lax.ppermute(values, AXES, [(i, i ^ offset) for i in range(total)])


class Gather:
    def __init__(self, shard, first, left, right, plain):
        self.shard = shard
        self.first = first
        self.widths = (left, right)
        self.rows = shard.shape[0]
        self.table = {name: (stride, size) for name, stride, size in digits()}
        self.names = (("y", "x"), ("x", "y"))
        self.plain = plain

    def send_z(self):
        stride, size = self.table["z"]
        self.got = [exchange(self.shard, k * stride) for k in range(1, size)]
        return self.got

    def join(self, targets, passing, after):
        if self.plain:
            flats = []
            for _, parts in targets:
                flats.append(
                    jnp.concatenate(
                        [
                            array if array.ndim == 3 else array[None, :, cut]
                            for array, cut, _ in parts
                        ]
                    )
                )
            return flats, passing
        return run_join(targets, passing, after)

    def join_z(self, passing=(), after=()):
        stride, size = self.table["z"]
        pieces = [self.shard] + self.got
        targets = []
        at = self.first
        for width in self.widths:
            parts = [(piece, slice(at, at + width), k) for k, piece in enumerate(pieces)]
            targets.append(((size, self.rows, width), parts))
            at += width
        self.flats, passing = self.join(targets, passing, after)
        self.offsets = [[k * stride for k in range(size)]] * 2
        return passing

    def send(self, turn):
        self.got = []
        for half in range(2):
            stride, size = self.table[self.names[half][turn]]
            self.got.append([exchange(self.flats[half], k * stride) for k in range(1, size)])
        return self.got[0] + self.got[1]

    def pieces(self, turn):
        halves = []
        for half in range(2):
            stride, size = self.table[self.names[half][turn]]
            arrays = [self.flats[half]] + self.got[half]
            halves.append(
                (arrays, [[offset ^ (k * stride) for offset in self.offsets[half]] for k in range(size)])
            )
        return halves

    def join_first(self, passing=(), after=()):
        targets = []
        offsets = []
        for arrays, groups in self.pieces(0):
            count = arrays[0].shape[0]
            parts = [(array, None, k * count) for k, array in enumerate(arrays)]
            targets.append(((count * len(arrays),) + arrays[0].shape[1:], parts))
            offsets.append([offset for group in groups for offset in group])
        self.flats, passing = self.join(targets, passing, after)
        self.offsets = offsets
        return passing

    def held(self):
        return list(self.flats) + self.got[0] + self.got[1]

    def release(self, arrays):
        self.flats = arrays[:2]
        count = len(self.got[0])
        self.got = [list(arrays[2 : 2 + count]), list(arrays[2 + count :])]

    def send_across(self):
        stride = self.table["c"][0]
        self.state = []
        fresh = []
        for arrays, offsets in self.pieces(1):
            sent = [exchange(array, stride) for array in arrays]
            fresh += sent
            self.state.append(
                (
                    arrays + sent,
                    offsets + [[offset ^ stride for offset in group] for group in offsets],
                )
            )
        return fresh

    def done(self):
        halves = []
        me = device_index()
        total = lax.axis_size(AXES)
        for arrays, offsets in self.state:
            if not self.plain:
                halves.append(Half(arrays, offsets, self.rows))
            else:
                flat = jnp.concatenate(arrays)
                spots = jnp.argsort(jnp.array([o for group in offsets for o in group]) ^ me)
                flat = jnp.take(flat, spots, axis=0).reshape(1, total * self.rows, -1)
                halves.append(Half([flat], None, total * self.rows))
        return halves


class Scatter:
    def __init__(self, me, keep, send, cut, plain, extra=None):
        self.me = me
        self.keep = keep
        self.columns = keep.shape[2]
        self.cut = cut
        self.plain = plain
        self.table = {name: (stride, size) for name, stride, size in digits()}
        self.pairs = [(keep, send)] + ([extra] if extra is not None else [])
        self.names = (("x", "y"), ("y", "x"), ("y", "x"))
        self.last = keep

    def send_across(self):
        stride = self.table["c"][0]
        fresh = [exchange(send, stride) for _, send in self.pairs]
        if not self.plain:
            terms = [self.keep, fresh[0]]
            self.state = [(terms, 0, self.cut), (terms, self.cut, self.columns)]
            return fresh
        sizes = tuple(self.table[name][1] for name in ("z", "y", "x"))
        self.state = []
        for number, ((keep, _), received) in enumerate(zip(self.pairs, fresh)):
            rows = keep.shape[0] * keep.shape[1] // (sizes[0] * sizes[1] * sizes[2])
            terms = [term.reshape(sizes + (rows, keep.shape[2])) for term in (keep, received)]
            if number == 0:
                self.state.append((["z", "y", "x"], [term[..., : self.cut] for term in terms]))
                self.state.append((["z", "y", "x"], [term[..., self.cut :] for term in terms]))
            else:
                self.state.append((["z", "y", "x"], terms))
        return fresh

    def send(self, turn, after=()):
        fresh = []
        if not self.plain:
            if turn == 2:
                kept, *sends = run_fold_z(self.me, [terms for terms, _, _ in self.state], after)
                stride = self.table["z"][0]
                fresh = [exchange(send, (k + 1) * stride) for k, send in enumerate(sends)]
                self.state = [kept] + fresh
                self.last = kept
                return fresh
            names = [ways[turn] for ways in self.names]
            pairs = run_fold(
                self.me, [entry + (name,) for entry, name in zip(self.state, names)], after
            )
            self.state = []
            for (kept, send), name in zip(pairs, names):
                received = exchange(send, self.table[name][0])
                fresh.append(received)
                self.state.append(([kept, received], 0, kept.shape[2]))
            self.last = pairs[0][0]
            return fresh
        me = device_index()
        for number, (left, terms) in enumerate(self.state):
            name = (self.names[number] + ("z",))[turn]
            stride, size = self.table[name]
            mine = (me // stride) % size
            axis = left.index(name)

            def part(index):
                return lowered(
                    sum(
                        lax.dynamic_index_in_dim(term, index, axis, keepdims=False).astype(jnp.float32)
                        for term in terms
                    )
                )

            kept = part(mine)
            sent = [exchange(part(mine ^ k), k * stride) for k in range(1, size)]
            fresh += sent
            self.state[number] = ([entry for entry in left if entry != name], [kept] + sent)
            self.last = kept
        return fresh

    def done(self):
        if not self.plain:
            return sum(term.astype(jnp.float32) for term in self.state)
        sums = [sum(term.astype(jnp.float32) for term in terms) for _, terms in self.state]
        rows = sums[0].shape[0]
        if len(sums) > 2:
            sums[2:] = [sums[2][:rows], sums[2][rows:]]
        return jnp.concatenate(sums, axis=1)


def share(values):
    total = lax.axis_size(AXES)
    spread = jnp.broadcast_to(values[None], (total,) + values.shape)
    return lax.all_to_all(spread, AXES, 0, 0, tiled=True)


def on_device(
    pixels,
    labels,
    partner,
    pair_on,
    step_count,
    matrices,
    kv_weight,
    norm_gains,
    head_weight,
    latent_init,
    matrices_first,
    kv_first,
    gains_first,
    head_first,
    latent_first,
    matrices_second,
    kv_second,
    gains_second,
    head_second,
    latent_second,
):
    axis_count = lax.axis_size(AXES)
    n_narrow = lax.axis_size("narrow")
    index = device_index()
    me = jnp.stack([index, jnp.int32(n_narrow)]).astype(jnp.int32)
    micro = pixels.shape[0]
    tokens = latent_init.shape[1]
    width = matrices.shape[1] // 10
    rows = matrices.shape[0]
    channels = pixels.shape[3]
    wide_channels = -(-channels // 128) * 128
    classes = head_weight.shape[1]

    half = width // 2
    wide_half = width + half
    small_columns = tokens + 128
    plain = rows % 16 != 0 or tuple(size for _, _, size in digits()) != (4, 2, 2, 2)
    pictures = jnp.pad(pixels[:, 0], ((0, 0), (0, 0), (0, wide_channels - channels)))
    blocks = ((2, 4), (4, 7), (7, 10))
    shards = run_shards(matrices, kv_weight, norm_gains, head_weight, latent_init, blocks)
    chunks = [
        Gather(shards[0], 0, small_columns + width, width + 2 * wide_channels, plain),
        Gather(shards[1], 0, width, width, plain),
        Gather(shards[2], 0, wide_half, wide_half, plain),
        Gather(shards[3], 0, 2 * width, 2 * width, plain),
    ]

    def block(halves, column, last=width):
        left = halves[0].arrays[0].shape[2]
        if column >= left:
            return [(halves[1], column - left, 0, last)]
        if column + last <= left:
            return [(halves[0], column, 0, last)]
        return [(halves[0], column, 0, left - column), (halves[1], 0, left - column, last)]

    first, second, third, fourth = chunks
    first.send_z()
    second.send_z()
    first.join_z()
    first.send(0)
    first.join_first()
    first.send(1)
    (third.shard,) = second.join_z([third.shard], after=first.flats)
    second.send(0)
    third.send_z()
    first.send_across()
    second.join_first()
    second.send(1)
    halves = first.done()
    weights = {0: (halves[0], small_columns), 1: (halves[1], 0)}
    small_half, kv_half = (halves[0], 0), (halves[1], width)
    if kv_half[0].offsets is None:
        array = kv_half[0].arrays[0][..., width:].reshape(axis_count, rows, 2, wide_channels)
        array = array.transpose(0, 2, 1, 3).reshape(1, 2 * width, wide_channels)
        kv_half = (Half([array], None, 2 * width), 0)
    latent_one, blended, attend, pairs, initial, hidden_zero, queries, scales = run_cross_forward(
        me, pictures, small_half, kv_half, weights[0], weights[1], width, tokens,
        after=second.flats,
    )
    *held, fourth.shard = third.join_z(second.held() + [fourth.shard], after=[latent_one])
    second.release(held)
    second.send_across()
    third.send(0)
    fourth.send_z()
    third.join_first(after=third.flats)
    third.send(1)
    for number in range(2):
        weights[2 + number] = (second.done()[number], 0)
    latent_two, hidden_one, active_one, steep_one = run_feed_forward(
        me, scales, latent_one, weights[2], weights[3], 2, micro, False,
        after=third.flats,
    )
    third.release(fourth.join_z(third.held(), after=[latent_two]))
    third.send_across()
    fourth.send(0)
    fourth.join_first()
    fourth.send(1)
    halves = third.done()
    for number in range(3):
        weights[4 + number] = (Joint(block(halves, number * width)), 0)
    hidden_two, packed, attend_self, blended_self = [], [], [], []
    for crop in range(micro):
        outs = run_self_forward(
            crop, me, scales, latent_two, weights[4], weights[5], weights[6], micro,
            after=fourth.flats if crop == 0 else fourth.flats,
        )
        for entries, out in zip((hidden_two, packed, attend_self, blended_self), outs):
            entries.append(out)
        if crop == 0:
            fourth.release(fourth.join([], fourth.held(), [blended_self[0]])[1])
            fourth.send_across()
    halves = fourth.done()
    weights[7], weights[8], weights[9] = (halves[0], 0), (halves[0], width), (halves[1], 0)
    result, hidden_three, active_three, steep_three, pooled, latent_three = run_feed_forward(
        me, scales, latent_two, weights[8], weights[9], 6, micro, True, (blended_self, weights[7])
    )
    marks = jnp.stack(
        [labels[:, 0] // 256, labels[:, 0] % 256, partner[:, 0] // 256, partner[:, 0] % 256, pair_on[:, 0]],
        axis=1,
    )
    marks = jnp.pad(lowered(marks), ((0, 0), (0, MARKS - marks.shape[1])))
    pooled_all = share(jnp.concatenate([pooled.reshape(micro, width), marks], axis=1))
    pooled_all = pooled_all.reshape(axis_count * micro, width + MARKS)
    loss_tile, grad_logits, grad_pooled = run_losses(
        me, pooled_all, [(halves[1], width), (halves[1], width + half)], classes, axis_count, micro
    )
    total_loss = loss_tile[0, 0]
    counts = loss_tile[1 : 1 + micro, 0].astype(jnp.int32)
    pooled_rows = lax.dynamic_slice_in_dim(pooled_all, index * rows, rows, axis=1)
    grad_head = dot_tn(pooled_rows, grad_logits)[:, :classes]

    sender = Sender(width, n_narrow * rows)
    total_tokens = micro * tokens

    def single(left, right):
        return [(left, 0, total_tokens)], [(right, 0, 0)]

    upstream, gain_high, low, before, behind = run_feed_backward(
        me, scales, latent_three, (result, grad_pooled), steep_three, weights[8], weights[9], 6, micro, True
    )
    keep, send = run_weights(
        me,
        [
            (
                [(rows_of, 0, tokens) for rows_of in blended_self],
                [(behind, crop * tokens, 0) for crop in range(micro)],
            ),
            single(hidden_three, before),
            single(active_three, low),
        ],
        sender,
    )
    one = Scatter(me, keep, send, wide_half, plain)
    one.send_across()
    grads = []
    gain_mid = 0.0
    onward = None
    for crop in range(micro):
        waits = ()
        if crop == 1:
            one.send(0, after=[onward])
            waits = [one.last]
        grad_packed, onward, gain = run_self_backward(
            crop, me, scales, latent_two, upstream, (packed[crop], attend_self[crop]),
            weights[4], weights[5], weights[6], weights[7], micro, onward, after=waits,
        )
        grads.append(grad_packed)
        gain_mid = gain_mid + gain
    upstream = onward
    one.send(1, after=[onward])
    keep, send = run_weights(
        me,
        [
            (
                [(hidden_two[crop], 0, tokens) for crop in range(micro)],
                [(grads[crop], 0, number * width) for crop in range(micro)],
            )
            for number in range(3)
        ],
        sender,
        after=[one.last],
    )
    two = Scatter(me, keep, send, wide_half, plain)
    two.send_across()
    ups, lows, befores, behinds = [], [], [], []
    gain_low = 0.0
    for crop in range(micro):
        outs = run_feed_backward(
            me, scales, latent_one, upstream, steep_one, weights[2], weights[3], 2, micro, False, crop,
            after=[keep] if crop == 0 else [two.last, one.last],
        )
        gain_low = gain_low + outs[1]
        for entries, out in zip((ups, lows, befores, behinds), (outs[0],) + tuple(outs[2:])):
            entries.append(out)
        if crop == 0:
            arriving = two.send(0, after=[outs[0]])
            one_z = one.send(2, after=[two.last])
    keep, send = run_weights(
        me,
        [
            (
                [(left, crop * tokens, tokens) for crop in range(micro)],
                [(rights[crop], 0, 0) for crop in range(micro)],
            )
            for left, rights in ((blended, behinds), (hidden_one, befores), (active_one, lows))
        ],
        sender,
        after=ups[-1:] + arriving,
    )
    three = Scatter(me, keep, send, wide_half, plain)
    three.send_across()
    two.send(1, after=[keep])
    gains = jnp.concatenate(
        [
            jnp.zeros((2, width), jnp.float32),
            gain_low[:2],
            gain_mid[:2],
            gain_high[:4],
            jnp.zeros((6, width), jnp.float32),
        ]
    )
    grad_queries, grad_pairs = [], []
    back = None
    for crop in range(micro):
        outs = run_cross_backward(
            crop, me, scales, initial, ups, (queries, attend, pairs), gains,
            weights[0], weights[1], micro, back, after=[two.last],
        )
        grad_queries.append(outs[0])
        grad_pairs.append(outs[1])
        back = outs[2]
        if crop == 0:
            arriving = three.send(0, after=[back] + one_z)
            two_z = two.send(2, after=[three.last])
    grad_small = back
    keep, send, *extra = run_last_weights(
        me, hidden_zero, grad_queries, grad_pairs, pictures, grad_small,
        sender, rows, plain, after=arriving,
    )
    four = Scatter(me, keep, send, width, plain, extra or None)
    four.send_across()
    arriving = three.send(1, after=[keep])
    four.send(0, after=arriving + two_z)
    arriving = three.send(2, after=[four.last])
    four.send(1, after=arriving)
    four.send(2)
    if plain:
        last = four.done()
        grad_matrices = jnp.concatenate(
            [last[:, :width], three.done(), two.done(), one.done()], axis=1
        )
        grad_kv = last[:, width + small_columns :]
        grad_kv = jnp.concatenate(
            [grad_kv[:, :channels], grad_kv[:, wide_channels : wide_channels + channels]]
        )
        grad_small = last[:, width : width + small_columns]
        grad_gains, grad_latent = grad_small[:, tokens : tokens + 10], grad_small[:, :tokens]
        shares = (grad_matrices, grad_kv, grad_gains, grad_head, grad_latent)
        square = sum(jnp.sum(member * member) for member in shares)
        square = jnp.broadcast_to(square, (1, 128))
    else:
        grad_matrices, grad_kv, grad_gains, grad_latent, square = run_totals(
            [four.state, three.state, two.state, one.state],
            grad_head,
            channels,
            tokens,
            norm_gains.shape[1],
        )
    shares = (grad_matrices, grad_kv, grad_gains, grad_head, grad_latent)
    norm, *results = run_update(
        share(square[0]),
        step_count,
        shares,
        (matrices, kv_weight, None, head_weight, None),
        (matrices_first, kv_first, gains_first, head_first, latent_first),
        (matrices_second, kv_second, gains_second, head_second, latent_second),
    )
    return (total_loss, norm[0, 0], counts, *results)


def solution(mesh):
    in_specs = (
        P(None, ("wide", "narrow"), None, None),
        P(None, ("wide", "narrow")),
        P(None, ("wide", "narrow")),
        P(None, ("wide", "narrow")),
        P(),
        P(("wide", "narrow"), None),
        P(("wide", "narrow"), None),
        P(("wide", "narrow"), None),
        P(("wide", "narrow"), None),
        P(("wide", "narrow"), None),
        P(("wide", "narrow"), None),
        P(("wide", "narrow"), None),
        P(("wide", "narrow"), None),
        P(("wide", "narrow"), None),
        P(("wide", "narrow"), None),
        P(("wide", "narrow"), None),
        P(("wide", "narrow"), None),
        P(("wide", "narrow"), None),
        P(("wide", "narrow"), None),
        P(("wide", "narrow"), None),
    )
    out_specs = (
        P(),
        P(),
        P(),
        P(("wide", "narrow"), None),
        P(("wide", "narrow"), None),
        P(("wide", "narrow"), None),
        P(("wide", "narrow"), None),
        P(("wide", "narrow"), None),
        P(("wide", "narrow"), None),
        P(("wide", "narrow"), None),
        P(("wide", "narrow"), None),
        P(("wide", "narrow"), None),
        P(("wide", "narrow"), None),
        P(("wide", "narrow"), None),
        P(("wide", "narrow"), None),
        P(("wide", "narrow"), None),
        P(("wide", "narrow"), None),
        P(("wide", "narrow"), None),
    )
    return jax.shard_map(
        on_device, mesh=mesh, in_specs=in_specs, out_specs=out_specs, check_vma=False
    )
```

```python
import functools

import jax
import jax.numpy as jnp
from jax import lax
from jax.experimental import pallas as pl
from jax.experimental.pallas import tpu as pltpu
from jax.sharding import PartitionSpec as P

HEADS = 8
GROUP = 4
BACK_GROUP = 2
STEPS = 2
FORWARD_STEPS = 1
AXES = ("wide", "narrow")

EPSILON = 1e-05
RATE = 0.03
DECAY = 0.1
TINY = 1e-08
THRESH = 0.01
BEND = 0.044715
MARKS = 128
SLOPE = 0.7978845608028654
VMEM = pltpu.VMEM
MIB = 1 << 20
BIG = 48
PACE = 0.5


def lowered(values):
    return values.astype(jnp.bfloat16)


def dot_nn(first_op, second_op):
    return jnp.dot(first_op, second_op, preferred_element_type=jnp.float32)


def dot_tn(first_op, second_op):
    return lax.dot_general(
        first_op, second_op, (((0,), (0,)), ((), ())), preferred_element_type=jnp.float32
    )


def dot_nt(first_op, second_op):
    return lax.dot_general(
        first_op, second_op, (((1,), (1,)), ((), ())), preferred_element_type=jnp.float32
    )


def standard(inputs):
    center = inputs - jnp.mean(inputs, axis=-1, keepdims=True)
    scale = lax.rsqrt(jnp.mean(center * center, axis=-1, keepdims=True) + EPSILON)
    return center * scale, scale


def layer_norm(inputs, scales, column):
    return standard(inputs)[0] * scales[column : column + 1, :] + scales[column + 1 : column + 2, :]


def norm_back(inputs, scales, column, upstream):
    unit, scale = standard(inputs)
    gain = jnp.sum(upstream * unit, axis=0, keepdims=True)
    bias = jnp.sum(upstream, axis=0, keepdims=True)
    inner = upstream * scales[column : column + 1, :]
    back = scale * (
        inner
        - jnp.mean(inner, axis=-1, keepdims=True)
        - unit * jnp.mean(inner * unit, axis=-1, keepdims=True)
    )
    return back, gain, bias


def gelu_both(values):
    square = values * values
    bent = jnp.tanh(SLOPE * values * (1.0 + BEND * square))
    half = 0.5 * (1.0 + bent)
    steep = half + 0.5 * values * (1.0 - bent * bent) * SLOPE * (1.0 + 3.0 * BEND * square)
    return values * half, steep


def softmax(scores):
    raised = jnp.exp(scores - jnp.max(scores, axis=-1, keepdims=True))
    return raised * (1.0 / jnp.sum(raised, axis=-1, keepdims=True))


def softmax_back(attend, upstream):
    return attend * (upstream - jnp.sum(upstream * attend, axis=-1, keepdims=True))


class Half:
    def __init__(self, arrays, offsets, rows):
        self.arrays = arrays
        self.offsets = offsets
        self.rows = rows

    def start(self, refs, me, target, sem, column, stride=None, shift=0):
        width = target.shape[1]
        if self.offsets is None:
            pltpu.make_async_copy(refs[0].at[0, :, column : column + width], target, sem).start()
            return
        stride = self.rows if stride is None else stride
        for ref, offsets in zip(refs, self.offsets):
            for group, offset in enumerate(offsets):
                spot = pl.multiple_of((me ^ offset) * stride + shift, self.rows)
                pltpu.make_async_copy(
                    ref.at[group, :, column : column + width],
                    target.at[pl.ds(spot, self.rows), :],
                    sem,
                ).start()


class Joint:
    def __init__(self, pieces):
        self.pieces = pieces
        self.arrays = [array for half, *_ in pieces for array in half.arrays]

    def start(self, refs, me, target, sem, column):
        at = 0
        for half, spot, first, last in self.pieces:
            count = len(half.arrays)
            half.start(refs[at : at + count], me, target.at[:, first:last], sem, spot)
            at += count


def arrived(target, sem):
    pltpu.make_async_copy(target, target, sem).wait()


def cost(micros):
    return pl.CostEstimate(flops=int(micros * PACE * 1.1e9), bytes_accessed=1 << 10, transcendentals=0)


def params(mib, dims=1, big=None):
    return pltpu.CompilerParams(
        vmem_limit_bytes=(big or max(mib, BIG)) * MIB, dimension_semantics=("arbitrary",) * dims
    )


def launch(kernel, after, operands, in_specs, **rest):
    extra = len(after)

    def inner(*refs):
        kernel(*refs[: len(operands)], *refs[len(operands) + extra :])

    return pl.pallas_call(inner, in_specs=list(in_specs) + [ANY] * extra, **rest)(*operands, *after)


ANY = pl.BlockSpec(memory_space=pl.ANY)
SMEM = pl.BlockSpec(memory_space=pltpu.SMEM)


def whole(shape):
    return pl.BlockSpec(shape, lambda *ids: (0,) * len(shape))


def by_crop(shape, rank=1):
    return pl.BlockSpec(shape, lambda m, *ids: (m,) + (0,) * (len(shape) - 1))


def shaped(shape, dtype):
    return jax.ShapeDtypeStruct(shape, dtype)


def run_cross_forward(me, pictures, small, kv, first, second, width, tokens, after=()):
    micro, spots, channels = pictures.shape
    parts = (small, kv, first, second)
    counts = [len(part[0].arrays) for part in parts]
    small_columns = tokens + 128

    def kernel(me_ref, pic_ref, *refs):
        groups = []
        at = 0
        for count in counts:
            groups.append(refs[at : at + count])
            at += count
        latent_ref, blended_ref, attend_ref, pair_ref, initial_ref, hidden_ref, query_ref, scale_ref = refs[at : at + 8]
        small_s, kv_s, first_s, second_s, sems = refs[at + 8 :]
        me_now = me_ref[0]
        step = pl.program_id(0)

        @pl.when(step == 0)
        def _():
            small[0].start(groups[0], me_now, small_s, sems.at[0], small[1])
            if kv[0].offsets is None:
                kv[0].start(groups[1], me_now, kv_s, sems.at[1], 0)
            else:
                rows = kv[0].rows
                kv[0].start(groups[1], me_now, kv_s, sems.at[1], kv[1], 2 * rows, 0)
                kv[0].start(groups[1], me_now, kv_s, sems.at[1], kv[1] + channels, 2 * rows, rows)
            first[0].start(groups[2], me_now, first_s, sems.at[2], first[1])
            second[0].start(groups[3], me_now, second_s, sems.at[3], second[1])
            arrived(small_s, sems.at[0])
            turned = small_s[...].astype(jnp.float32).T
            initial_ref[...] = turned[:tokens]
            scale_ref[...] = turned[tokens : tokens + 16]
            hidden_ref[...] = lowered(layer_norm(initial_ref[...], scale_ref, 0))
            arrived(first_s, sems.at[2])
            query_ref[...] = lowered(dot_nn(hidden_ref[...], first_s[...]))
            arrived(kv_s, sems.at[1])
            arrived(second_s, sems.at[3])

        pair_ref[0] = lowered(dot_nt(pic_ref[0], kv_s[...]))
        scores = dot_nt(query_ref[...], pair_ref[0, :, :width]) * width ** (-0.5)
        attend = softmax(scores)
        attend_ref[0] = attend
        blended_ref[...] = lowered(dot_nn(lowered(attend), pair_ref[0, :, width:]))
        latent_ref[...] = initial_ref[...] + dot_nn(blended_ref[...], second_s[...])

    total = micro * tokens
    return launch(
        kernel,
        after,
        [me, pictures, *[array for part in parts for array in part[0].arrays]],
        grid=(micro,),
        in_specs=[SMEM, by_crop((1, spots, channels))] + [ANY] * sum(counts),
        out_specs=[
            by_crop((tokens, width)),
            by_crop((tokens, width)),
            by_crop((1, tokens, spots)),
            by_crop((1, spots, 2 * width)),
            whole((tokens, width)),
            whole((tokens, width)),
            whole((tokens, width)),
            whole((16, width)),
        ],
        out_shape=[
            shaped((total, width), jnp.float32),
            shaped((total, width), jnp.bfloat16),
            shaped((micro, tokens, spots), jnp.float32),
            shaped((micro, spots, 2 * width), jnp.bfloat16),
            shaped((tokens, width), jnp.float32),
            shaped((tokens, width), jnp.bfloat16),
            shaped((tokens, width), jnp.bfloat16),
            shaped((16, width), jnp.float32),
        ],
        scratch_shapes=[
            VMEM((width, small_columns), jnp.bfloat16),
            VMEM((2 * width, channels), jnp.bfloat16),
            VMEM((width, width), jnp.bfloat16),
            VMEM((width, width), jnp.bfloat16),
            pltpu.SemaphoreType.DMA((4,)),
        ],
        compiler_params=params(48),
        cost_estimate=cost(18),
        name="cross_forward",
    )


def run_feed_forward(me, scales, latent, first, second, column, micro, pool, prior=None, after=()):
    total, width = latent.shape
    tokens = total // micro
    rows = tokens // FORWARD_STEPS
    parts = [first, second] + ([prior[1]] if prior else [])
    counts = [len(part[0].arrays) for part in parts]

    def kernel(me_ref, scale_ref, latent_ref, *refs):
        if prior:
            prior_refs, refs = refs[:micro], refs[micro:]
        groups = []
        at = 0
        for count in counts:
            groups.append(refs[at : at + count])
            at += count
        out_ref, hidden_ref, active_ref, steep_ref = refs[at : at + 4]
        more = refs[at + 4 : -2 - len(parts)]
        blocks, pool_s, sems = refs[-2 - len(parts) : -2], refs[-2], refs[-1]
        first_s, second_s = blocks[:2]
        step = pl.program_id(0)

        @pl.when(step == 0)
        def _():
            for number in range(len(parts) - 1, -1, -1) if prior else range(len(parts)):
                parts[number][0].start(
                    groups[number], me_ref[0], blocks[number], sems.at[number], parts[number][1]
                )

        source_ref = latent_ref
        if prior:
            source_ref = more[-1]

            @pl.when(step == 0)
            def _():
                arrived(blocks[2], sems.at[2])

            for number in range(micro * FORWARD_STEPS):

                @pl.when(step == number)
                def _():
                    first_row = (number % FORWARD_STEPS) * rows
                    source_ref[...] = latent_ref[...] + dot_nn(
                        prior_refs[number // FORWARD_STEPS][first_row : first_row + rows, :], blocks[2][...]
                    )

        hidden_ref[...] = lowered(layer_norm(source_ref[...], scale_ref, column))

        @pl.when(step == 0)
        def _():
            arrived(first_s, sems.at[0])

        pieces = 4
        span = width // pieces
        for piece in range(pieces):
            cut = slice(piece * span, (piece + 1) * span)
            active, steep = gelu_both(dot_nn(hidden_ref[...], first_s[:, cut]))
            active_ref[:, cut] = lowered(active)
            steep_ref[:, cut] = lowered(steep)

        @pl.when(step == 0)
        def _():
            arrived(second_s, sems.at[1])

        out_ref[...] = source_ref[...] + dot_nn(active_ref[...], second_s[...])
        if pool:
            normed = layer_norm(out_ref[...], scale_ref, 8)
            part = jnp.sum(normed, axis=0, keepdims=True)

            @pl.when(step % FORWARD_STEPS == 0)
            def _():
                pool_s[...] = part

            @pl.when(step % FORWARD_STEPS != 0)
            def _():
                pool_s[...] += part

            @pl.when(step % FORWARD_STEPS == FORWARD_STEPS - 1)
            def _():
                more[0][0] = lowered(pool_s[...] / tokens)

    out_shape = [shaped((total, width), jnp.float32)] + [shaped((total, width), jnp.bfloat16)] * 3
    out_specs = [by_crop((rows, width))] * 4
    if pool:
        out_shape.append(shaped((micro, 1, width), jnp.bfloat16))
        out_specs.append(pl.BlockSpec((1, 1, width), lambda m: (m // FORWARD_STEPS, 0, 0)))
    in_specs = [SMEM, whole((16, width)), by_crop((rows, width))]
    operands = [me, scales, latent]
    if prior:
        out_shape.append(shaped((total, width), jnp.float32))
        out_specs.append(by_crop((rows, width)))
        in_specs += [whole((tokens, width))] * micro
        operands += prior[0]
    return launch(
        kernel,
        after,
        operands + [array for part in parts for array in part[0].arrays],
        in_specs + [ANY] * sum(counts),
        grid=(micro * FORWARD_STEPS,),
        out_specs=out_specs,
        out_shape=out_shape,
        scratch_shapes=[VMEM((width, width), jnp.bfloat16)] * len(parts)
        + [VMEM((1, width), jnp.float32), pltpu.SemaphoreType.DMA((len(parts),))],
        compiler_params=params(48, big=60),
        cost_estimate=cost(18),
        name="feed_forward",
    )


def run_self_forward(crop, me, scales, latent, query, key, value, micro, after=()):
    total, width = latent.shape
    tokens = total // micro
    part = width // HEADS
    pair = GROUP * part
    turns = HEADS // GROUP
    parts = (query, key, value)
    counts = [len(entry[0].arrays) for entry in parts]

    def kernel(me_ref, scale_ref, latent_ref, *refs):
        groups = []
        at = 0
        for count in counts:
            groups.append(refs[at : at + count])
            at += count
        hidden_ref, packed_ref, attend_ref, blended_ref, packed_s, sems = refs[at:]
        turn = pl.program_id(0)

        @pl.when(turn == 0)
        def _():
            for number in range(3):
                parts[number][0].start(
                    groups[number], me_ref[0], packed_s.at[number], sems.at[number], parts[number][1]
                )
            hidden_ref[...] = lowered(layer_norm(latent_ref[...], scale_ref, 4))
            for number in range(3):
                arrived(packed_s.at[number], sems.at[number])
                packed_ref[:, number * width : (number + 1) * width] = lowered(
                    dot_nn(hidden_ref[...], packed_s[number])
                )

        base = pl.multiple_of(turn * pair, pair)
        queries = packed_ref[:, pl.ds(base, pair)]
        keys = packed_ref[:, pl.ds(pl.multiple_of(width + base, pair), pair)]
        values = packed_ref[:, pl.ds(pl.multiple_of(2 * width + base, pair), pair)]
        joined = []
        for head in range(GROUP):
            cut = slice(head * part, (head + 1) * part)
            attend = lowered(softmax(dot_nt(queries[:, cut], keys[:, cut]) * part ** (-0.5)))
            attend_ref[head] = attend
            joined.append(lowered(dot_nn(attend, values[:, cut])))
        blended_ref[:, pl.ds(base, pair)] = jnp.concatenate(joined, axis=1)

    return launch(
        kernel,
        after,
        [me, scales, latent, *[array for entry in parts for array in entry[0].arrays]],
        [
            SMEM,
            whole((16, width)),
            pl.BlockSpec((tokens, width), lambda h: (crop, 0)),
        ]
        + [ANY] * sum(counts),
        grid=(turns,),
        out_specs=[
            whole((tokens, width)),
            whole((tokens, 3 * width)),
            pl.BlockSpec((GROUP, tokens, tokens), lambda h: (h, 0, 0)),
            whole((tokens, width)),
        ],
        out_shape=[
            shaped((tokens, width), jnp.bfloat16),
            shaped((tokens, 3 * width), jnp.bfloat16),
            shaped((HEADS, tokens, tokens), jnp.bfloat16),
            shaped((tokens, width), jnp.bfloat16),
        ],
        scratch_shapes=[
            VMEM((3, width, width), jnp.bfloat16),
            pltpu.SemaphoreType.DMA((3,)),
        ],
        compiler_params=params(48, big=60),
        cost_estimate=cost(14),
        name="self_forward",
    )


def run_losses(me, pooled, head, classes, examples, micro, after=()):
    count, width = pooled.shape[0], pooled.shape[1] - MARKS
    parts = (head[0], head[1])
    counts = [len(entry[0].arrays) for entry in parts]
    span = width // 2

    def kernel(me_ref, pooled_ref, *refs):
        groups = (refs[: counts[0]], refs[counts[0] : counts[0] + counts[1]])
        loss_ref, logits_ref, grad_ref, left_s, right_s, sems = refs[counts[0] + counts[1] :]
        me_now = me_ref[0]
        halves = (left_s, right_s)
        for number in range(2):
            parts[number][0].start(
                groups[number], me_now, halves[number], sems.at[number], parts[number][1]
            )
        rows = lax.broadcasted_iota(jnp.int32, (count, 1), 0)
        turn = rows % micro
        marks = pooled_ref[:, width:].astype(jnp.float32)
        labels = (marks[:, 0:1] * 256.0 + marks[:, 1:2]).astype(jnp.int32)
        partner = (marks[:, 2:3] * 256.0 + marks[:, 3:4]).astype(jnp.int32)
        active = marks[:, 4:5]
        pooled_low = pooled_ref[:, :width]
        pooled_wide = pooled_low.astype(jnp.float32)
        columns = lax.broadcasted_iota(jnp.int32, (count, count), 1)
        aimed = lowered((columns == partner * micro + turn).astype(jnp.float32))
        distance = pooled_wide - dot_nn(aimed, pooled_low)
        divisor = jnp.zeros((count, 1), jnp.float32)
        for number in range(micro):
            here = (turn == number).astype(jnp.float32)
            counted = jnp.sum(here * active, axis=0, keepdims=True)
            loss_ref[1 + number : 2 + number] = jnp.broadcast_to(counted, (1, 128))
            counted = jnp.maximum(counted, 1.0)
            divisor = divisor + here * (counted * width**0.5)
        agreement = active * jnp.sum(distance * distance, axis=-1, keepdims=True) / divisor
        pull = (2.0 / micro) * (active / divisor) * distance
        for number in range(2):
            arrived(halves[number], sems.at[number])
        logits = jnp.concatenate([dot_nn(pooled_low, half[...]) for half in halves], axis=1)
        column = lax.broadcasted_iota(jnp.int32, (count, 2 * span), 1)
        logits = jnp.where(column < classes, logits, -1e30)
        top = jnp.max(logits, axis=-1, keepdims=True)
        raised = jnp.exp(logits - top)
        mass = jnp.sum(raised, axis=-1, keepdims=True)
        hot = (column == labels).astype(jnp.float32)
        entropy = top + jnp.log(mass) - jnp.sum(logits * hot, axis=-1, keepdims=True)
        loss = jnp.sum(entropy / examples + agreement, axis=0, keepdims=True) / micro
        loss_ref[0:1] = jnp.broadcast_to(loss, (1, 128))
        grad_logits = lowered((raised / mass - hot) / (examples * micro))
        logits_ref[...] = grad_logits
        grad = pull + sum(
            dot_nt(grad_logits[:, number * span : (number + 1) * span], halves[number][...])
            for number in range(2)
        )
        for number in range(micro):
            own = (rows == me_now * micro + number).astype(jnp.float32)
            aiming = ((partner == me_now) & (turn == number)).astype(jnp.float32)
            grad_ref[number] = jnp.sum(own * grad - aiming * pull, axis=0, keepdims=True)

    return launch(
        kernel,
        after,
        [me, pooled, *[array for entry in parts for array in entry[0].arrays]],
        in_specs=[SMEM, whole(pooled.shape)] + [ANY] * sum(counts),
        grid=(1,),
        out_specs=[whole((8, 128)), whole((count, width)), whole((micro, 1, width))],
        out_shape=[
            shaped((8, 128), jnp.float32),
            shaped((count, width), jnp.bfloat16),
            shaped((micro, 1, width), jnp.float32),
        ],
        scratch_shapes=[
            VMEM((width, span), jnp.bfloat16),
            VMEM((width, span), jnp.bfloat16),
            pltpu.SemaphoreType.DMA((2,)),
        ],
        compiler_params=pltpu.CompilerParams(vmem_limit_bytes=24 * MIB),
        cost_estimate=cost(5),
        name="losses",
    )


class Sender:
    def __init__(self, total, core_rows):
        self.total = total
        self.core_rows = core_rows
        self.groups = total // (2 * core_rows)

    def shapes(self, columns):
        return [shaped((self.groups, self.core_rows, columns), jnp.bfloat16)] * 2

    def start(self, source, core, keep, send, column, sem):
        width = source.shape[1]
        rows = self.core_rows
        for group in range(self.groups):
            for target, side in ((send, 1 - core), (keep, core)):
                spot = pl.multiple_of((2 * group + side) * rows, rows)
                pltpu.make_async_copy(
                    source.at[pl.ds(spot, rows), :],
                    target.at[group, :, column : column + width],
                    sem,
                ).start()


    def start_rows(self, source, core, keep, send, column, rows, side, sem):
        width = source.shape[1]
        each = self.core_rows // rows
        for group in range(self.groups):
            for target, half in ((send, 1 - core), (keep, core)):
                for device in range(each):
                    first = ((2 * group + half) * each + device) * 2 * rows + side * rows
                    pltpu.make_async_copy(
                        source.at[pl.ds(pl.multiple_of(first, rows), rows), :],
                        target.at[group, device * rows : (device + 1) * rows, column : column + width],
                        sem,
                    ).start()


def run_feed_backward(
    me, scales, latent, upstream, steep, first, second, column, micro, pool, crop=None, after=()
):
    total, width = latent.shape
    tokens = total // micro
    rows = tokens // STEPS
    parts = (first, second)
    counts = [len(entry[0].arrays) for entry in parts]
    span = width // 2

    def kernel(me_ref, scale_ref, latent_ref, up_ref, *refs):
        if pool:
            pooled_ref, refs = refs[0], refs[1:]
        steep_ref, refs = refs[0], refs[1:]
        first_refs, refs = refs[: counts[0]], refs[counts[0] :]
        second_refs, refs = refs[: counts[1]], refs[counts[1] :]
        out_ref, gain_ref, low_ref, before_ref, after_ref, first_s, second_s, sems = refs
        step = pl.program_id(0)

        @pl.when(step == 0)
        def _():
            second[0].start(second_refs, me_ref[0], second_s, sems.at[1], second[1])
            first[0].start(first_refs, me_ref[0], first_s, sems.at[0], first[1])
            gain_ref[...] = jnp.zeros(gain_ref.shape, jnp.float32)

        if pool:
            spread = jnp.broadcast_to(pooled_ref[0] / tokens, (rows, width))
            upstream, gain, bias = norm_back(up_ref[...], scale_ref, 8, spread)
            gain_ref[2:3] += gain
            gain_ref[3:4] += bias
            out_ref[...] = upstream
        else:
            out_ref[...] = up_ref[...]
        low_ref[...] = lowered(out_ref[...])

        @pl.when(step == 0)
        def _():
            arrived(second_s, sems.at[1])

        for number in range(2):
            cut = slice(number * span, (number + 1) * span)
            grad = dot_nt(low_ref[...], second_s[cut, :])
            before_ref[:, cut] = lowered(grad * steep_ref[:, cut].astype(jnp.float32))

        @pl.when(step == 0)
        def _():
            arrived(first_s, sems.at[0])

        back, gain, bias = norm_back(
            latent_ref[...], scale_ref, column, dot_nt(before_ref[...], first_s[...])
        )
        gain_ref[0:1] += gain
        gain_ref[1:2] += bias
        out_ref[...] += back
        after_ref[...] = lowered(out_ref[...])

    rows_of = by_crop((rows, width))
    if crop is not None:
        rows_of = pl.BlockSpec((rows, width), lambda m: (crop * STEPS + m, 0))
        total = tokens
    in_specs = [SMEM, whole((16, width)), rows_of, rows_of]
    operands = [me, scales, latent]
    if pool:
        in_specs.append(pl.BlockSpec((1, 1, width), lambda m: (m // STEPS, 0, 0)))
        operands += list(upstream)
    else:
        operands.append(upstream)
    in_specs += [rows_of] + [ANY] * sum(counts)
    operands += [steep] + [array for entry in parts for array in entry[0].arrays]
    return launch(
        kernel,
        after,
        operands,
        in_specs,
        grid=(micro * STEPS if crop is None else STEPS,),
        out_specs=[by_crop((rows, width)), whole((8, width))] + [by_crop((rows, width))] * 3,
        out_shape=[shaped((total, width), jnp.float32), shaped((8, width), jnp.float32)]
        + [shaped((total, width), jnp.bfloat16)] * 3,
        scratch_shapes=[
            VMEM((width, width), jnp.bfloat16),
            VMEM((width, width), jnp.bfloat16),
            pltpu.SemaphoreType.DMA((2,)),
        ],
        compiler_params=params(48, big=60),
        cost_estimate=cost(16 if crop is None else 9),
        name="feed_backward",
    )


def run_self_backward(crop, me, scales, latent, upstream, stored, query, key, value, out, micro, onward, after=()):
    total, width = latent.shape
    tokens = total // micro
    part = width // HEADS
    pair = BACK_GROUP * part
    turns = HEADS // BACK_GROUP
    packed, attend = stored
    parts = (query, key, value, out)
    counts = [len(entry[0].arrays) for entry in parts]

    def kernel(me_ref, scale_ref, latent_ref, up_ref, packed_any, attend_ref, *refs):
        groups = []
        at = 0
        for count in counts:
            groups.append(refs[at : at + count])
            at += count
        if onward is not None:
            at += 1
        grad_out, out_ref, gain_ref, packed_s, out_s, blend_s, grad_ref, latent_s, packed_ref, sems = (
            refs[at:]
        )
        turn = pl.program_id(0)

        @pl.when(turn == 0)
        def _():
            out[0].start(groups[3], me_ref[0], out_s, sems.at[3], out[1])
            pltpu.make_async_copy(packed_any, packed_ref, sems.at[6]).start()
            for number in range(3):
                parts[number][0].start(
                    groups[number], me_ref[0], packed_s.at[number], sems.at[number], parts[number][1]
                )
            pltpu.make_async_copy(
                latent_ref.at[crop * tokens : (crop + 1) * tokens, :], latent_s, sems.at[4]
            ).start()
            arrived(out_s, sems.at[3])
            blend_s[...] = lowered(dot_nt(lowered(up_ref[...]), out_s[...]))
            arrived(packed_ref, sems.at[6])

        base = pl.multiple_of(turn * pair, pair)
        queries = packed_ref[:, pl.ds(base, pair)]
        keys = packed_ref[:, pl.ds(pl.multiple_of(width + base, pair), pair)]
        values = packed_ref[:, pl.ds(pl.multiple_of(2 * width + base, pair), pair)]
        blends = blend_s[:, pl.ds(base, pair)]
        grads = ([], [], [])
        for head in range(BACK_GROUP):
            cut = slice(head * part, (head + 1) * part)
            attend = attend_ref[head]
            grad_attend = dot_nt(blends[:, cut], values[:, cut])
            scores = lowered(
                softmax_back(attend.astype(jnp.float32), grad_attend) * part ** (-0.5)
            )
            grads[2].append(lowered(dot_tn(attend, blends[:, cut])))
            grads[0].append(lowered(dot_nn(scores, keys[:, cut])))
            grads[1].append(lowered(dot_tn(scores, queries[:, cut])))
        for number in range(3):
            spot = pl.ds(pl.multiple_of(number * width + base, pair), pair)
            grad_ref[:, spot] = jnp.concatenate(grads[number], axis=1)
            pltpu.make_async_copy(grad_ref.at[:, spot], grad_out.at[:, spot], sems.at[5]).start()

        @pl.when(turn == turns - 1)
        def _():
            for number in range(3):
                arrived(packed_s.at[number], sems.at[number])
            grad_hidden = sum(
                dot_nt(grad_ref[:, number * width : (number + 1) * width], packed_s[number])
                for number in range(3)
            )
            arrived(latent_s, sems.at[4])
            back, gain, bias = norm_back(latent_s[...], scale_ref, 4, grad_hidden)
            gain_ref[0:1] = gain
            gain_ref[1:2] = bias
            out_ref[...] = up_ref[...] + back
            arrived(grad_ref, sems.at[5])

    def crop_rows(columns):
        return pl.BlockSpec((tokens, columns), lambda h: (crop, 0))

    operands = [me, scales, latent, upstream, packed, attend]
    operands += [array for entry in parts for array in entry[0].arrays]
    aliases = {}
    if onward is not None:
        aliases = {len(operands): 1}
        operands.append(onward)
    return launch(
        kernel,
        after,
        operands,
        grid=(turns,),
        in_specs=[
            SMEM,
            whole((16, width)),
            ANY,
            crop_rows(width),
            ANY,
            pl.BlockSpec((BACK_GROUP, tokens, tokens), lambda h: (h, 0, 0)),
        ]
        + [ANY] * (sum(counts) + len(aliases)),
        input_output_aliases=aliases,
        out_specs=[ANY, crop_rows(width), whole((8, width))],
        out_shape=[
            shaped((tokens, 3 * width), jnp.bfloat16),
            shaped((total, width), jnp.float32),
            shaped((8, width), jnp.float32),
        ],
        scratch_shapes=[
            VMEM((3, width, width), jnp.bfloat16),
            VMEM((width, width), jnp.bfloat16),
            VMEM((tokens, width), jnp.bfloat16),
            VMEM((tokens, 3 * width), jnp.bfloat16),
            VMEM((tokens, width), jnp.float32),
            VMEM((tokens, 3 * width), jnp.bfloat16),
            pltpu.SemaphoreType.DMA((7,)),
        ],
        compiler_params=params(56),
        cost_estimate=cost(20),
        name="self_backward",
    )


def run_weights(me, products, sender, after=()):
    flat = []
    for lefts, rights in products:
        for array, *_ in lefts + rights:
            if not any(array is known for known in flat):
                flat.append(array)
    where = {id(array): number for number, array in enumerate(flat)}
    width = products[0][0][0][0].shape[1]
    count = len(products)
    span = width // 2

    def kernel(me_ref, *refs):
        sources, (keep, send, mat_s), sems = refs[: len(flat)], refs[len(flat) : len(flat) + 3], refs[-1]
        held = refs[len(flat) + 3 : -1]
        core = (me_ref[0] // me_ref[1]) % 2
        copies = [
            pltpu.make_async_copy(source, target, sems.at[1 + number])
            for number, (source, target) in enumerate(zip(sources, held))
        ]
        for copy in copies:
            copy.start()
        there = set()
        for number, (lefts, rights) in enumerate(products):
            for array, *_ in lefts + rights:
                if where[id(array)] not in there:
                    there.add(where[id(array)])
                    copies[where[id(array)]].wait()
            for side in range(2):
                cut = slice(side * span, (side + 1) * span)
                mat_s[number, :, cut] = lowered(
                    sum(
                        dot_tn(
                            held[where[id(left)]][begin : begin + size, :],
                            held[where[id(right)]][
                                top : top + size, at + side * span : at + (side + 1) * span
                            ],
                        )
                        for (left, begin, size), (right, top, at) in zip(lefts, rights)
                    )
                )
            sender.start(mat_s.at[number], core, keep, send, number * width, sems.at[0])
        arrived(mat_s, sems.at[0])

    return launch(
        kernel,
        after,
        [me] + flat,
        [SMEM] + [ANY] * len(flat),
        out_specs=[ANY] * 2,
        out_shape=sender.shapes(count * width),
        scratch_shapes=[VMEM((count, width, width), jnp.bfloat16)]
        + [VMEM(array.shape, array.dtype) for array in flat]
        + [pltpu.SemaphoreType.DMA((1 + len(flat),))],
        compiler_params=pltpu.CompilerParams(vmem_limit_bytes=60 * MIB),
        cost_estimate=cost(3 * count),
        name="weights",
    )


def run_cross_backward(
    crop, me, scales, initial, ups, stored, gains, first, second, micro, before, after=()
):
    tokens, width = ups[crop].shape
    queries, attend, pairs = stored
    spots = pairs.shape[1]
    parts = (first, second)
    counts = [len(entry[0].arrays) for entry in parts]
    small_columns = tokens + 128
    last = crop == micro - 1

    def kernel(me_ref, scale_ref, initial_ref, up_ref, query_ref, attend_ref, pair_ref, gains_ref, *refs):
        if before is not None:
            before_ref, refs = refs[0], refs[1:]
        if last:
            others, refs = refs[: micro - 1], refs[micro - 1 :]
        first_refs, refs = refs[: counts[0]], refs[counts[0] :]
        second_refs, refs = refs[: counts[1]], refs[counts[1] :]
        query_out, pair_out, back_ref, first_s, second_s, sems = refs
        second[0].start(second_refs, me_ref[0], second_s, sems.at[1], second[1])
        first[0].start(first_refs, me_ref[0], first_s, sems.at[0], first[1])
        keys, values = pair_ref[0, :, :width], pair_ref[0, :, width:]
        attend = attend_ref[0]
        arrived(second_s, sems.at[1])
        blend = lowered(dot_nt(lowered(up_ref[...]), second_s[...]))
        scores = lowered(softmax_back(attend, dot_nt(blend, values)) * width ** (-0.5))
        query_out[...] = lowered(dot_nn(scores, keys))
        pair_out[:, :width] = lowered(dot_tn(scores, query_ref[...]))
        pair_out[:, width:] = lowered(dot_tn(lowered(attend), blend))
        arrived(first_s, sems.at[0])
        back = dot_nt(query_out[...], first_s[...])
        if before is not None:
            back = before_ref[...] + back
        if not last:
            back_ref[...] = back
            return
        back, gain, bias = norm_back(initial_ref[...], scale_ref, 0, back)
        for other in (up_ref, *others):
            back = back + other[...]
        gains_all = jnp.concatenate(
            [gain, bias, gains_ref[2:, :], jnp.zeros((128 - gains_ref.shape[0], width), jnp.float32)], axis=0
        )
        back_ref[:, :tokens] = lowered(back.T)
        back_ref[:, tokens:] = lowered(gains_all.T)

    back_shape = (
        shaped((width, small_columns), jnp.bfloat16) if last else shaped((tokens, width), jnp.float32)
    )
    extra = [] if before is None else [before]
    if last:
        extra += ups[:crop]
    return launch(
        kernel,
        after,
        [me, scales, initial, ups[crop], queries, attend, pairs, gains]
        + extra
        + [array for entry in parts for array in entry[0].arrays],
        [
            SMEM,
            whole((16, width)),
            whole((tokens, width)),
            whole((tokens, width)),
            whole((tokens, width)),
            pl.BlockSpec((1, tokens, spots), lambda i: (crop, 0, 0)),
            pl.BlockSpec((1, spots, 2 * width), lambda i: (crop, 0, 0)),
            whole((16, width)),
        ]
        + [whole((tokens, width))] * len(extra)
        + [ANY] * sum(counts),
        grid=(1,),
        out_specs=[whole((tokens, width)), whole((spots, 2 * width)), whole(back_shape.shape)],
        out_shape=[
            shaped((tokens, width), jnp.bfloat16),
            shaped((spots, 2 * width), jnp.bfloat16),
            back_shape,
        ],
        scratch_shapes=[
            VMEM((width, width), jnp.bfloat16),
            VMEM((width, width), jnp.bfloat16),
            pltpu.SemaphoreType.DMA((2,)),
        ],
        compiler_params=params(48),
        cost_estimate=cost(9),
        name="cross_backward",
    )


def run_last_weights(me, hidden, grad_queries, grad_pairs, pictures, small, sender, rows, apart, after=()):
    tokens, width = hidden.shape
    micro = len(grad_queries)
    channels = pictures.shape[2]
    small_columns = small.shape[1]
    kv_sender = Sender(2 * width, 2 * sender.core_rows)

    def kernel(me_ref, hidden_ref, *refs):
        query_refs, pair_refs = refs[:micro], refs[micro : 2 * micro]
        pic_ref, small_ref, keep, send = refs[2 * micro : 2 * micro + 4]
        refs = refs[2 * micro + 4 :]
        mat_s, kv_s, sems = refs[-3:]
        core = (me_ref[0] // me_ref[1]) % 2
        sender.start(small_ref, core, keep, send, width, sems.at[2])
        span = width // 2
        for number in range(2):
            cut = slice(number * span, (number + 1) * span)
            mat_s[:, cut] = lowered(
                sum(
                    dot_tn(hidden_ref[...], query_refs[crop][:, cut]) for crop in range(micro)
                )
            )
        sender.start(mat_s, core, keep, send, 0, sems.at[0])
        kv_s[...] = lowered(sum(dot_tn(pair_refs[crop][...], pic_ref[crop]) for crop in range(micro)))
        if apart:
            kv_sender.start(kv_s, core, refs[0], refs[1], 0, sems.at[1])
        else:
            for side in range(2):
                sender.start_rows(
                    kv_s, core, keep, send, width + small_columns + side * channels, rows, side, sems.at[1]
                )
        arrived(mat_s, sems.at[0])
        arrived(kv_s, sems.at[1])
        arrived(small_ref, sems.at[2])

    operands = [me, hidden, *grad_queries, *grad_pairs, pictures, small]
    if apart:
        shapes = sender.shapes(width + small_columns) + kv_sender.shapes(channels)
    else:
        shapes = sender.shapes(width + small_columns + 2 * channels)
    return launch(
        kernel,
        after,
        operands,
        [SMEM] + [whole(array.shape) for array in operands[1:]],
        grid=(1,),
        out_specs=[ANY] * len(shapes),
        out_shape=shapes,
        scratch_shapes=[
            VMEM((width, width), jnp.bfloat16),
            VMEM((2 * width, channels), jnp.bfloat16),
            pltpu.SemaphoreType.DMA((3,)),
        ],
        compiler_params=pltpu.CompilerParams(vmem_limit_bytes=BIG * MIB),
        cost_estimate=cost(6),
        name="last_weights",
    )


def run_shards(matrices, kv_weight, norm_gains, head_weight, latent_init, columns):
    rows = matrices.shape[0]
    tokens, gains = latent_init.shape[1], norm_gains.shape[0]
    channels = kv_weight.shape[1]
    wide_channels = -(-channels // 128) * 128
    classes = head_weight.shape[1]
    width = matrices.shape[1] // 10
    small = tokens + 128

    def kernel(mat_ref, kv_ref, gain_ref, head_ref, latent_ref, first_ref, *refs):
        first_ref[:, tokens:small] = jnp.zeros((rows, small - tokens), jnp.bfloat16)
        first_ref[:, :tokens] = lowered(latent_ref[...])
        first_ref[:, tokens : tokens + gains] = lowered(gain_ref[...].T)
        first_ref[:, small : small + 2 * width] = lowered(mat_ref[:, : 2 * width])
        first_ref[:, small + 2 * width :] = jnp.zeros((rows, 2 * wide_channels), jnp.bfloat16)
        for side in range(2):
            at = small + 2 * width + side * wide_channels
            first_ref[:, at : at + channels] = lowered(kv_ref[side * rows : (side + 1) * rows, :])
        for (begin, end), ref in zip(columns, refs):
            ref[:, : (end - begin) * width] = lowered(mat_ref[:, begin * width : end * width])
        at = refs[-1].shape[1] - width
        refs[-1][:, at:] = jnp.zeros((rows, width), jnp.bfloat16)
        refs[-1][:, at : at + classes] = lowered(head_ref[...])

    widths = [small + 2 * width + 2 * wide_channels] + [(end - begin) * width for begin, end in columns]
    widths[-1] += width
    return pl.pallas_call(
        kernel,
        grid=(1,),
        in_specs=[
            whole(array.shape)
            for array in (matrices, kv_weight, norm_gains, head_weight, latent_init)
        ],
        out_specs=[whole((rows, number)) for number in widths],
        out_shape=[shaped((rows, number), jnp.bfloat16) for number in widths],
        compiler_params=pltpu.CompilerParams(vmem_limit_bytes=62 * MIB),
        cost_estimate=cost(3),
        name="shards",
    )(matrices, kv_weight, norm_gains, head_weight, latent_init)


def run_join(targets, passing, after):
    moves = [move for _, parts in targets for move in parts]
    sources = []
    for array, _, _ in moves:
        if not any(array is known for known in sources):
            sources.append(array)
    where = {id(array): number for number, array in enumerate(sources)}
    count, kept = len(sources), len(passing)

    def kernel(*refs):
        outs = refs[count + kept : count + kept + len(targets)]
        for target, (_, parts) in zip(outs, targets):
            for array, cut, first in parts:
                source = refs[where[id(array)]]
                if cut is None:
                    target[first : first + source.shape[0]] = source[...]
                else:
                    target[first] = source[:, cut]

    vmem = pl.BlockSpec(memory_space=pltpu.VMEM)
    outs = launch(
        kernel,
        after,
        sources + list(passing),
        [vmem] * count + [ANY] * kept,
        out_specs=[vmem] * len(targets) + [ANY] * kept,
        out_shape=[shaped(shape, jnp.bfloat16) for shape, _ in targets]
        + [shaped(array.shape, array.dtype) for array in passing],
        input_output_aliases={count + number: len(targets) + number for number in range(kept)},
        compiler_params=pltpu.CompilerParams(vmem_limit_bytes=16 * MIB),
        cost_estimate=cost(3),
        name="join",
    )
    return outs[: len(targets)], outs[len(targets) :]


def run_fold(me, parts, after):
    depth = 4
    operands = []
    in_specs = []
    out_specs = []
    out_shape = []
    for terms, first, last, axis in parts:
        groups, rows, _ = terms[0].shape
        each = groups // depth
        for term in terms:
            if not any(term is known for known in operands):
                operands.append(term)
                in_specs.append(
                    pl.BlockSpec((each, rows, term.shape[2]), lambda z: (z, 0, 0))
                )
        block = (each, rows // 2, last - first) if axis == "x" else (1, rows, last - first)
        for _ in range(2):
            out_specs.append(pl.BlockSpec(block, lambda z: (z, 0, 0)))
            out_shape.append(shaped((block[0] * depth,) + block[1:], jnp.bfloat16))
    where = {id(term): number for number, term in enumerate(operands)}

    def kernel(me_ref, *refs):
        out = len(operands)
        mine = {"x": me_ref[0] % 2, "y": (me_ref[0] // 4) % 2}
        for terms, first, last, axis in parts:
            sources = [refs[where[id(term)]] for term in terms]
            for side in range(2):
                spot = mine[axis] if side == 0 else 1 - mine[axis]
                if axis == "x":
                    rows = sources[0].shape[1] // 2
                    cut = (slice(None), pl.ds(pl.multiple_of(spot * rows, rows), rows), slice(first, last))
                else:
                    cut = (pl.ds(spot, 1), slice(None), slice(first, last))
                refs[out][...] = lowered(sum(source[cut].astype(jnp.float32) for source in sources))
                out += 1

    outs = launch(
        kernel,
        after,
        [me] + operands,
        [SMEM] + in_specs,
        grid=(depth,),
        out_specs=out_specs,
        out_shape=out_shape,
        compiler_params=params(32),
        cost_estimate=cost(4),
        name="fold",
    )
    return [(outs[2 * number], outs[2 * number + 1]) for number in range(len(parts))]


def run_fold_z(me, parts, after):
    depth = 4
    columns = [terms[0].shape[2] for terms in parts]

    def kernel(me_ref, *refs):
        mine = me_ref[0] // 8
        outs = refs[-depth:]
        at = 0
        column = 0
        for terms, number in zip(parts, columns):
            sources = refs[at : at + len(terms)]
            at += len(terms)
            for k in range(depth):
                outs[k][:, column : column + number] = lowered(
                    sum(source[pl.ds(mine ^ k, 1)].astype(jnp.float32) for source in sources)
                )[0]
            column += number

    vmem = pl.BlockSpec(memory_space=pltpu.VMEM)
    operands = [me] + [term for terms in parts for term in terms]
    shape = shaped((parts[0][0].shape[1], sum(columns)), jnp.bfloat16)
    return launch(
        kernel,
        after,
        operands,
        [SMEM] + [vmem] * (len(operands) - 1),
        out_specs=[vmem] * depth,
        out_shape=[shape] * depth,
        compiler_params=pltpu.CompilerParams(vmem_limit_bytes=24 * MIB),
        cost_estimate=cost(3),
        name="fold_z",
    )


def run_totals(states, grad_head, channels, tokens, gains):
    rows = grad_head.shape[0]
    flat = [term for terms in states for term in terms]
    widths = [terms[0].shape[1] for terms in states]
    small = tokens + 128
    width = widths[1] // 3
    wide_channels = (widths[0] - width - small) // 2
    blocks = width + sum(widths[1:])

    def kernel(head_ref, *refs):
        mat_ref, kv_ref, gain_ref, latent_ref, square_ref = refs[len(flat) :]
        at = 0
        column = width
        square = jnp.sum(head_ref[...] * head_ref[...], axis=0, keepdims=True)
        square = jnp.sum(square, axis=1, keepdims=True)
        for number, (terms, span) in enumerate(zip(states, widths)):
            total = sum(ref[...].astype(jnp.float32) for ref in refs[at : at + len(terms)])
            at += len(terms)
            part = jnp.sum(total * total, axis=0, keepdims=True)
            square = square + jnp.sum(part, axis=1, keepdims=True)
            if number > 0:
                mat_ref[:, column : column + span] = total
                column += span
                continue
            mat_ref[:, :width] = total[:, :width]
            latent_ref[...] = total[:, width : width + tokens]
            gain_ref[...] = total[:, width + tokens : width + small].T[:gains]
            for side in range(2):
                first = width + small + side * wide_channels
                kv_ref[side * rows : (side + 1) * rows, :] = total[:, first : first + channels]
        square_ref[...] = jnp.broadcast_to(square, square_ref.shape)

    shapes = [
            shaped((rows, blocks), jnp.float32),
            shaped((2 * rows, channels), jnp.float32),
            shaped((gains, rows), jnp.float32),
            shaped((rows, tokens), jnp.float32),
            shaped((1, 128), jnp.float32),
    ]
    return pl.pallas_call(
        kernel,
        grid=(1,),
        in_specs=[whole(array.shape) for array in [grad_head] + flat],
        out_specs=[whole(shape.shape) for shape in shapes],
        out_shape=shapes,
        compiler_params=pltpu.CompilerParams(vmem_limit_bytes=32 * MIB),
        cost_estimate=cost(3),
        name="totals",
    )(grad_head, *flat)


def run_update(squares, step_count, shares, masters, firsts, seconds):
    count = len(shares)
    given = [master for master in masters if master is not None]

    def kernel(step_ref, square_ref, *refs):
        share_refs, refs = refs[:count], refs[count:]
        master_refs, refs = list(refs[: len(given)]), refs[len(given) :]
        first_refs, second_refs, outs = refs[:count], refs[count : 2 * count], refs[2 * count :]
        norm = jnp.sqrt(jnp.sum(square_ref[...], axis=0, keepdims=True))
        outs[0][...] = norm
        factor = jnp.minimum(1.0, THRESH / norm[:, 0:1])
        steps = jnp.zeros((1, 1), jnp.float32) + step_ref[0].astype(jnp.float32)
        scale = 1.0 / (1.0 - jnp.exp2(-steps))
        for number in range(count):
            clipped = share_refs[number][...] * factor
            moment_one = 0.5 * first_refs[number][...] + 0.5 * clipped
            moment_two = 0.5 * second_refs[number][...] + 0.5 * clipped * clipped
            outs[1 + 3 * number][...] = moment_one
            outs[2 + 3 * number][...] = moment_two
            if masters[number] is None:
                outs[3 + 3 * number][...] = clipped
                continue
            master = master_refs.pop(0)[...]
            outs[3 + 3 * number][...] = master - RATE * (
                moment_one * scale / (jnp.sqrt(moment_two * scale) + TINY) + DECAY * master
            )

    shapes = [shaped((1, 128), jnp.float32)]
    shapes += [shaped(share.shape, jnp.float32) for share in shares for _ in range(3)]
    operands = [step_count, squares, *shares, *given, *firsts, *seconds]
    return pl.pallas_call(
        kernel,
        grid=(1,),
        in_specs=[SMEM] + [whole(array.shape) for array in operands[1:]],
        out_specs=[whole(shape.shape) for shape in shapes],
        out_shape=shapes,
        compiler_params=pltpu.CompilerParams(vmem_limit_bytes=62 * MIB),
        cost_estimate=cost(5),
        name="update",
    )(*operands)


def digits():
    n_wide = lax.axis_size("wide")
    n_narrow = lax.axis_size("narrow")
    rest = n_wide // 2
    top = min(4, rest)
    return (
        ("z", n_narrow * n_wide // top, top),
        ("y", 2 * n_narrow, rest // top),
        ("c", n_narrow, 2),
        ("x", 1, n_narrow),
    )


def device_index():
    return lax.axis_index("wide") * lax.axis_size("narrow") + lax.axis_index("narrow")


def exchange(values, offset):
    total = lax.axis_size(AXES)
    return lax.ppermute(values, AXES, [(i, i ^ offset) for i in range(total)])


class Gather:
    def __init__(self, shard, first, left, right, plain):
        self.shard = shard
        self.first = first
        self.widths = (left, right)
        self.rows = shard.shape[0]
        self.table = {name: (stride, size) for name, stride, size in digits()}
        self.names = (("y", "x"), ("x", "y"))
        self.plain = plain

    def send_z(self):
        stride, size = self.table["z"]
        self.got = [exchange(self.shard, k * stride) for k in range(1, size)]
        return self.got

    def join(self, targets, passing, after):
        if self.plain:
            flats = []
            for _, parts in targets:
                flats.append(
                    jnp.concatenate(
                        [
                            array if array.ndim == 3 else array[None, :, cut]
                            for array, cut, _ in parts
                        ]
                    )
                )
            return flats, passing
        return run_join(targets, passing, after)

    def join_z(self, passing=(), after=()):
        stride, size = self.table["z"]
        pieces = [self.shard] + self.got
        targets = []
        at = self.first
        for width in self.widths:
            parts = [(piece, slice(at, at + width), k) for k, piece in enumerate(pieces)]
            targets.append(((size, self.rows, width), parts))
            at += width
        self.flats, passing = self.join(targets, passing, after)
        self.offsets = [[k * stride for k in range(size)]] * 2
        return passing

    def send(self, turn):
        self.got = []
        for half in range(2):
            stride, size = self.table[self.names[half][turn]]
            self.got.append([exchange(self.flats[half], k * stride) for k in range(1, size)])
        return self.got[0] + self.got[1]

    def pieces(self, turn):
        halves = []
        for half in range(2):
            stride, size = self.table[self.names[half][turn]]
            arrays = [self.flats[half]] + self.got[half]
            halves.append(
                (arrays, [[offset ^ (k * stride) for offset in self.offsets[half]] for k in range(size)])
            )
        return halves

    def join_first(self, passing=(), after=()):
        targets = []
        offsets = []
        for arrays, groups in self.pieces(0):
            count = arrays[0].shape[0]
            parts = [(array, None, k * count) for k, array in enumerate(arrays)]
            targets.append(((count * len(arrays),) + arrays[0].shape[1:], parts))
            offsets.append([offset for group in groups for offset in group])
        self.flats, passing = self.join(targets, passing, after)
        self.offsets = offsets
        return passing

    def held(self):
        return list(self.flats) + self.got[0] + self.got[1]

    def release(self, arrays):
        self.flats = arrays[:2]
        count = len(self.got[0])
        self.got = [list(arrays[2 : 2 + count]), list(arrays[2 + count :])]

    def send_across(self):
        stride = self.table["c"][0]
        self.state = []
        fresh = []
        for arrays, offsets in self.pieces(1):
            sent = [exchange(array, stride) for array in arrays]
            fresh += sent
            self.state.append(
                (
                    arrays + sent,
                    offsets + [[offset ^ stride for offset in group] for group in offsets],
                )
            )
        return fresh

    def done(self):
        halves = []
        me = device_index()
        total = lax.axis_size(AXES)
        for arrays, offsets in self.state:
            if not self.plain:
                halves.append(Half(arrays, offsets, self.rows))
            else:
                flat = jnp.concatenate(arrays)
                spots = jnp.argsort(jnp.array([o for group in offsets for o in group]) ^ me)
                flat = jnp.take(flat, spots, axis=0).reshape(1, total * self.rows, -1)
                halves.append(Half([flat], None, total * self.rows))
        return halves


class Scatter:
    def __init__(self, me, keep, send, cut, plain, extra=None):
        self.me = me
        self.keep = keep
        self.columns = keep.shape[2]
        self.cut = cut
        self.plain = plain
        self.table = {name: (stride, size) for name, stride, size in digits()}
        self.pairs = [(keep, send)] + ([extra] if extra is not None else [])
        self.names = (("x", "y"), ("y", "x"), ("y", "x"))
        self.last = keep

    def send_across(self):
        stride = self.table["c"][0]
        fresh = [exchange(send, stride) for _, send in self.pairs]
        if not self.plain:
            terms = [self.keep, fresh[0]]
            self.state = [(terms, 0, self.cut), (terms, self.cut, self.columns)]
            return fresh
        sizes = tuple(self.table[name][1] for name in ("z", "y", "x"))
        self.state = []
        for number, ((keep, _), received) in enumerate(zip(self.pairs, fresh)):
            rows = keep.shape[0] * keep.shape[1] // (sizes[0] * sizes[1] * sizes[2])
            terms = [term.reshape(sizes + (rows, keep.shape[2])) for term in (keep, received)]
            if number == 0:
                self.state.append((["z", "y", "x"], [term[..., : self.cut] for term in terms]))
                self.state.append((["z", "y", "x"], [term[..., self.cut :] for term in terms]))
            else:
                self.state.append((["z", "y", "x"], terms))
        return fresh

    def send(self, turn, after=()):
        fresh = []
        if not self.plain:
            if turn == 2:
                kept, *sends = run_fold_z(self.me, [terms for terms, _, _ in self.state], after)
                stride = self.table["z"][0]
                fresh = [exchange(send, (k + 1) * stride) for k, send in enumerate(sends)]
                self.state = [kept] + fresh
                self.last = kept
                return fresh
            names = [ways[turn] for ways in self.names]
            pairs = run_fold(
                self.me, [entry + (name,) for entry, name in zip(self.state, names)], after
            )
            self.state = []
            for (kept, send), name in zip(pairs, names):
                received = exchange(send, self.table[name][0])
                fresh.append(received)
                self.state.append(([kept, received], 0, kept.shape[2]))
            self.last = pairs[0][0]
            return fresh
        me = device_index()
        for number, (left, terms) in enumerate(self.state):
            name = (self.names[number] + ("z",))[turn]
            stride, size = self.table[name]
            mine = (me // stride) % size
            axis = left.index(name)

            def part(index):
                return lowered(
                    sum(
                        lax.dynamic_index_in_dim(term, index, axis, keepdims=False).astype(jnp.float32)
                        for term in terms
                    )
                )

            kept = part(mine)
            sent = [exchange(part(mine ^ k), k * stride) for k in range(1, size)]
            fresh += sent
            self.state[number] = ([entry for entry in left if entry != name], [kept] + sent)
            self.last = kept
        return fresh

    def done(self):
        if not self.plain:
            return sum(term.astype(jnp.float32) for term in self.state)
        sums = [sum(term.astype(jnp.float32) for term in terms) for _, terms in self.state]
        rows = sums[0].shape[0]
        if len(sums) > 2:
            sums[2:] = [sums[2][:rows], sums[2][rows:]]
        return jnp.concatenate(sums, axis=1)


def share(values):
    total = lax.axis_size(AXES)
    spread = jnp.broadcast_to(values[None], (total,) + values.shape)
    return lax.all_to_all(spread, AXES, 0, 0, tiled=True)


def on_device(
    pixels,
    labels,
    partner,
    pair_on,
    step_count,
    matrices,
    kv_weight,
    norm_gains,
    head_weight,
    latent_init,
    matrices_first,
    kv_first,
    gains_first,
    head_first,
    latent_first,
    matrices_second,
    kv_second,
    gains_second,
    head_second,
    latent_second,
):
    axis_count = lax.axis_size(AXES)
    n_narrow = lax.axis_size("narrow")
    index = device_index()
    me = jnp.stack([index, jnp.int32(n_narrow)]).astype(jnp.int32)
    micro = pixels.shape[0]
    tokens = latent_init.shape[1]
    width = matrices.shape[1] // 10
    rows = matrices.shape[0]
    channels = pixels.shape[3]
    wide_channels = -(-channels // 128) * 128
    classes = head_weight.shape[1]

    half = width // 2
    wide_half = width + half
    small_columns = tokens + 128
    plain = rows % 16 != 0 or tuple(size for _, _, size in digits()) != (4, 2, 2, 2)
    pictures = jnp.pad(pixels[:, 0], ((0, 0), (0, 0), (0, wide_channels - channels)))
    blocks = ((2, 4), (4, 7), (7, 10))
    shards = run_shards(matrices, kv_weight, norm_gains.T, head_weight, latent_init, blocks)
    chunks = [
        Gather(shards[0], 0, small_columns + width, width + 2 * wide_channels, plain),
        Gather(shards[1], 0, width, width, plain),
        Gather(shards[2], 0, wide_half, wide_half, plain),
        Gather(shards[3], 0, 2 * width, 2 * width, plain),
    ]

    def block(halves, column, last=width):
        left = halves[0].arrays[0].shape[2]
        if column >= left:
            return [(halves[1], column - left, 0, last)]
        if column + last <= left:
            return [(halves[0], column, 0, last)]
        return [(halves[0], column, 0, left - column), (halves[1], 0, left - column, last)]

    first, second, third, fourth = chunks
    first.send_z()
    second.send_z()
    (pictures,) = first.join_z([pictures])
    first.send(0)
    first.join_first()
    first.send(1)
    (third.shard,) = second.join_z([third.shard], after=first.flats)
    second.send(0)
    third.send_z()
    first.send_across()
    second.join_first()
    second.send(1)
    halves = first.done()
    weights = {0: (halves[0], small_columns), 1: (halves[1], 0)}
    small_half, kv_half = (halves[0], 0), (halves[1], width)
    if kv_half[0].offsets is None:
        array = kv_half[0].arrays[0][..., width:].reshape(axis_count, rows, 2, wide_channels)
        array = array.transpose(0, 2, 1, 3).reshape(1, 2 * width, wide_channels)
        kv_half = (Half([array], None, 2 * width), 0)
    latent_one, blended, attend, pairs, initial, hidden_zero, queries, scales = run_cross_forward(
        me, pictures, small_half, kv_half, weights[0], weights[1], width, tokens,
        after=second.flats,
    )
    second.release(second.join([], second.held(), [latent_one])[1])
    second.send_across()
    (fourth.shard,) = third.join_z([fourth.shard], after=second.flats)
    third.send(0)
    fourth.send_z()
    third.join_first(after=third.flats)
    third.send(1)
    for number in range(2):
        weights[2 + number] = (second.done()[number], 0)
    latent_two, hidden_one, active_one, steep_one = run_feed_forward(
        me, scales, latent_one, weights[2], weights[3], 2, micro, False,
        after=third.flats,
    )
    third.release(fourth.join_z(third.held(), after=[latent_two]))
    third.send_across()
    fourth.send(0)
    fourth.join_first()
    fourth.send(1)
    halves = third.done()
    for number in range(3):
        weights[4 + number] = (Joint(block(halves, number * width)), 0)
    hidden_two, packed, attend_self, blended_self = [], [], [], []
    for crop in range(micro):
        outs = run_self_forward(
            crop, me, scales, latent_two, weights[4], weights[5], weights[6], micro,
            after=fourth.flats if crop == 0 else fourth.flats,
        )
        for entries, out in zip((hidden_two, packed, attend_self, blended_self), outs):
            entries.append(out)
        if crop == 0:
            fourth.release(fourth.join([], fourth.held(), [blended_self[0]])[1])
            fourth.send_across()
    halves = fourth.done()
    weights[7], weights[8], weights[9] = (halves[0], 0), (halves[0], width), (halves[1], 0)
    result, hidden_three, active_three, steep_three, pooled, latent_three = run_feed_forward(
        me, scales, latent_two, weights[8], weights[9], 6, micro, True, (blended_self, weights[7])
    )
    marks = jnp.stack(
        [labels[:, 0] // 256, labels[:, 0] % 256, partner[:, 0] // 256, partner[:, 0] % 256, pair_on[:, 0]],
        axis=1,
    )
    marks = jnp.pad(lowered(marks), ((0, 0), (0, MARKS - marks.shape[1])))
    pooled_all = share(jnp.concatenate([pooled.reshape(micro, width), marks], axis=1))
    pooled_all = pooled_all.reshape(axis_count * micro, width + MARKS)
    loss_tile, grad_logits, grad_pooled = run_losses(
        me, pooled_all, [(halves[1], width), (halves[1], width + half)], classes, axis_count, micro
    )
    total_loss = loss_tile[0, 0]
    counts = loss_tile[1 : 1 + micro, 0].astype(jnp.int32)
    pooled_rows = lax.dynamic_slice_in_dim(pooled_all, index * rows, rows, axis=1)
    grad_head = dot_tn(pooled_rows, grad_logits)[:, :classes]

    sender = Sender(width, n_narrow * rows)
    total_tokens = micro * tokens

    def single(left, right):
        return [(left, 0, total_tokens)], [(right, 0, 0)]

    upstream, gain_high, low, before, behind = run_feed_backward(
        me, scales, latent_three, (result, grad_pooled), steep_three, weights[8], weights[9], 6, micro, True
    )
    keep, send = run_weights(
        me,
        [
            (
                [(rows_of, 0, tokens) for rows_of in blended_self],
                [(behind, crop * tokens, 0) for crop in range(micro)],
            ),
            single(hidden_three, before),
            single(active_three, low),
        ],
        sender,
    )
    one = Scatter(me, keep, send, wide_half, plain)
    one.send_across()
    grads = []
    gain_mid = 0.0
    onward = None
    for crop in range(micro):
        waits = ()
        if crop == 1:
            one.send(0, after=[onward])
            waits = [one.last]
        grad_packed, onward, gain = run_self_backward(
            crop, me, scales, latent_two, upstream, (packed[crop], attend_self[crop]),
            weights[4], weights[5], weights[6], weights[7], micro, onward, after=waits,
        )
        grads.append(grad_packed)
        gain_mid = gain_mid + gain
    upstream = onward
    one.send(1, after=[onward])
    keep, send = run_weights(
        me,
        [
            (
                [(hidden_two[crop], 0, tokens) for crop in range(micro)],
                [(grads[crop], 0, number * width) for crop in range(micro)],
            )
            for number in range(3)
        ],
        sender,
        after=[one.last],
    )
    two = Scatter(me, keep, send, wide_half, plain)
    two.send_across()
    ups, lows, befores, behinds = [], [], [], []
    gain_low = 0.0
    for crop in range(micro):
        outs = run_feed_backward(
            me, scales, latent_one, upstream, steep_one, weights[2], weights[3], 2, micro, False, crop,
            after=[keep] if crop == 0 else [two.last, one.last],
        )
        gain_low = gain_low + outs[1]
        for entries, out in zip((ups, lows, befores, behinds), (outs[0],) + tuple(outs[2:])):
            entries.append(out)
        if crop == 0:
            arriving = two.send(0, after=[outs[0]])
            one_z = one.send(2, after=[two.last])
    keep, send = run_weights(
        me,
        [
            (
                [(left, crop * tokens, tokens) for crop in range(micro)],
                [(rights[crop], 0, 0) for crop in range(micro)],
            )
            for left, rights in ((blended, behinds), (hidden_one, befores), (active_one, lows))
        ],
        sender,
        after=ups[-1:] + arriving,
    )
    three = Scatter(me, keep, send, wide_half, plain)
    three.send_across()
    two.send(1, after=[keep])
    gains = jnp.concatenate(
        [
            jnp.zeros((2, width), jnp.float32),
            gain_low[:2],
            gain_mid[:2],
            gain_high[:4],
            jnp.zeros((6, width), jnp.float32),
        ]
    )
    grad_queries, grad_pairs = [], []
    back = None
    for crop in range(micro):
        outs = run_cross_backward(
            crop, me, scales, initial, ups, (queries, attend, pairs), gains,
            weights[0], weights[1], micro, back, after=[two.last],
        )
        grad_queries.append(outs[0])
        grad_pairs.append(outs[1])
        back = outs[2]
        if crop == 0:
            arriving = three.send(0, after=[back] + one_z)
            two_z = two.send(2, after=[three.last])
    grad_small = back
    keep, send, *extra = run_last_weights(
        me, hidden_zero, grad_queries, grad_pairs, pictures, grad_small,
        sender, rows, plain, after=arriving + two_z,
    )
    four = Scatter(me, keep, send, width, plain, extra or None)
    four.send_across()
    arriving = three.send(1, after=[keep])
    four.send(0, after=arriving)
    arriving = three.send(2, after=[four.last])
    four.send(1, after=arriving)
    four.send(2)
    if plain:
        last = four.done()
        grad_matrices = jnp.concatenate(
            [last[:, :width], three.done(), two.done(), one.done()], axis=1
        )
        grad_kv = last[:, width + small_columns :]
        grad_kv = jnp.concatenate(
            [grad_kv[:, :channels], grad_kv[:, wide_channels : wide_channels + channels]]
        )
        grad_small = last[:, width : width + small_columns]
        grad_gains, grad_latent = grad_small[:, tokens : tokens + 10].T, grad_small[:, :tokens]
        shares = (grad_matrices, grad_kv, grad_gains, grad_head, grad_latent)
        square = sum(jnp.sum(member * member) for member in shares)
        square = jnp.broadcast_to(square, (1, 128))
    else:
        grad_matrices, grad_kv, grad_gains, grad_latent, square = run_totals(
            [four.state, three.state, two.state, one.state],
            grad_head,
            channels,
            tokens,
            norm_gains.shape[1],
        )
    shares = (grad_matrices, grad_kv, grad_gains, grad_head, grad_latent)
    norm, *results = run_update(
        share(square[0]),
        step_count,
        shares,
        (matrices, kv_weight, None, head_weight, None),
        (matrices_first, kv_first, gains_first.T, head_first, latent_first),
        (matrices_second, kv_second, gains_second.T, head_second, latent_second),
    )
    results[6:9] = [result.T for result in results[6:9]]
    return (total_loss, norm[0, 0], counts, *results)


def solution(mesh):
    in_specs = (
        P(None, ("wide", "narrow"), None, None),
        P(None, ("wide", "narrow")),
        P(None, ("wide", "narrow")),
        P(None, ("wide", "narrow")),
        P(),
        P(("wide", "narrow"), None),
        P(("wide", "narrow"), None),
        P(("wide", "narrow"), None),
        P(("wide", "narrow"), None),
        P(("wide", "narrow"), None),
        P(("wide", "narrow"), None),
        P(("wide", "narrow"), None),
        P(("wide", "narrow"), None),
        P(("wide", "narrow"), None),
        P(("wide", "narrow"), None),
        P(("wide", "narrow"), None),
        P(("wide", "narrow"), None),
        P(("wide", "narrow"), None),
        P(("wide", "narrow"), None),
        P(("wide", "narrow"), None),
    )
    out_specs = (
        P(),
        P(),
        P(),
        P(("wide", "narrow"), None),
        P(("wide", "narrow"), None),
        P(("wide", "narrow"), None),
        P(("wide", "narrow"), None),
        P(("wide", "narrow"), None),
        P(("wide", "narrow"), None),
        P(("wide", "narrow"), None),
        P(("wide", "narrow"), None),
        P(("wide", "narrow"), None),
        P(("wide", "narrow"), None),
        P(("wide", "narrow"), None),
        P(("wide", "narrow"), None),
        P(("wide", "narrow"), None),
        P(("wide", "narrow"), None),
        P(("wide", "narrow"), None),
    )
    return jax.shard_map(
        on_device, mesh=mesh, in_specs=in_specs, out_specs=out_specs, check_vma=False
    )
```

```python
import functools

import jax
import jax.numpy as jnp
from jax import lax
from jax.experimental import pallas as pl
from jax.experimental.pallas import tpu as pltpu
from jax.sharding import PartitionSpec as P

HEADS = 8
GROUP = 4
BACK_GROUP = 2
STEPS = 2
FORWARD_STEPS = 1
AXES = ("wide", "narrow")

EPSILON = 1e-05
RATE = 0.03
DECAY = 0.1
TINY = 1e-08
THRESH = 0.01
BEND = 0.044715
MARKS = 128
SLOPE = 0.7978845608028654
VMEM = pltpu.VMEM
MIB = 1 << 20
BIG = 48
PACE = 0.5


def lowered(values):
    return values.astype(jnp.bfloat16)


def dot_nn(first_op, second_op):
    return jnp.dot(first_op, second_op, preferred_element_type=jnp.float32)


def dot_tn(first_op, second_op):
    return lax.dot_general(
        first_op, second_op, (((0,), (0,)), ((), ())), preferred_element_type=jnp.float32
    )


def dot_nt(first_op, second_op):
    return lax.dot_general(
        first_op, second_op, (((1,), (1,)), ((), ())), preferred_element_type=jnp.float32
    )


def standard(inputs):
    center = inputs - jnp.mean(inputs, axis=-1, keepdims=True)
    scale = lax.rsqrt(jnp.mean(center * center, axis=-1, keepdims=True) + EPSILON)
    return center * scale, scale


def layer_norm(inputs, scales, column):
    return standard(inputs)[0] * scales[column : column + 1, :] + scales[column + 1 : column + 2, :]


def norm_back(inputs, scales, column, upstream):
    unit, scale = standard(inputs)
    gain = jnp.sum(upstream * unit, axis=0, keepdims=True)
    bias = jnp.sum(upstream, axis=0, keepdims=True)
    inner = upstream * scales[column : column + 1, :]
    back = scale * (
        inner
        - jnp.mean(inner, axis=-1, keepdims=True)
        - unit * jnp.mean(inner * unit, axis=-1, keepdims=True)
    )
    return back, gain, bias


def gelu_both(values):
    square = values * values
    bent = jnp.tanh(SLOPE * values * (1.0 + BEND * square))
    half = 0.5 * (1.0 + bent)
    steep = half + 0.5 * values * (1.0 - bent * bent) * SLOPE * (1.0 + 3.0 * BEND * square)
    return values * half, steep


def softmax(scores):
    raised = jnp.exp(scores - jnp.max(scores, axis=-1, keepdims=True))
    return raised * (1.0 / jnp.sum(raised, axis=-1, keepdims=True))


def softmax_back(attend, upstream):
    return attend * (upstream - jnp.sum(upstream * attend, axis=-1, keepdims=True))


class Half:
    def __init__(self, arrays, offsets, rows):
        self.arrays = arrays
        self.offsets = offsets
        self.rows = rows

    def start(self, refs, me, target, sem, column, stride=None, shift=0):
        width = target.shape[1]
        if self.offsets is None:
            pltpu.make_async_copy(refs[0].at[0, :, column : column + width], target, sem).start()
            return
        stride = self.rows if stride is None else stride
        for ref, offsets in zip(refs, self.offsets):
            for group, offset in enumerate(offsets):
                spot = pl.multiple_of((me ^ offset) * stride + shift, self.rows)
                pltpu.make_async_copy(
                    ref.at[group, :, column : column + width],
                    target.at[pl.ds(spot, self.rows), :],
                    sem,
                ).start()


class Joint:
    def __init__(self, pieces):
        self.pieces = pieces
        self.arrays = [array for half, *_ in pieces for array in half.arrays]

    def start(self, refs, me, target, sem, column):
        at = 0
        for half, spot, first, last in self.pieces:
            count = len(half.arrays)
            half.start(refs[at : at + count], me, target.at[:, first:last], sem, spot)
            at += count


def arrived(target, sem):
    pltpu.make_async_copy(target, target, sem).wait()


def cost(micros):
    return pl.CostEstimate(flops=int(micros * PACE * 1.1e9), bytes_accessed=1 << 10, transcendentals=0)


def params(mib, dims=1, big=None):
    return pltpu.CompilerParams(
        vmem_limit_bytes=(big or max(mib, BIG)) * MIB, dimension_semantics=("arbitrary",) * dims
    )


def launch(kernel, after, operands, in_specs, **rest):
    extra = len(after)

    def inner(*refs):
        kernel(*refs[: len(operands)], *refs[len(operands) + extra :])

    return pl.pallas_call(inner, in_specs=list(in_specs) + [ANY] * extra, **rest)(*operands, *after)


ANY = pl.BlockSpec(memory_space=pl.ANY)
SMEM = pl.BlockSpec(memory_space=pltpu.SMEM)


def whole(shape):
    return pl.BlockSpec(shape, lambda *ids: (0,) * len(shape))


def by_crop(shape, rank=1):
    return pl.BlockSpec(shape, lambda m, *ids: (m,) + (0,) * (len(shape) - 1))


def shaped(shape, dtype):
    return jax.ShapeDtypeStruct(shape, dtype)


def run_cross_forward(me, pictures, small, kv, first, second, width, tokens, after=()):
    micro, spots, channels = pictures.shape
    parts = (small, kv, first, second)
    counts = [len(part[0].arrays) for part in parts]
    small_columns = tokens + 128

    def kernel(me_ref, pic_ref, *refs):
        groups = []
        at = 0
        for count in counts:
            groups.append(refs[at : at + count])
            at += count
        latent_ref, blended_ref, attend_ref, pair_ref, initial_ref, hidden_ref, query_ref, scale_ref = refs[at : at + 8]
        small_s, kv_s, first_s, second_s, sems = refs[at + 8 :]
        me_now = me_ref[0]
        step = pl.program_id(0)

        @pl.when(step == 0)
        def _():
            small[0].start(groups[0], me_now, small_s, sems.at[0], small[1])
            if kv[0].offsets is None:
                kv[0].start(groups[1], me_now, kv_s, sems.at[1], 0)
            else:
                rows = kv[0].rows
                kv[0].start(groups[1], me_now, kv_s, sems.at[1], kv[1], 2 * rows, 0)
                kv[0].start(groups[1], me_now, kv_s, sems.at[1], kv[1] + channels, 2 * rows, rows)
            first[0].start(groups[2], me_now, first_s, sems.at[2], first[1])
            second[0].start(groups[3], me_now, second_s, sems.at[3], second[1])
            arrived(small_s, sems.at[0])
            turned = small_s[...].astype(jnp.float32).T
            initial_ref[...] = turned[:tokens]
            scale_ref[...] = turned[tokens : tokens + 16]
            hidden_ref[...] = lowered(layer_norm(initial_ref[...], scale_ref, 0))
            arrived(first_s, sems.at[2])
            query_ref[...] = lowered(dot_nn(hidden_ref[...], first_s[...]))
            arrived(kv_s, sems.at[1])
            arrived(second_s, sems.at[3])

        pair_ref[0] = lowered(dot_nt(pic_ref[0], kv_s[...]))
        scores = dot_nt(query_ref[...], pair_ref[0, :, :width]) * width ** (-0.5)
        attend = softmax(scores)
        attend_ref[0] = attend
        blended_ref[...] = lowered(dot_nn(lowered(attend), pair_ref[0, :, width:]))
        latent_ref[...] = initial_ref[...] + dot_nn(blended_ref[...], second_s[...])

    total = micro * tokens
    return launch(
        kernel,
        after,
        [me, pictures, *[array for part in parts for array in part[0].arrays]],
        grid=(micro,),
        in_specs=[SMEM, by_crop((1, spots, channels))] + [ANY] * sum(counts),
        out_specs=[
            by_crop((tokens, width)),
            by_crop((tokens, width)),
            by_crop((1, tokens, spots)),
            by_crop((1, spots, 2 * width)),
            whole((tokens, width)),
            whole((tokens, width)),
            whole((tokens, width)),
            whole((16, width)),
        ],
        out_shape=[
            shaped((total, width), jnp.float32),
            shaped((total, width), jnp.bfloat16),
            shaped((micro, tokens, spots), jnp.float32),
            shaped((micro, spots, 2 * width), jnp.bfloat16),
            shaped((tokens, width), jnp.float32),
            shaped((tokens, width), jnp.bfloat16),
            shaped((tokens, width), jnp.bfloat16),
            shaped((16, width), jnp.float32),
        ],
        scratch_shapes=[
            VMEM((width, small_columns), jnp.bfloat16),
            VMEM((2 * width, channels), jnp.bfloat16),
            VMEM((width, width), jnp.bfloat16),
            VMEM((width, width), jnp.bfloat16),
            pltpu.SemaphoreType.DMA((4,)),
        ],
        compiler_params=params(48),
        cost_estimate=cost(18),
        name="cross_forward",
    )


def run_feed_forward(me, scales, latent, first, second, column, micro, pool, prior=None, after=()):
    total, width = latent.shape
    tokens = total // micro
    rows = tokens // FORWARD_STEPS
    parts = [first, second] + ([prior[1]] if prior else [])
    counts = [len(part[0].arrays) for part in parts]

    def kernel(me_ref, scale_ref, latent_ref, *refs):
        if prior:
            prior_refs, refs = refs[:micro], refs[micro:]
        groups = []
        at = 0
        for count in counts:
            groups.append(refs[at : at + count])
            at += count
        out_ref, hidden_ref, active_ref, steep_ref = refs[at : at + 4]
        more = refs[at + 4 : -2 - len(parts)]
        blocks, pool_s, sems = refs[-2 - len(parts) : -2], refs[-2], refs[-1]
        first_s, second_s = blocks[:2]
        step = pl.program_id(0)

        @pl.when(step == 0)
        def _():
            for number in range(len(parts) - 1, -1, -1) if prior else range(len(parts)):
                parts[number][0].start(
                    groups[number], me_ref[0], blocks[number], sems.at[number], parts[number][1]
                )

        source_ref = latent_ref
        if prior:
            source_ref = more[-1]

            @pl.when(step == 0)
            def _():
                arrived(blocks[2], sems.at[2])

            for number in range(micro * FORWARD_STEPS):

                @pl.when(step == number)
                def _():
                    first_row = (number % FORWARD_STEPS) * rows
                    source_ref[...] = latent_ref[...] + dot_nn(
                        prior_refs[number // FORWARD_STEPS][first_row : first_row + rows, :], blocks[2][...]
                    )

        hidden_ref[...] = lowered(layer_norm(source_ref[...], scale_ref, column))

        @pl.when(step == 0)
        def _():
            arrived(first_s, sems.at[0])

        pieces = 4
        span = width // pieces
        for piece in range(pieces):
            cut = slice(piece * span, (piece + 1) * span)
            active, steep = gelu_both(dot_nn(hidden_ref[...], first_s[:, cut]))
            active_ref[:, cut] = lowered(active)
            steep_ref[:, cut] = lowered(steep)

        @pl.when(step == 0)
        def _():
            arrived(second_s, sems.at[1])

        out_ref[...] = source_ref[...] + dot_nn(active_ref[...], second_s[...])
        if pool:
            normed = layer_norm(out_ref[...], scale_ref, 8)
            part = jnp.sum(normed, axis=0, keepdims=True)

            @pl.when(step % FORWARD_STEPS == 0)
            def _():
                pool_s[...] = part

            @pl.when(step % FORWARD_STEPS != 0)
            def _():
                pool_s[...] += part

            @pl.when(step % FORWARD_STEPS == FORWARD_STEPS - 1)
            def _():
                more[0][0] = lowered(pool_s[...] / tokens)

    out_shape = [shaped((total, width), jnp.float32)] + [shaped((total, width), jnp.bfloat16)] * 3
    out_specs = [by_crop((rows, width))] * 4
    if pool:
        out_shape.append(shaped((micro, 1, width), jnp.bfloat16))
        out_specs.append(pl.BlockSpec((1, 1, width), lambda m: (m // FORWARD_STEPS, 0, 0)))
    in_specs = [SMEM, whole((16, width)), by_crop((rows, width))]
    operands = [me, scales, latent]
    if prior:
        out_shape.append(shaped((total, width), jnp.float32))
        out_specs.append(by_crop((rows, width)))
        in_specs += [whole((tokens, width))] * micro
        operands += prior[0]
    return launch(
        kernel,
        after,
        operands + [array for part in parts for array in part[0].arrays],
        in_specs + [ANY] * sum(counts),
        grid=(micro * FORWARD_STEPS,),
        out_specs=out_specs,
        out_shape=out_shape,
        scratch_shapes=[VMEM((width, width), jnp.bfloat16)] * len(parts)
        + [VMEM((1, width), jnp.float32), pltpu.SemaphoreType.DMA((len(parts),))],
        compiler_params=params(48, big=60),
        cost_estimate=cost(18),
        name="feed_forward",
    )


def run_self_forward(crop, me, scales, latent, query, key, value, micro, after=()):
    total, width = latent.shape
    tokens = total // micro
    part = width // HEADS
    pair = GROUP * part
    turns = HEADS // GROUP
    parts = (query, key, value)
    counts = [len(entry[0].arrays) for entry in parts]

    def kernel(me_ref, scale_ref, latent_ref, *refs):
        groups = []
        at = 0
        for count in counts:
            groups.append(refs[at : at + count])
            at += count
        hidden_ref, packed_ref, attend_ref, blended_ref, packed_s, sems = refs[at:]
        turn = pl.program_id(0)

        @pl.when(turn == 0)
        def _():
            for number in range(3):
                parts[number][0].start(
                    groups[number], me_ref[0], packed_s.at[number], sems.at[number], parts[number][1]
                )
            hidden_ref[...] = lowered(layer_norm(latent_ref[...], scale_ref, 4))
            for number in range(3):
                arrived(packed_s.at[number], sems.at[number])
                packed_ref[:, number * width : (number + 1) * width] = lowered(
                    dot_nn(hidden_ref[...], packed_s[number])
                )

        base = pl.multiple_of(turn * pair, pair)
        queries = packed_ref[:, pl.ds(base, pair)]
        keys = packed_ref[:, pl.ds(pl.multiple_of(width + base, pair), pair)]
        values = packed_ref[:, pl.ds(pl.multiple_of(2 * width + base, pair), pair)]
        joined = []
        for head in range(GROUP):
            cut = slice(head * part, (head + 1) * part)
            attend = lowered(softmax(dot_nt(queries[:, cut], keys[:, cut]) * part ** (-0.5)))
            attend_ref[head] = attend
            joined.append(lowered(dot_nn(attend, values[:, cut])))
        blended_ref[:, pl.ds(base, pair)] = jnp.concatenate(joined, axis=1)

    return launch(
        kernel,
        after,
        [me, scales, latent, *[array for entry in parts for array in entry[0].arrays]],
        [
            SMEM,
            whole((16, width)),
            pl.BlockSpec((tokens, width), lambda h: (crop, 0)),
        ]
        + [ANY] * sum(counts),
        grid=(turns,),
        out_specs=[
            whole((tokens, width)),
            whole((tokens, 3 * width)),
            pl.BlockSpec((GROUP, tokens, tokens), lambda h: (h, 0, 0)),
            whole((tokens, width)),
        ],
        out_shape=[
            shaped((tokens, width), jnp.bfloat16),
            shaped((tokens, 3 * width), jnp.bfloat16),
            shaped((HEADS, tokens, tokens), jnp.bfloat16),
            shaped((tokens, width), jnp.bfloat16),
        ],
        scratch_shapes=[
            VMEM((3, width, width), jnp.bfloat16),
            pltpu.SemaphoreType.DMA((3,)),
        ],
        compiler_params=params(48, big=60),
        cost_estimate=cost(14),
        name="self_forward",
    )


def run_losses(me, pooled, head, classes, examples, micro, after=()):
    count, width = pooled.shape[0], pooled.shape[1] - MARKS
    parts = (head[0], head[1])
    counts = [len(entry[0].arrays) for entry in parts]
    span = width // 2

    def kernel(me_ref, pooled_ref, *refs):
        groups = (refs[: counts[0]], refs[counts[0] : counts[0] + counts[1]])
        loss_ref, logits_ref, grad_ref, left_s, right_s, sems = refs[counts[0] + counts[1] :]
        me_now = me_ref[0]
        halves = (left_s, right_s)
        for number in range(2):
            parts[number][0].start(
                groups[number], me_now, halves[number], sems.at[number], parts[number][1]
            )
        rows = lax.broadcasted_iota(jnp.int32, (count, 1), 0)
        turn = rows % micro
        marks = pooled_ref[:, width:].astype(jnp.float32)
        labels = (marks[:, 0:1] * 256.0 + marks[:, 1:2]).astype(jnp.int32)
        partner = (marks[:, 2:3] * 256.0 + marks[:, 3:4]).astype(jnp.int32)
        active = marks[:, 4:5]
        pooled_low = pooled_ref[:, :width]
        pooled_wide = pooled_low.astype(jnp.float32)
        columns = lax.broadcasted_iota(jnp.int32, (count, count), 1)
        aimed = lowered((columns == partner * micro + turn).astype(jnp.float32))
        distance = pooled_wide - dot_nn(aimed, pooled_low)
        divisor = jnp.zeros((count, 1), jnp.float32)
        for number in range(micro):
            here = (turn == number).astype(jnp.float32)
            counted = jnp.sum(here * active, axis=0, keepdims=True)
            loss_ref[1 + number : 2 + number] = jnp.broadcast_to(counted, (1, 128))
            counted = jnp.maximum(counted, 1.0)
            divisor = divisor + here * (counted * width**0.5)
        agreement = active * jnp.sum(distance * distance, axis=-1, keepdims=True) / divisor
        pull = (2.0 / micro) * (active / divisor) * distance
        for number in range(2):
            arrived(halves[number], sems.at[number])
        logits = jnp.concatenate([dot_nn(pooled_low, half[...]) for half in halves], axis=1)
        column = lax.broadcasted_iota(jnp.int32, (count, 2 * span), 1)
        logits = jnp.where(column < classes, logits, -1e30)
        top = jnp.max(logits, axis=-1, keepdims=True)
        raised = jnp.exp(logits - top)
        mass = jnp.sum(raised, axis=-1, keepdims=True)
        hot = (column == labels).astype(jnp.float32)
        entropy = top + jnp.log(mass) - jnp.sum(logits * hot, axis=-1, keepdims=True)
        loss = jnp.sum(entropy / examples + agreement, axis=0, keepdims=True) / micro
        loss_ref[0:1] = jnp.broadcast_to(loss, (1, 128))
        grad_logits = lowered((raised / mass - hot) / (examples * micro))
        logits_ref[...] = grad_logits
        grad = pull + sum(
            dot_nt(grad_logits[:, number * span : (number + 1) * span], halves[number][...])
            for number in range(2)
        )
        for number in range(micro):
            own = (rows == me_now * micro + number).astype(jnp.float32)
            aiming = ((partner == me_now) & (turn == number)).astype(jnp.float32)
            grad_ref[number] = jnp.sum(own * grad - aiming * pull, axis=0, keepdims=True)

    return launch(
        kernel,
        after,
        [me, pooled, *[array for entry in parts for array in entry[0].arrays]],
        in_specs=[SMEM, whole(pooled.shape)] + [ANY] * sum(counts),
        grid=(1,),
        out_specs=[whole((8, 128)), whole((count, width)), whole((micro, 1, width))],
        out_shape=[
            shaped((8, 128), jnp.float32),
            shaped((count, width), jnp.bfloat16),
            shaped((micro, 1, width), jnp.float32),
        ],
        scratch_shapes=[
            VMEM((width, span), jnp.bfloat16),
            VMEM((width, span), jnp.bfloat16),
            pltpu.SemaphoreType.DMA((2,)),
        ],
        compiler_params=pltpu.CompilerParams(vmem_limit_bytes=24 * MIB),
        cost_estimate=cost(5),
        name="losses",
    )


class Sender:
    def __init__(self, total, core_rows):
        self.total = total
        self.core_rows = core_rows
        self.groups = total // (2 * core_rows)

    def shapes(self, columns):
        return [shaped((self.groups, self.core_rows, columns), jnp.bfloat16)] * 2

    def start(self, source, core, keep, send, column, sem):
        width = source.shape[1]
        rows = self.core_rows
        for group in range(self.groups):
            for target, side in ((send, 1 - core), (keep, core)):
                spot = pl.multiple_of((2 * group + side) * rows, rows)
                pltpu.make_async_copy(
                    source.at[pl.ds(spot, rows), :],
                    target.at[group, :, column : column + width],
                    sem,
                ).start()


    def start_rows(self, source, core, keep, send, column, rows, side, sem):
        width = source.shape[1]
        each = self.core_rows // rows
        for group in range(self.groups):
            for target, half in ((send, 1 - core), (keep, core)):
                for device in range(each):
                    first = ((2 * group + half) * each + device) * 2 * rows + side * rows
                    pltpu.make_async_copy(
                        source.at[pl.ds(pl.multiple_of(first, rows), rows), :],
                        target.at[group, device * rows : (device + 1) * rows, column : column + width],
                        sem,
                    ).start()


def run_feed_backward(
    me, scales, latent, upstream, steep, first, second, column, micro, pool, crop=None, after=()
):
    total, width = latent.shape
    tokens = total // micro
    rows = tokens // STEPS
    parts = (first, second)
    counts = [len(entry[0].arrays) for entry in parts]
    span = width // 2

    def kernel(me_ref, scale_ref, latent_ref, up_ref, *refs):
        if pool:
            pooled_ref, refs = refs[0], refs[1:]
        steep_ref, refs = refs[0], refs[1:]
        first_refs, refs = refs[: counts[0]], refs[counts[0] :]
        second_refs, refs = refs[: counts[1]], refs[counts[1] :]
        out_ref, gain_ref, low_ref, before_ref, after_ref, first_s, second_s, sems = refs
        step = pl.program_id(0)

        @pl.when(step == 0)
        def _():
            second[0].start(second_refs, me_ref[0], second_s, sems.at[1], second[1])
            first[0].start(first_refs, me_ref[0], first_s, sems.at[0], first[1])
            gain_ref[...] = jnp.zeros(gain_ref.shape, jnp.float32)

        if pool:
            spread = jnp.broadcast_to(pooled_ref[0] / tokens, (rows, width))
            upstream, gain, bias = norm_back(up_ref[...], scale_ref, 8, spread)
            gain_ref[2:3] += gain
            gain_ref[3:4] += bias
            out_ref[...] = upstream
        else:
            out_ref[...] = up_ref[...]
        low_ref[...] = lowered(out_ref[...])

        @pl.when(step == 0)
        def _():
            arrived(second_s, sems.at[1])

        for number in range(2):
            cut = slice(number * span, (number + 1) * span)
            grad = dot_nt(low_ref[...], second_s[cut, :])
            before_ref[:, cut] = lowered(grad * steep_ref[:, cut].astype(jnp.float32))

        @pl.when(step == 0)
        def _():
            arrived(first_s, sems.at[0])

        back, gain, bias = norm_back(
            latent_ref[...], scale_ref, column, dot_nt(before_ref[...], first_s[...])
        )
        gain_ref[0:1] += gain
        gain_ref[1:2] += bias
        out_ref[...] += back
        after_ref[...] = lowered(out_ref[...])

    rows_of = by_crop((rows, width))
    if crop is not None:
        rows_of = pl.BlockSpec((rows, width), lambda m: (crop * STEPS + m, 0))
        total = tokens
    in_specs = [SMEM, whole((16, width)), rows_of, rows_of]
    operands = [me, scales, latent]
    if pool:
        in_specs.append(pl.BlockSpec((1, 1, width), lambda m: (m // STEPS, 0, 0)))
        operands += list(upstream)
    else:
        operands.append(upstream)
    in_specs += [rows_of] + [ANY] * sum(counts)
    operands += [steep] + [array for entry in parts for array in entry[0].arrays]
    return launch(
        kernel,
        after,
        operands,
        in_specs,
        grid=(micro * STEPS if crop is None else STEPS,),
        out_specs=[by_crop((rows, width)), whole((8, width))] + [by_crop((rows, width))] * 3,
        out_shape=[shaped((total, width), jnp.float32), shaped((8, width), jnp.float32)]
        + [shaped((total, width), jnp.bfloat16)] * 3,
        scratch_shapes=[
            VMEM((width, width), jnp.bfloat16),
            VMEM((width, width), jnp.bfloat16),
            pltpu.SemaphoreType.DMA((2,)),
        ],
        compiler_params=params(48, big=60),
        cost_estimate=cost(16 if crop is None else 9),
        name="feed_backward",
    )


def run_self_backward(crop, me, scales, latent, upstream, stored, query, key, value, out, micro, onward, after=()):
    total, width = latent.shape
    tokens = total // micro
    part = width // HEADS
    pair = BACK_GROUP * part
    turns = HEADS // BACK_GROUP
    packed, attend = stored
    parts = (query, key, value, out)
    counts = [len(entry[0].arrays) for entry in parts]

    def kernel(me_ref, scale_ref, latent_ref, up_ref, packed_any, attend_ref, *refs):
        groups = []
        at = 0
        for count in counts:
            groups.append(refs[at : at + count])
            at += count
        if onward is not None:
            at += 1
        grad_out, out_ref, gain_ref, packed_s, out_s, blend_s, grad_ref, latent_s, packed_ref, sems = (
            refs[at:]
        )
        turn = pl.program_id(0)

        @pl.when(turn == 0)
        def _():
            out[0].start(groups[3], me_ref[0], out_s, sems.at[3], out[1])
            pltpu.make_async_copy(packed_any, packed_ref, sems.at[6]).start()
            for number in range(3):
                parts[number][0].start(
                    groups[number], me_ref[0], packed_s.at[number], sems.at[number], parts[number][1]
                )
            pltpu.make_async_copy(
                latent_ref.at[crop * tokens : (crop + 1) * tokens, :], latent_s, sems.at[4]
            ).start()
            arrived(out_s, sems.at[3])
            blend_s[...] = lowered(dot_nt(lowered(up_ref[...]), out_s[...]))
            arrived(packed_ref, sems.at[6])

        base = pl.multiple_of(turn * pair, pair)
        queries = packed_ref[:, pl.ds(base, pair)]
        keys = packed_ref[:, pl.ds(pl.multiple_of(width + base, pair), pair)]
        values = packed_ref[:, pl.ds(pl.multiple_of(2 * width + base, pair), pair)]
        blends = blend_s[:, pl.ds(base, pair)]
        grads = ([], [], [])
        for head in range(BACK_GROUP):
            cut = slice(head * part, (head + 1) * part)
            attend = attend_ref[head]
            grad_attend = dot_nt(blends[:, cut], values[:, cut])
            scores = lowered(
                softmax_back(attend.astype(jnp.float32), grad_attend) * part ** (-0.5)
            )
            grads[2].append(lowered(dot_tn(attend, blends[:, cut])))
            grads[0].append(lowered(dot_nn(scores, keys[:, cut])))
            grads[1].append(lowered(dot_tn(scores, queries[:, cut])))
        for number in range(3):
            spot = pl.ds(pl.multiple_of(number * width + base, pair), pair)
            grad_ref[:, spot] = jnp.concatenate(grads[number], axis=1)
            pltpu.make_async_copy(grad_ref.at[:, spot], grad_out.at[:, spot], sems.at[5]).start()

        @pl.when(turn == turns - 1)
        def _():
            for number in range(3):
                arrived(packed_s.at[number], sems.at[number])
            grad_hidden = sum(
                dot_nt(grad_ref[:, number * width : (number + 1) * width], packed_s[number])
                for number in range(3)
            )
            arrived(latent_s, sems.at[4])
            back, gain, bias = norm_back(latent_s[...], scale_ref, 4, grad_hidden)
            gain_ref[0:1] = gain
            gain_ref[1:2] = bias
            out_ref[...] = up_ref[...] + back
            arrived(grad_ref, sems.at[5])

    def crop_rows(columns):
        return pl.BlockSpec((tokens, columns), lambda h: (crop, 0))

    operands = [me, scales, latent, upstream, packed, attend]
    operands += [array for entry in parts for array in entry[0].arrays]
    aliases = {}
    if onward is not None:
        aliases = {len(operands): 1}
        operands.append(onward)
    return launch(
        kernel,
        after,
        operands,
        grid=(turns,),
        in_specs=[
            SMEM,
            whole((16, width)),
            ANY,
            crop_rows(width),
            ANY,
            pl.BlockSpec((BACK_GROUP, tokens, tokens), lambda h: (h, 0, 0)),
        ]
        + [ANY] * (sum(counts) + len(aliases)),
        input_output_aliases=aliases,
        out_specs=[ANY, crop_rows(width), whole((8, width))],
        out_shape=[
            shaped((tokens, 3 * width), jnp.bfloat16),
            shaped((total, width), jnp.float32),
            shaped((8, width), jnp.float32),
        ],
        scratch_shapes=[
            VMEM((3, width, width), jnp.bfloat16),
            VMEM((width, width), jnp.bfloat16),
            VMEM((tokens, width), jnp.bfloat16),
            VMEM((tokens, 3 * width), jnp.bfloat16),
            VMEM((tokens, width), jnp.float32),
            VMEM((tokens, 3 * width), jnp.bfloat16),
            pltpu.SemaphoreType.DMA((7,)),
        ],
        compiler_params=params(56),
        cost_estimate=cost(20),
        name="self_backward",
    )


def run_weights(me, products, sender, after=()):
    flat = []
    for lefts, rights in products:
        for array, *_ in lefts + rights:
            if not any(array is known for known in flat):
                flat.append(array)
    where = {id(array): number for number, array in enumerate(flat)}
    width = products[0][0][0][0].shape[1]
    count = len(products)
    span = width // 2

    def kernel(me_ref, *refs):
        sources, (keep, send, mat_s), sems = refs[: len(flat)], refs[len(flat) : len(flat) + 3], refs[-1]
        held = refs[len(flat) + 3 : -1]
        core = (me_ref[0] // me_ref[1]) % 2
        copies = [
            pltpu.make_async_copy(source, target, sems.at[1 + number])
            for number, (source, target) in enumerate(zip(sources, held))
        ]
        for copy in copies:
            copy.start()
        there = set()
        for number, (lefts, rights) in enumerate(products):
            for array, *_ in lefts + rights:
                if where[id(array)] not in there:
                    there.add(where[id(array)])
                    copies[where[id(array)]].wait()
            for side in range(2):
                cut = slice(side * span, (side + 1) * span)
                mat_s[number, :, cut] = lowered(
                    sum(
                        dot_tn(
                            held[where[id(left)]][begin : begin + size, :],
                            held[where[id(right)]][
                                top : top + size, at + side * span : at + (side + 1) * span
                            ],
                        )
                        for (left, begin, size), (right, top, at) in zip(lefts, rights)
                    )
                )
            sender.start(mat_s.at[number], core, keep, send, number * width, sems.at[0])
        arrived(mat_s, sems.at[0])

    return launch(
        kernel,
        after,
        [me] + flat,
        [SMEM] + [ANY] * len(flat),
        out_specs=[ANY] * 2,
        out_shape=sender.shapes(count * width),
        scratch_shapes=[VMEM((count, width, width), jnp.bfloat16)]
        + [VMEM(array.shape, array.dtype) for array in flat]
        + [pltpu.SemaphoreType.DMA((1 + len(flat),))],
        compiler_params=pltpu.CompilerParams(vmem_limit_bytes=60 * MIB),
        cost_estimate=cost(3 * count),
        name="weights",
    )


def run_cross_backward(
    crop, me, scales, initial, ups, stored, gains, first, second, micro, before, after=()
):
    tokens, width = ups[crop].shape
    queries, attend, pairs = stored
    spots = pairs.shape[1]
    parts = (first, second)
    counts = [len(entry[0].arrays) for entry in parts]
    small_columns = tokens + 128
    last = crop == micro - 1

    def kernel(me_ref, scale_ref, initial_ref, up_ref, query_ref, attend_ref, pair_ref, gains_ref, *refs):
        if before is not None:
            before_ref, refs = refs[0], refs[1:]
        if last:
            others, refs = refs[: micro - 1], refs[micro - 1 :]
        first_refs, refs = refs[: counts[0]], refs[counts[0] :]
        second_refs, refs = refs[: counts[1]], refs[counts[1] :]
        query_out, pair_out, back_ref, first_s, second_s, *held, sems = refs
        second[0].start(second_refs, me_ref[0], second_s, sems.at[1], second[1])
        first[0].start(first_refs, me_ref[0], first_s, sems.at[0], first[1])
        later = []
        if last:
            sources = [initial_ref, before_ref, *others]
            later = [
                pltpu.make_async_copy(source, target, sems.at[2 + number])
                for number, (source, target) in enumerate(zip(sources, held))
            ]
        for copy in later:
            copy.start()
        keys, values = pair_ref[0, :, :width], pair_ref[0, :, width:]
        attend = attend_ref[0]
        arrived(second_s, sems.at[1])
        blend = lowered(dot_nt(lowered(up_ref[...]), second_s[...]))
        scores = lowered(softmax_back(attend, dot_nt(blend, values)) * width ** (-0.5))
        query_out[...] = lowered(dot_nn(scores, keys))
        pair_out[:, :width] = lowered(dot_tn(scores, query_ref[...]))
        pair_out[:, width:] = lowered(dot_tn(lowered(attend), blend))
        arrived(first_s, sems.at[0])
        back = dot_nt(query_out[...], first_s[...])
        if not last:
            back_ref[...] = back if before is None else before_ref[...] + back
            return
        for copy in later:
            copy.wait()
        back, gain, bias = norm_back(held[0][...], scale_ref, 0, held[1][...] + back)
        for other in (up_ref, *held[2:]):
            back = back + other[...]
        gains_all = jnp.concatenate(
            [gain, bias, gains_ref[2:, :], jnp.zeros((128 - gains_ref.shape[0], width), jnp.float32)], axis=0
        )
        back_ref[:, :tokens] = lowered(back.T)
        back_ref[:, tokens:] = lowered(gains_all.T)

    back_shape = (
        shaped((width, small_columns), jnp.bfloat16) if last else shaped((tokens, width), jnp.float32)
    )
    extra = [] if before is None else [before]
    if last:
        extra += ups[:crop]
    return launch(
        kernel,
        after,
        [me, scales, initial, ups[crop], queries, attend, pairs, gains]
        + extra
        + [array for entry in parts for array in entry[0].arrays],
        [
            SMEM,
            whole((16, width)),
            ANY,
            whole((tokens, width)),
            whole((tokens, width)),
            pl.BlockSpec((1, tokens, spots), lambda i: (crop, 0, 0)),
            pl.BlockSpec((1, spots, 2 * width), lambda i: (crop, 0, 0)),
            whole((16, width)),
        ]
        + [ANY if last else whole((tokens, width))] * len(extra)
        + [ANY] * sum(counts),
        grid=(1,),
        out_specs=[whole((tokens, width)), whole((spots, 2 * width)), whole(back_shape.shape)],
        out_shape=[
            shaped((tokens, width), jnp.bfloat16),
            shaped((spots, 2 * width), jnp.bfloat16),
            back_shape,
        ],
        scratch_shapes=[
            VMEM((width, width), jnp.bfloat16),
            VMEM((width, width), jnp.bfloat16),
        ]
        + [VMEM((tokens, width), jnp.float32)] * (1 + len(extra) if last else 0)
        + [pltpu.SemaphoreType.DMA((3 + len(extra),))],
        compiler_params=params(48),
        cost_estimate=cost(9),
        name="cross_backward",
    )


def run_last_weights(me, hidden, grad_queries, grad_pairs, pictures, small, sender, rows, apart, after=()):
    tokens, width = hidden.shape
    micro = len(grad_queries)
    channels = pictures.shape[2]
    small_columns = small.shape[1]
    kv_sender = Sender(2 * width, 2 * sender.core_rows)

    def kernel(me_ref, hidden_ref, *refs):
        query_refs, pair_refs = refs[:micro], refs[micro : 2 * micro]
        pic_any, small_any, keep, send = refs[2 * micro : 2 * micro + 4]
        refs = refs[2 * micro + 4 :]
        mat_s, kv_s, pic_ref, small_ref, *pair_held, sems = refs[-5 - micro :]
        later = [
            pltpu.make_async_copy(source, target, sems.at[3 + number])
            for number, (source, target) in enumerate(
                zip((small_any, pic_any, *pair_refs), (small_ref, pic_ref, *pair_held))
            )
        ]
        for copy in later:
            copy.start()
        pair_refs = pair_held
        core = (me_ref[0] // me_ref[1]) % 2
        span = width // 2
        for number in range(2):
            cut = slice(number * span, (number + 1) * span)
            mat_s[:, cut] = lowered(
                sum(
                    dot_tn(hidden_ref[...], query_refs[crop][:, cut]) for crop in range(micro)
                )
            )
        sender.start(mat_s, core, keep, send, 0, sems.at[0])
        for copy in later:
            copy.wait()
        sender.start(small_ref, core, keep, send, width, sems.at[2])
        kv_s[...] = lowered(sum(dot_tn(pair_refs[crop][...], pic_ref[crop]) for crop in range(micro)))
        if apart:
            kv_sender.start(kv_s, core, refs[0], refs[1], 0, sems.at[1])
        else:
            for side in range(2):
                sender.start_rows(
                    kv_s, core, keep, send, width + small_columns + side * channels, rows, side, sems.at[1]
                )
        arrived(mat_s, sems.at[0])
        arrived(kv_s, sems.at[1])
        arrived(small_ref, sems.at[2])

    operands = [me, hidden, *grad_queries, *grad_pairs, pictures, small]
    if apart:
        shapes = sender.shapes(width + small_columns) + kv_sender.shapes(channels)
    else:
        shapes = sender.shapes(width + small_columns + 2 * channels)
    return launch(
        kernel,
        after,
        operands,
        [SMEM] + [whole(array.shape) for array in operands[1 : 2 + micro]] + [ANY] * (micro + 2),
        grid=(1,),
        out_specs=[ANY] * len(shapes),
        out_shape=shapes,
        scratch_shapes=[
            VMEM((width, width), jnp.bfloat16),
            VMEM((2 * width, channels), jnp.bfloat16),
            VMEM(pictures.shape, jnp.bfloat16),
            VMEM(small.shape, jnp.bfloat16),
        ]
        + [VMEM(array.shape, jnp.bfloat16) for array in grad_pairs]
        + [pltpu.SemaphoreType.DMA((5 + micro,))],
        compiler_params=pltpu.CompilerParams(vmem_limit_bytes=BIG * MIB),
        cost_estimate=cost(6),
        name="last_weights",
    )


def run_shards(matrices, kv_weight, norm_gains, head_weight, latent_init, columns):
    rows = matrices.shape[0]
    tokens, gains = latent_init.shape[1], norm_gains.shape[0]
    channels = kv_weight.shape[1]
    wide_channels = -(-channels // 128) * 128
    classes = head_weight.shape[1]
    width = matrices.shape[1] // 10
    small = tokens + 128

    def kernel(mat_ref, kv_ref, gain_ref, head_ref, latent_ref, first_ref, *refs):
        first_ref[:, tokens:small] = jnp.zeros((rows, small - tokens), jnp.bfloat16)
        first_ref[:, :tokens] = lowered(latent_ref[...])
        first_ref[:, tokens : tokens + gains] = lowered(gain_ref[...].T)
        first_ref[:, small : small + 2 * width] = lowered(mat_ref[:, : 2 * width])
        first_ref[:, small + 2 * width :] = jnp.zeros((rows, 2 * wide_channels), jnp.bfloat16)
        for side in range(2):
            at = small + 2 * width + side * wide_channels
            first_ref[:, at : at + channels] = lowered(kv_ref[side * rows : (side + 1) * rows, :])
        for (begin, end), ref in zip(columns, refs):
            ref[:, : (end - begin) * width] = lowered(mat_ref[:, begin * width : end * width])
        at = refs[-1].shape[1] - width
        refs[-1][:, at:] = jnp.zeros((rows, width), jnp.bfloat16)
        refs[-1][:, at : at + classes] = lowered(head_ref[...])

    widths = [small + 2 * width + 2 * wide_channels] + [(end - begin) * width for begin, end in columns]
    widths[-1] += width
    return pl.pallas_call(
        kernel,
        grid=(1,),
        in_specs=[
            whole(array.shape)
            for array in (matrices, kv_weight, norm_gains, head_weight, latent_init)
        ],
        out_specs=[whole((rows, number)) for number in widths],
        out_shape=[shaped((rows, number), jnp.bfloat16) for number in widths],
        compiler_params=pltpu.CompilerParams(vmem_limit_bytes=62 * MIB),
        cost_estimate=cost(3),
        name="shards",
    )(matrices, kv_weight, norm_gains, head_weight, latent_init)


def run_join(targets, passing, after):
    moves = [move for _, parts in targets for move in parts]
    sources = []
    for array, _, _ in moves:
        if not any(array is known for known in sources):
            sources.append(array)
    where = {id(array): number for number, array in enumerate(sources)}
    count, kept = len(sources), len(passing)

    def kernel(*refs):
        outs = refs[count + kept : count + kept + len(targets)]
        for target, (_, parts) in zip(outs, targets):
            for array, cut, first in parts:
                source = refs[where[id(array)]]
                if cut is None:
                    target[first : first + source.shape[0]] = source[...]
                else:
                    target[first] = source[:, cut]

    vmem = pl.BlockSpec(memory_space=pltpu.VMEM)
    outs = launch(
        kernel,
        after,
        sources + list(passing),
        [vmem] * count + [ANY] * kept,
        out_specs=[vmem] * len(targets) + [ANY] * kept,
        out_shape=[shaped(shape, jnp.bfloat16) for shape, _ in targets]
        + [shaped(array.shape, array.dtype) for array in passing],
        input_output_aliases={count + number: len(targets) + number for number in range(kept)},
        compiler_params=pltpu.CompilerParams(vmem_limit_bytes=16 * MIB),
        cost_estimate=cost(3),
        name="join",
    )
    return outs[: len(targets)], outs[len(targets) :]


def run_fold(me, parts, after):
    depth = 4
    operands = []
    in_specs = []
    out_specs = []
    out_shape = []
    for terms, first, last, axis in parts:
        groups, rows, _ = terms[0].shape
        each = groups // depth
        for term in terms:
            if not any(term is known for known in operands):
                operands.append(term)
                in_specs.append(
                    pl.BlockSpec((each, rows, term.shape[2]), lambda z: (z, 0, 0))
                )
        block = (each, rows // 2, last - first) if axis == "x" else (1, rows, last - first)
        for _ in range(2):
            out_specs.append(pl.BlockSpec(block, lambda z: (z, 0, 0)))
            out_shape.append(shaped((block[0] * depth,) + block[1:], jnp.bfloat16))
    where = {id(term): number for number, term in enumerate(operands)}

    def kernel(me_ref, *refs):
        out = len(operands)
        mine = {"x": me_ref[0] % 2, "y": (me_ref[0] // 4) % 2}
        for terms, first, last, axis in parts:
            sources = [refs[where[id(term)]] for term in terms]
            for side in range(2):
                spot = mine[axis] if side == 0 else 1 - mine[axis]
                if axis == "x":
                    rows = sources[0].shape[1] // 2
                    cut = (slice(None), pl.ds(pl.multiple_of(spot * rows, rows), rows), slice(first, last))
                else:
                    cut = (pl.ds(spot, 1), slice(None), slice(first, last))
                refs[out][...] = lowered(sum(source[cut].astype(jnp.float32) for source in sources))
                out += 1

    outs = launch(
        kernel,
        after,
        [me] + operands,
        [SMEM] + in_specs,
        grid=(depth,),
        out_specs=out_specs,
        out_shape=out_shape,
        compiler_params=params(32),
        cost_estimate=cost(4),
        name="fold",
    )
    return [(outs[2 * number], outs[2 * number + 1]) for number in range(len(parts))]


def run_fold_z(me, parts, after):
    depth = 4
    columns = [terms[0].shape[2] for terms in parts]

    def kernel(me_ref, *refs):
        mine = me_ref[0] // 8
        outs = refs[-depth:]
        at = 0
        column = 0
        for terms, number in zip(parts, columns):
            sources = refs[at : at + len(terms)]
            at += len(terms)
            for k in range(depth):
                outs[k][:, column : column + number] = lowered(
                    sum(source[pl.ds(mine ^ k, 1)].astype(jnp.float32) for source in sources)
                )[0]
            column += number

    vmem = pl.BlockSpec(memory_space=pltpu.VMEM)
    operands = [me] + [term for terms in parts for term in terms]
    shape = shaped((parts[0][0].shape[1], sum(columns)), jnp.bfloat16)
    return launch(
        kernel,
        after,
        operands,
        [SMEM] + [vmem] * (len(operands) - 1),
        out_specs=[vmem] * depth,
        out_shape=[shape] * depth,
        compiler_params=pltpu.CompilerParams(vmem_limit_bytes=24 * MIB),
        cost_estimate=cost(3),
        name="fold_z",
    )


def run_totals(states, grad_head, channels, tokens, gains):
    rows = grad_head.shape[0]
    flat = [term for terms in states for term in terms]
    widths = [terms[0].shape[1] for terms in states]
    small = tokens + 128
    width = widths[1] // 3
    wide_channels = (widths[0] - width - small) // 2
    blocks = width + sum(widths[1:])

    def kernel(head_ref, *refs):
        mat_ref, kv_ref, gain_ref, latent_ref, square_ref = refs[len(flat) :]
        at = 0
        column = width
        square = jnp.sum(head_ref[...] * head_ref[...], axis=0, keepdims=True)
        square = jnp.sum(square, axis=1, keepdims=True)
        for number, (terms, span) in enumerate(zip(states, widths)):
            total = sum(ref[...].astype(jnp.float32) for ref in refs[at : at + len(terms)])
            at += len(terms)
            part = jnp.sum(total * total, axis=0, keepdims=True)
            square = square + jnp.sum(part, axis=1, keepdims=True)
            if number > 0:
                mat_ref[:, column : column + span] = total
                column += span
                continue
            mat_ref[:, :width] = total[:, :width]
            latent_ref[...] = total[:, width : width + tokens]
            gain_ref[...] = total[:, width + tokens : width + small].T[:gains]
            for side in range(2):
                first = width + small + side * wide_channels
                kv_ref[side * rows : (side + 1) * rows, :] = total[:, first : first + channels]
        square_ref[...] = jnp.broadcast_to(square, square_ref.shape)

    shapes = [
            shaped((rows, blocks), jnp.float32),
            shaped((2 * rows, channels), jnp.float32),
            shaped((gains, rows), jnp.float32),
            shaped((rows, tokens), jnp.float32),
            shaped((1, 128), jnp.float32),
    ]
    return pl.pallas_call(
        kernel,
        grid=(1,),
        in_specs=[whole(array.shape) for array in [grad_head] + flat],
        out_specs=[whole(shape.shape) for shape in shapes],
        out_shape=shapes,
        compiler_params=pltpu.CompilerParams(vmem_limit_bytes=32 * MIB),
        cost_estimate=cost(3),
        name="totals",
    )(grad_head, *flat)


def run_update(squares, step_count, shares, masters, firsts, seconds):
    count = len(shares)
    given = [master for master in masters if master is not None]

    def kernel(step_ref, square_ref, *refs):
        share_refs, refs = refs[:count], refs[count:]
        master_refs, refs = list(refs[: len(given)]), refs[len(given) :]
        first_refs, second_refs, outs = refs[:count], refs[count : 2 * count], refs[2 * count :]
        norm = jnp.sqrt(jnp.sum(square_ref[...], axis=0, keepdims=True))
        outs[0][...] = norm
        factor = jnp.minimum(1.0, THRESH / norm[:, 0:1])
        steps = jnp.zeros((1, 1), jnp.float32) + step_ref[0].astype(jnp.float32)
        scale = 1.0 / (1.0 - jnp.exp2(-steps))
        for number in range(count):
            clipped = share_refs[number][...] * factor
            moment_one = 0.5 * first_refs[number][...] + 0.5 * clipped
            moment_two = 0.5 * second_refs[number][...] + 0.5 * clipped * clipped
            outs[1 + 3 * number][...] = moment_one
            outs[2 + 3 * number][...] = moment_two
            if masters[number] is None:
                outs[3 + 3 * number][...] = clipped
                continue
            master = master_refs.pop(0)[...]
            outs[3 + 3 * number][...] = master - RATE * (
                moment_one * scale / (jnp.sqrt(moment_two * scale) + TINY) + DECAY * master
            )

    shapes = [shaped((1, 128), jnp.float32)]
    shapes += [shaped(share.shape, jnp.float32) for share in shares for _ in range(3)]
    operands = [step_count, squares, *shares, *given, *firsts, *seconds]
    return pl.pallas_call(
        kernel,
        grid=(1,),
        in_specs=[SMEM] + [whole(array.shape) for array in operands[1:]],
        out_specs=[whole(shape.shape) for shape in shapes],
        out_shape=shapes,
        compiler_params=pltpu.CompilerParams(vmem_limit_bytes=62 * MIB),
        cost_estimate=cost(5),
        name="update",
    )(*operands)


def digits():
    n_wide = lax.axis_size("wide")
    n_narrow = lax.axis_size("narrow")
    rest = n_wide // 2
    top = min(4, rest)
    return (
        ("z", n_narrow * n_wide // top, top),
        ("y", 2 * n_narrow, rest // top),
        ("c", n_narrow, 2),
        ("x", 1, n_narrow),
    )


def device_index():
    return lax.axis_index("wide") * lax.axis_size("narrow") + lax.axis_index("narrow")


def exchange(values, offset):
    total = lax.axis_size(AXES)
    return lax.ppermute(values, AXES, [(i, i ^ offset) for i in range(total)])


class Gather:
    def __init__(self, shard, first, left, right, plain):
        self.shard = shard
        self.first = first
        self.widths = (left, right)
        self.rows = shard.shape[0]
        self.table = {name: (stride, size) for name, stride, size in digits()}
        self.names = (("y", "x"), ("x", "y"))
        self.plain = plain

    def send_z(self):
        stride, size = self.table["z"]
        self.got = [exchange(self.shard, k * stride) for k in range(1, size)]
        return self.got

    def join(self, targets, passing, after):
        if self.plain:
            flats = []
            for _, parts in targets:
                flats.append(
                    jnp.concatenate(
                        [
                            array if array.ndim == 3 else array[None, :, cut]
                            for array, cut, _ in parts
                        ]
                    )
                )
            return flats, passing
        return run_join(targets, passing, after)

    def join_z(self, passing=(), after=()):
        stride, size = self.table["z"]
        pieces = [self.shard] + self.got
        targets = []
        at = self.first
        for width in self.widths:
            parts = [(piece, slice(at, at + width), k) for k, piece in enumerate(pieces)]
            targets.append(((size, self.rows, width), parts))
            at += width
        self.flats, passing = self.join(targets, passing, after)
        self.offsets = [[k * stride for k in range(size)]] * 2
        return passing

    def send(self, turn):
        self.got = []
        for half in range(2):
            stride, size = self.table[self.names[half][turn]]
            self.got.append([exchange(self.flats[half], k * stride) for k in range(1, size)])
        return self.got[0] + self.got[1]

    def pieces(self, turn):
        halves = []
        for half in range(2):
            stride, size = self.table[self.names[half][turn]]
            arrays = [self.flats[half]] + self.got[half]
            halves.append(
                (arrays, [[offset ^ (k * stride) for offset in self.offsets[half]] for k in range(size)])
            )
        return halves

    def join_first(self, passing=(), after=()):
        targets = []
        offsets = []
        for arrays, groups in self.pieces(0):
            count = arrays[0].shape[0]
            parts = [(array, None, k * count) for k, array in enumerate(arrays)]
            targets.append(((count * len(arrays),) + arrays[0].shape[1:], parts))
            offsets.append([offset for group in groups for offset in group])
        self.flats, passing = self.join(targets, passing, after)
        self.offsets = offsets
        return passing

    def held(self):
        return list(self.flats) + self.got[0] + self.got[1]

    def release(self, arrays):
        self.flats = arrays[:2]
        count = len(self.got[0])
        self.got = [list(arrays[2 : 2 + count]), list(arrays[2 + count :])]

    def send_across(self):
        stride = self.table["c"][0]
        self.state = []
        fresh = []
        for arrays, offsets in self.pieces(1):
            sent = [exchange(array, stride) for array in arrays]
            fresh += sent
            self.state.append(
                (
                    arrays + sent,
                    offsets + [[offset ^ stride for offset in group] for group in offsets],
                )
            )
        return fresh

    def done(self):
        halves = []
        me = device_index()
        total = lax.axis_size(AXES)
        for arrays, offsets in self.state:
            if not self.plain:
                halves.append(Half(arrays, offsets, self.rows))
            else:
                flat = jnp.concatenate(arrays)
                spots = jnp.argsort(jnp.array([o for group in offsets for o in group]) ^ me)
                flat = jnp.take(flat, spots, axis=0).reshape(1, total * self.rows, -1)
                halves.append(Half([flat], None, total * self.rows))
        return halves


class Scatter:
    def __init__(self, me, keep, send, cut, plain, extra=None):
        self.me = me
        self.keep = keep
        self.columns = keep.shape[2]
        self.cut = cut
        self.plain = plain
        self.table = {name: (stride, size) for name, stride, size in digits()}
        self.pairs = [(keep, send)] + ([extra] if extra is not None else [])
        self.names = (("x", "y"), ("y", "x"), ("y", "x"))
        self.last = keep

    def send_across(self):
        stride = self.table["c"][0]
        fresh = [exchange(send, stride) for _, send in self.pairs]
        if not self.plain:
            terms = [self.keep, fresh[0]]
            self.state = [(terms, 0, self.cut), (terms, self.cut, self.columns)]
            return fresh
        sizes = tuple(self.table[name][1] for name in ("z", "y", "x"))
        self.state = []
        for number, ((keep, _), received) in enumerate(zip(self.pairs, fresh)):
            rows = keep.shape[0] * keep.shape[1] // (sizes[0] * sizes[1] * sizes[2])
            terms = [term.reshape(sizes + (rows, keep.shape[2])) for term in (keep, received)]
            if number == 0:
                self.state.append((["z", "y", "x"], [term[..., : self.cut] for term in terms]))
                self.state.append((["z", "y", "x"], [term[..., self.cut :] for term in terms]))
            else:
                self.state.append((["z", "y", "x"], terms))
        return fresh

    def send(self, turn, after=()):
        fresh = []
        if not self.plain:
            if turn == 2:
                kept, *sends = run_fold_z(self.me, [terms for terms, _, _ in self.state], after)
                stride = self.table["z"][0]
                fresh = [exchange(send, (k + 1) * stride) for k, send in enumerate(sends)]
                self.state = [kept] + fresh
                self.last = kept
                return fresh
            names = [ways[turn] for ways in self.names]
            pairs = run_fold(
                self.me, [entry + (name,) for entry, name in zip(self.state, names)], after
            )
            self.state = []
            for (kept, send), name in zip(pairs, names):
                received = exchange(send, self.table[name][0])
                fresh.append(received)
                self.state.append(([kept, received], 0, kept.shape[2]))
            self.last = pairs[0][0]
            return fresh
        me = device_index()
        for number, (left, terms) in enumerate(self.state):
            name = (self.names[number] + ("z",))[turn]
            stride, size = self.table[name]
            mine = (me // stride) % size
            axis = left.index(name)

            def part(index):
                return lowered(
                    sum(
                        lax.dynamic_index_in_dim(term, index, axis, keepdims=False).astype(jnp.float32)
                        for term in terms
                    )
                )

            kept = part(mine)
            sent = [exchange(part(mine ^ k), k * stride) for k in range(1, size)]
            fresh += sent
            self.state[number] = ([entry for entry in left if entry != name], [kept] + sent)
            self.last = kept
        return fresh

    def done(self):
        if not self.plain:
            return sum(term.astype(jnp.float32) for term in self.state)
        sums = [sum(term.astype(jnp.float32) for term in terms) for _, terms in self.state]
        rows = sums[0].shape[0]
        if len(sums) > 2:
            sums[2:] = [sums[2][:rows], sums[2][rows:]]
        return jnp.concatenate(sums, axis=1)


def share(values):
    total = lax.axis_size(AXES)
    spread = jnp.broadcast_to(values[None], (total,) + values.shape)
    return lax.all_to_all(spread, AXES, 0, 0, tiled=True)


def on_device(
    pixels,
    labels,
    partner,
    pair_on,
    step_count,
    matrices,
    kv_weight,
    norm_gains,
    head_weight,
    latent_init,
    matrices_first,
    kv_first,
    gains_first,
    head_first,
    latent_first,
    matrices_second,
    kv_second,
    gains_second,
    head_second,
    latent_second,
):
    axis_count = lax.axis_size(AXES)
    n_narrow = lax.axis_size("narrow")
    index = device_index()
    me = jnp.stack([index, jnp.int32(n_narrow)]).astype(jnp.int32)
    micro = pixels.shape[0]
    tokens = latent_init.shape[1]
    width = matrices.shape[1] // 10
    rows = matrices.shape[0]
    channels = pixels.shape[3]
    wide_channels = -(-channels // 128) * 128
    classes = head_weight.shape[1]

    half = width // 2
    wide_half = width + half
    small_columns = tokens + 128
    plain = rows % 16 != 0 or tuple(size for _, _, size in digits()) != (4, 2, 2, 2)
    pictures = jnp.pad(pixels[:, 0], ((0, 0), (0, 0), (0, wide_channels - channels)))
    blocks = ((2, 4), (4, 7), (7, 10))
    shards = run_shards(matrices, kv_weight, norm_gains.T, head_weight, latent_init, blocks)
    chunks = [
        Gather(shards[0], 0, small_columns + width, width + 2 * wide_channels, plain),
        Gather(shards[1], 0, width, width, plain),
        Gather(shards[2], 0, wide_half, wide_half, plain),
        Gather(shards[3], 0, 2 * width, 2 * width, plain),
    ]

    def block(halves, column, last=width):
        left = halves[0].arrays[0].shape[2]
        if column >= left:
            return [(halves[1], column - left, 0, last)]
        if column + last <= left:
            return [(halves[0], column, 0, last)]
        return [(halves[0], column, 0, left - column), (halves[1], 0, left - column, last)]

    first, second, third, fourth = chunks
    first.send_z()
    second.send_z()
    (pictures,) = first.join_z([pictures])
    first.send(0)
    first.join_first()
    first.send(1)
    (third.shard,) = second.join_z([third.shard], after=first.flats)
    second.send(0)
    third.send_z()
    first.send_across()
    second.join_first()
    second.send(1)
    halves = first.done()
    weights = {0: (halves[0], small_columns), 1: (halves[1], 0)}
    small_half, kv_half = (halves[0], 0), (halves[1], width)
    if kv_half[0].offsets is None:
        array = kv_half[0].arrays[0][..., width:].reshape(axis_count, rows, 2, wide_channels)
        array = array.transpose(0, 2, 1, 3).reshape(1, 2 * width, wide_channels)
        kv_half = (Half([array], None, 2 * width), 0)
    latent_one, blended, attend, pairs, initial, hidden_zero, queries, scales = run_cross_forward(
        me, pictures, small_half, kv_half, weights[0], weights[1], width, tokens,
        after=second.flats,
    )
    second.release(second.join([], second.held(), [latent_one])[1])
    second.send_across()
    (fourth.shard,) = third.join_z([fourth.shard], after=second.flats)
    third.send(0)
    fourth.send_z()
    third.join_first(after=third.flats)
    third.send(1)
    for number in range(2):
        weights[2 + number] = (second.done()[number], 0)
    latent_two, hidden_one, active_one, steep_one = run_feed_forward(
        me, scales, latent_one, weights[2], weights[3], 2, micro, False,
        after=third.flats,
    )
    third.release(fourth.join_z(third.held(), after=[latent_two]))
    third.send_across()
    fourth.send(0)
    fourth.join_first()
    fourth.send(1)
    halves = third.done()
    for number in range(3):
        weights[4 + number] = (Joint(block(halves, number * width)), 0)
    hidden_two, packed, attend_self, blended_self = [], [], [], []
    for crop in range(micro):
        outs = run_self_forward(
            crop, me, scales, latent_two, weights[4], weights[5], weights[6], micro,
            after=fourth.flats if crop == 0 else fourth.flats,
        )
        for entries, out in zip((hidden_two, packed, attend_self, blended_self), outs):
            entries.append(out)
        if crop == 0:
            fourth.release(fourth.join([], fourth.held(), [blended_self[0]])[1])
            fourth.send_across()
    halves = fourth.done()
    weights[7], weights[8], weights[9] = (halves[0], 0), (halves[0], width), (halves[1], 0)
    result, hidden_three, active_three, steep_three, pooled, latent_three = run_feed_forward(
        me, scales, latent_two, weights[8], weights[9], 6, micro, True, (blended_self, weights[7])
    )
    marks = jnp.stack(
        [labels[:, 0] // 256, labels[:, 0] % 256, partner[:, 0] // 256, partner[:, 0] % 256, pair_on[:, 0]],
        axis=1,
    )
    marks = jnp.pad(lowered(marks), ((0, 0), (0, MARKS - marks.shape[1])))
    pooled_all = share(jnp.concatenate([pooled.reshape(micro, width), marks], axis=1))
    pooled_all = pooled_all.reshape(axis_count * micro, width + MARKS)
    loss_tile, grad_logits, grad_pooled = run_losses(
        me, pooled_all, [(halves[1], width), (halves[1], width + half)], classes, axis_count, micro
    )
    total_loss = loss_tile[0, 0]
    counts = loss_tile[1 : 1 + micro, 0].astype(jnp.int32)
    pooled_rows = lax.dynamic_slice_in_dim(pooled_all, index * rows, rows, axis=1)
    grad_head = dot_tn(pooled_rows, grad_logits)[:, :classes]

    sender = Sender(width, n_narrow * rows)
    total_tokens = micro * tokens

    def single(left, right):
        return [(left, 0, total_tokens)], [(right, 0, 0)]

    upstream, gain_high, low, before, behind = run_feed_backward(
        me, scales, latent_three, (result, grad_pooled), steep_three, weights[8], weights[9], 6, micro, True
    )
    keep, send = run_weights(
        me,
        [
            (
                [(rows_of, 0, tokens) for rows_of in blended_self],
                [(behind, crop * tokens, 0) for crop in range(micro)],
            ),
            single(hidden_three, before),
            single(active_three, low),
        ],
        sender,
    )
    one = Scatter(me, keep, send, wide_half, plain)
    one.send_across()
    grads = []
    gain_mid = 0.0
    onward = None
    for crop in range(micro):
        waits = ()
        if crop == 1:
            one.send(0, after=[onward])
            waits = [one.last]
        grad_packed, onward, gain = run_self_backward(
            crop, me, scales, latent_two, upstream, (packed[crop], attend_self[crop]),
            weights[4], weights[5], weights[6], weights[7], micro, onward, after=waits,
        )
        grads.append(grad_packed)
        gain_mid = gain_mid + gain
    upstream = onward
    one.send(1, after=[onward])
    keep, send = run_weights(
        me,
        [
            (
                [(hidden_two[crop], 0, tokens) for crop in range(micro)],
                [(grads[crop], 0, number * width) for crop in range(micro)],
            )
            for number in range(3)
        ],
        sender,
        after=[one.last],
    )
    two = Scatter(me, keep, send, wide_half, plain)
    two.send_across()
    ups, lows, befores, behinds = [], [], [], []
    gain_low = 0.0
    for crop in range(micro):
        outs = run_feed_backward(
            me, scales, latent_one, upstream, steep_one, weights[2], weights[3], 2, micro, False, crop,
            after=[keep] if crop == 0 else [two.last, one.last],
        )
        gain_low = gain_low + outs[1]
        for entries, out in zip((ups, lows, befores, behinds), (outs[0],) + tuple(outs[2:])):
            entries.append(out)
        if crop == 0:
            arriving = two.send(0, after=[outs[0]])
            one_z = one.send(2, after=[two.last])
    keep, send = run_weights(
        me,
        [
            (
                [(left, crop * tokens, tokens) for crop in range(micro)],
                [(rights[crop], 0, 0) for crop in range(micro)],
            )
            for left, rights in ((blended, behinds), (hidden_one, befores), (active_one, lows))
        ],
        sender,
        after=ups[-1:] + arriving,
    )
    three = Scatter(me, keep, send, wide_half, plain)
    three.send_across()
    two.send(1, after=[keep])
    gains = jnp.concatenate(
        [
            jnp.zeros((2, width), jnp.float32),
            gain_low[:2],
            gain_mid[:2],
            gain_high[:4],
            jnp.zeros((6, width), jnp.float32),
        ]
    )
    grad_queries, grad_pairs = [], []
    back = None
    for crop in range(micro):
        outs = run_cross_backward(
            crop, me, scales, initial, ups, (queries, attend, pairs), gains,
            weights[0], weights[1], micro, back, after=[two.last],
        )
        grad_queries.append(outs[0])
        grad_pairs.append(outs[1])
        back = outs[2]
        if crop == 0:
            arriving = three.send(0, after=[back] + one_z)
            two_z = two.send(2, after=[three.last])
    grad_small = back
    keep, send, *extra = run_last_weights(
        me, hidden_zero, grad_queries, grad_pairs, pictures, grad_small,
        sender, rows, plain, after=arriving + two_z,
    )
    four = Scatter(me, keep, send, 128 * round(keep.shape[2] / 256), plain, extra or None)
    four.send_across()
    arriving = three.send(1, after=[keep])
    four.send(0, after=arriving)
    arriving = three.send(2, after=[four.last])
    four.send(1, after=arriving)
    four.send(2)
    if plain:
        last = four.done()
        grad_matrices = jnp.concatenate(
            [last[:, :width], three.done(), two.done(), one.done()], axis=1
        )
        grad_kv = last[:, width + small_columns :]
        grad_kv = jnp.concatenate(
            [grad_kv[:, :channels], grad_kv[:, wide_channels : wide_channels + channels]]
        )
        grad_small = last[:, width : width + small_columns]
        grad_gains, grad_latent = grad_small[:, tokens : tokens + 10].T, grad_small[:, :tokens]
        shares = (grad_matrices, grad_kv, grad_gains, grad_head, grad_latent)
        square = sum(jnp.sum(member * member) for member in shares)
        square = jnp.broadcast_to(square, (1, 128))
    else:
        grad_matrices, grad_kv, grad_gains, grad_latent, square = run_totals(
            [four.state, three.state, two.state, one.state],
            grad_head,
            channels,
            tokens,
            norm_gains.shape[1],
        )
    shares = (grad_matrices, grad_kv, grad_gains, grad_head, grad_latent)
    norm, *results = run_update(
        share(square[0]),
        step_count,
        shares,
        (matrices, kv_weight, None, head_weight, None),
        (matrices_first, kv_first, gains_first.T, head_first, latent_first),
        (matrices_second, kv_second, gains_second.T, head_second, latent_second),
    )
    results[6:9] = [result.T for result in results[6:9]]
    return (total_loss, norm[0, 0], counts, *results)


def solution(mesh):
    in_specs = (
        P(None, ("wide", "narrow"), None, None),
        P(None, ("wide", "narrow")),
        P(None, ("wide", "narrow")),
        P(None, ("wide", "narrow")),
        P(),
        P(("wide", "narrow"), None),
        P(("wide", "narrow"), None),
        P(("wide", "narrow"), None),
        P(("wide", "narrow"), None),
        P(("wide", "narrow"), None),
        P(("wide", "narrow"), None),
        P(("wide", "narrow"), None),
        P(("wide", "narrow"), None),
        P(("wide", "narrow"), None),
        P(("wide", "narrow"), None),
        P(("wide", "narrow"), None),
        P(("wide", "narrow"), None),
        P(("wide", "narrow"), None),
        P(("wide", "narrow"), None),
        P(("wide", "narrow"), None),
    )
    out_specs = (
        P(),
        P(),
        P(),
        P(("wide", "narrow"), None),
        P(("wide", "narrow"), None),
        P(("wide", "narrow"), None),
        P(("wide", "narrow"), None),
        P(("wide", "narrow"), None),
        P(("wide", "narrow"), None),
        P(("wide", "narrow"), None),
        P(("wide", "narrow"), None),
        P(("wide", "narrow"), None),
        P(("wide", "narrow"), None),
        P(("wide", "narrow"), None),
        P(("wide", "narrow"), None),
        P(("wide", "narrow"), None),
        P(("wide", "narrow"), None),
        P(("wide", "narrow"), None),
    )
    return jax.shard_map(
        on_device, mesh=mesh, in_specs=in_specs, out_specs=out_specs, check_vma=False
    )
```
